32 devices in a mesh: strip: 8 (over z, x), chan: 4 (over y, core).
Axes of the slice: x: 2, y: 2, z: 4, core: 2. Of those that a mesh axis runs over, the one named last changes fastest.
Arguments:
- cam_feats: bfloat16 [80, 131072], P('chan', 'strip'), may hold values from -3 to 3
- cell_index: int32 [131072], P('strip'), may hold values from 0 to 4096
- lidar_bev: bfloat16 [16, 256, 16, 128], P(None, 'chan', 'strip'), may hold values from -12 to 12
- w_cam: float32 [3, 3, 80, 256], P(None, None, None, 'chan'), may hold values from -0.109375 to 0.109375
- w_lidar: float32 [3, 3, 256, 256], P(None, None, None, 'chan'), may hold values from -0.109375 to 0.109375
- w_mid: float32 [3, 3, 256, 256], P(None, None, 'chan'), may hold values from -0.125 to 0.125
- bn_params: float32 [4, 256], P(None, 'chan'), may hold values from -1.5 to 6.5
- cotangent: bfloat16 [16, 256, 16, 128], P(None, 'chan', 'strip'), may hold values from -12 to 12
- m_cam: float32 [3, 3, 80, 256], P(None, None, None, 'chan'), may hold values from -0.0014648438 to 0.0014648438
- v_cam: float32 [3, 3, 80, 256], P(None, None, None, 'chan'), may hold values from 7.3260503e-10 to 2.9304201e-09
- m_lidar: float32 [3, 3, 256, 256], P(None, None, None, 'chan'), may hold values from -0.0014648438 to 0.0014648438
- v_lidar: float32 [3, 3, 256, 256], P(None, None, None, 'chan'), may hold values from 7.3260503e-10 to 2.9304201e-09
- m_mid: float32 [3, 3, 256, 256], P(None, None, 'chan'), may hold values from -0.0014648438 to 0.0014648438
- v_mid: float32 [3, 3, 256, 256], P(None, None, 'chan'), may hold values from 7.3260503e-10 to 2.9304201e-09
- m_bn: float32 [4, 256], P(None, 'chan'), may hold values from -0.0014648438 to 0.0014648438
- v_bn: float32 [4, 256], P(None, 'chan'), may hold values from 7.3260503e-10 to 2.9304201e-09
Outputs:
- mixed: float32 [16, 256, 16, 128], P(None, 'chan', 'strip')
- grad_cam: float32 [80, 131072], P('chan', 'strip')
- grad_lidar: float32 [16, 256, 16, 128], P(None, 'chan', 'strip')
- grad_norm: float32 [], replicated
- new_w_cam: float32 [3, 3, 80, 256], P(None, None, None, 'chan')
- new_m_cam: float32 [3, 3, 80, 256], P(None, None, None, 'chan')
- new_v_cam: float32 [3, 3, 80, 256], P(None, None, None, 'chan')
- new_w_lidar: float32 [3, 3, 256, 256], P(None, None, None, 'chan')
- new_m_lidar: float32 [3, 3, 256, 256], P(None, None, None, 'chan')
- new_v_lidar: float32 [3, 3, 256, 256], P(None, None, None, 'chan')
- new_w_mid: float32 [3, 3, 256, 256], P(None, None, 'chan')
- new_m_mid: float32 [3, 3, 256, 256], P(None, None, 'chan')
- new_v_mid: float32 [3, 3, 256, 256], P(None, None, 'chan')
- new_bn: float32 [4, 256], P(None, 'chan')
- new_m_bn: float32 [4, 256], P(None, 'chan')
- new_v_bn: float32 [4, 256], P(None, 'chan')
The draws below stay inside these ranges and needn't reach their ends.
Inputs may be any that keep to these rules, and one draw needn't show every extreme that they name: `cell_index`: the cell of a point counts within the rows of the strip that holds the point, as (grid * 2 + row) * 128 + column; 4096 marks a point outside every grid.
All inputs are finite; a program needn't handle non-finite values.
Results may differ from the reference program's by a relative error of at most 0.0087.
Values may be sent and summed in bfloat16 or wider, within the bound.
No kernel may reach another device: no remote copies, remote signals or barrier semaphores. Data moves between devices by JAX's collectives and lax.ppermute only.
A program may use at most 128 MiB of HBM per device.

```python
import math
import jax
import jax.numpy as jnp
from jax import lax

C_CAM = 80
C_LID = 256
C_OUT = 256
GRIDS = 16
ROWS = 2
W = 128
STEP = 10
H = 16
CELLS_DEV = 4096
PTS_DEV = 16384
NPTS = 131072
NPARAM = 1364992
N_STRIP = 8


def rising_field(key, channels, spread):
    values = jax.random.truncated_normal(key, -4.0, 4.0, (GRIDS, channels, H, W), jnp.float32)
    row_scale = 1.0 + spread * jnp.arange(H, dtype=jnp.float32) / (H - 1)
    return values * row_scale[None, None, :, None]


def draw_lidar_bev(key, part):
    key = jax.random.fold_in(key, 11)
    return rising_field(key, C_LID, 2.0).astype(jnp.bfloat16)


def draw_cotangent(key, part):
    key = jax.random.fold_in(key, 12)
    return rising_field(key, C_OUT, 2.0).astype(jnp.bfloat16)


def draw_bn_params(key, part):
    key = jax.random.fold_in(key, 13)
    gain_key, shift_key = jax.random.split(key)
    position = jnp.arange(C_OUT, dtype=jnp.float32) / (C_OUT - 1)
    gains = (1.0 + 2.0 * position)[None, :] * jax.random.uniform(gain_key, (2, C_OUT), jnp.float32, 0.8, 1.25)
    shifts = 0.3 * jax.random.truncated_normal(shift_key, -4.0, 4.0, (2, C_OUT), jnp.float32)
    return jnp.stack([gains[0], shifts[0], gains[1], shifts[1]])


def set_ends(array, key, least, top_value):
    place = [jax.random.randint(jax.random.fold_in(key, axis), (), 0, length) for axis, length in enumerate(array.shape)]
    widest = array.shape.index(max(array.shape))
    neighbour = place[:widest] + [(place[widest] + 1) % array.shape[widest]] + place[widest + 1:]
    return array.at[tuple(place)].set(least).at[tuple(neighbour)].set(top_value)


def steps_of(rng, dims, cuts, smallest, top_value):
    level = 1.0
    for dim, blocks in cuts:
        heights = jax.random.uniform(jax.random.fold_in(jax.random.fold_in(rng, 6), dim), (blocks,), jnp.float32, smallest / len(cuts), top_value / len(cuts))
        level = level * jnp.repeat(jnp.exp(heights), dims[dim] // blocks).reshape((-1,) + (1,) * (len(dims) - 1 - dim))
    return level


def noise(key, dims, deviation, reach, pieces=(), kind=jnp.bfloat16):
    values = jax.random.normal(key, dims, jnp.float32) * deviation
    if len(pieces) > 0:
        values = steps_of(key, dims, pieces, -0.22, 0.18) * values
    return jnp.clip(values, min=-reach, max=reach).astype(kind)


def setup_inputs(seed: int = 0) -> dict:
    key_of = jax.random.split(jax.random.key(seed), 17)
    return {
        "cam_feats": noise(key_of[0], (C_CAM, NPTS), 0.5, 3.0, ((0, 4), (1, 8))),
        "cell_index": set_ends(jax.random.randint(key_of[1], (NPTS,), 0, CELLS_DEV + 1), jax.random.fold_in(key_of[1], 1), 0, CELLS_DEV).astype(jnp.int32),
        "lidar_bev": draw_lidar_bev(jax.random.fold_in(key_of[16], 71), 0),
        "w_cam": noise(key_of[3], (3, 3, C_CAM, C_OUT), (9 * (C_CAM + C_LID)) ** -0.5, 0.109375, ((3, 4),), jnp.float32),
        "w_lidar": noise(key_of[4], (3, 3, C_LID, C_OUT), (9 * (C_CAM + C_LID)) ** -0.5, 0.109375, ((3, 4),), jnp.float32),
        "w_mid": noise(key_of[5], (3, 3, C_OUT, C_OUT), (9 * C_OUT) ** -0.5, 0.125, ((2, 4),), jnp.float32),
        "bn_params": draw_bn_params(jax.random.fold_in(key_of[16], 71), 0),
        "cotangent": draw_cotangent(jax.random.fold_in(key_of[16], 71), 0),
        "m_cam": noise(key_of[8], (3, 3, C_CAM, C_OUT), (0.11 * NPARAM ** -0.5), 0.0014648438, ((3, 4),), jnp.float32),
        "v_cam": jnp.clip(jnp.exp(math.log(2.9304201287772003e-09) - 1.3862944 * jax.random.uniform(key_of[9], (3, 3, C_CAM, C_OUT), jnp.float32) ** steps_of(key_of[9], (3, 3, C_CAM, C_OUT), ((3, 4),), -0.2, 0.2)), 7.326050321943001e-10, 2.9304201287772003e-09),
        "m_lidar": noise(key_of[10], (3, 3, C_LID, C_OUT), (0.11 * NPARAM ** -0.5), 0.0014648438, ((3, 4),), jnp.float32),
        "v_lidar": jnp.clip(jnp.exp(math.log(2.9304201287772003e-09) - 1.3862944 * jax.random.uniform(key_of[11], (3, 3, C_LID, C_OUT), jnp.float32) ** steps_of(key_of[11], (3, 3, C_LID, C_OUT), ((3, 4),), -0.2, 0.2)), 7.326050321943001e-10, 2.9304201287772003e-09),
        "m_mid": noise(key_of[12], (3, 3, C_OUT, C_OUT), (0.11 * NPARAM ** -0.5), 0.0014648438, ((2, 4),), jnp.float32),
        "v_mid": jnp.clip(jnp.exp(math.log(2.9304201287772003e-09) - 1.3862944 * jax.random.uniform(key_of[13], (3, 3, C_OUT, C_OUT), jnp.float32) ** steps_of(key_of[13], (3, 3, C_OUT, C_OUT), ((2, 4),), -0.2, 0.2)), 7.326050321943001e-10, 2.9304201287772003e-09),
        "m_bn": noise(key_of[14], (4, C_OUT), (0.11 * NPARAM ** -0.5), 0.0014648438, ((1, 4),), jnp.float32),
        "v_bn": jnp.clip(jnp.exp(math.log(2.9304201287772003e-09) - 1.3862944 * jax.random.uniform(key_of[15], (4, C_OUT), jnp.float32) ** steps_of(key_of[15], (4, C_OUT), ((1, 4),), -0.2, 0.2)), 7.326050321943001e-10, 2.9304201287772003e-09),
    }


beta_one = 0.9
beta_two = 0.999
adam_eps = 1e-08
learn_rate = 0.02
norm_rate = 1.5
weight_decay = 0.01
norm_eps = 1e-05
clip_norm = 1.0

@jax.custom_vjp
def low(v):
    return lax.optimization_barrier(v.astype(jnp.bfloat16)).astype(jnp.float32)

@jax.custom_vjp
def low_back(v):
    return v

def low_keep(v):
    return (low(v), None)

def low_pass(kept, grad):
    return (grad,)

def back_keep(v):
    return (v, None)

def back_low(kept, grad):
    return (low(grad),)
low.defvjp(low_keep, low_pass)
low_back.defvjp(back_keep, back_low)

def conv_three(inputs, kernel):
    return lax.conv_general_dilated(inputs, kernel, (1, 1), ((1, 1), (1, 1)), dimension_numbers=('NCHW', 'HWIO', 'NCHW'), precision=lax.Precision.HIGHEST)

def batch_norm(raw, gain, shift):
    mean_value = lax.optimization_barrier(jnp.mean(raw, axis=(0, 2, 3)))
    variance = lax.optimization_barrier(jnp.mean(raw * raw, axis=(0, 2, 3))) - mean_value * mean_value
    centred = (raw - mean_value[None, :, None, None]) * lax.rsqrt(variance + norm_eps)[None, :, None, None]
    return gain[None, :, None, None] * centred + shift[None, :, None, None]

def pool_cells(camera, cell_index):
    channels = camera.shape[0]
    feat_strips = camera.reshape(channels, N_STRIP, PTS_DEV).transpose(1, 0, 2)
    cell_strips = cell_index.reshape(N_STRIP, PTS_DEV)
    slot_ids = jnp.arange(CELLS_DEV, dtype=jnp.int32)

    def one_strip(paired):
        feature, groups = paired
        table = (groups[None, :] == slot_ids[:, None]).astype(jnp.float32)
        return jnp.dot(feature, table.T, precision=lax.Precision.HIGHEST)
    pooled = lax.map(jax.checkpoint(one_strip), (feat_strips, cell_strips))
    pooled = pooled.reshape(N_STRIP, channels, GRIDS, ROWS, W).transpose(2, 1, 0, 3, 4)
    return pooled.reshape(GRIDS, channels, H, W)

def adam_update(weight, gradient, first, second, rate):
    first = beta_one * first + (1.0 - beta_one) * gradient
    second = beta_two * second + (1.0 - beta_two) * gradient * gradient
    fix_one = 1.0 - beta_one ** STEP
    fix_two = 1.0 - beta_two ** STEP
    stepped = first / fix_one / (jnp.sqrt(second / fix_two) + adam_eps)
    return (weight - rate * (stepped + weight_decay * weight), first, second)

def reference(cam_feats, cell_index, lidar_bev, w_cam, w_lidar, w_mid, bn_params, cotangent, m_cam, v_cam, m_lidar, v_lidar, m_mid, v_mid, m_bn, v_bn):

    def forward(camera, lidar, kernel_cam, kernel_lidar, kernel_mid, params):
        pooled = pool_cells(camera, cell_index)
        cam_in = low(low_back(pooled))
        merged_raw = low_back(conv_three(cam_in, low(kernel_cam)) + conv_three(lidar, low(kernel_lidar)))
        hidden = jax.nn.silu(batch_norm(merged_raw, params[0], params[1]))
        encoded = low_back(conv_three(low(hidden), low(kernel_mid)))
        return hidden + jax.nn.silu(batch_norm(encoded, params[2], params[3]))
    primals = (cam_feats.astype(jnp.float32), lidar_bev.astype(jnp.float32), w_cam, w_lidar, w_mid, bn_params)
    mixed, pullback = jax.vjp(forward, *primals)
    grad_cam, grad_lidar, grad_wc, grad_wl, grad_mid, grad_bn = pullback(cotangent.astype(jnp.float32))
    squares = jnp.sum(grad_wc * grad_wc) + jnp.sum(grad_wl * grad_wl) + jnp.sum(grad_mid * grad_mid) + jnp.sum(grad_bn * grad_bn)
    grad_norm = jnp.sqrt(squares)
    factor = jnp.minimum(1.0, clip_norm / (grad_norm + 1e-06))
    new_w_cam, new_m_cam, new_v_cam = adam_update(w_cam, factor * grad_wc, m_cam, v_cam, learn_rate)
    new_w_lidar, new_m_lidar, new_v_lidar = adam_update(w_lidar, factor * grad_wl, m_lidar, v_lidar, learn_rate)
    new_w_mid, new_m_mid, new_v_mid = adam_update(w_mid, factor * grad_mid, m_mid, v_mid, learn_rate)
    new_bn, new_m_bn, new_v_bn = adam_update(bn_params, factor * grad_bn, m_bn, v_bn, norm_rate)
    return (mixed, grad_cam, grad_lidar, grad_norm, new_w_cam, new_m_cam, new_v_cam, new_w_lidar, new_m_lidar, new_v_lidar, new_w_mid, new_m_mid, new_v_mid, new_bn, new_m_bn, new_v_bn)
```

```python
import functools
import math

import jax
import jax.numpy as jnp
from jax import lax
from jax.experimental import pallas as pl
from jax.experimental.pallas import tpu as pltpu
from jax.sharding import PartitionSpec as P

STEP = 10


beta_one = 0.9
beta_two = 0.999
adam_eps = 1e-08
learn_rate = 0.02
norm_rate = 1.5
weight_decay = 0.01
norm_eps = 1e-05
clip_norm = 1.0

AXES = ("strip", "chan")
LANES = 128
VMEM_BYTES = 48 * 1024 * 1024

f32 = jnp.float32
bf16 = jnp.bfloat16


def round_up(value, step):
    return (value + step - 1) // step * step


def call(body, out_shape, scratch=(), smem=0, **options):
    def run(*operands):
        specs = [pl.BlockSpec(memory_space=pltpu.SMEM)] * smem
        specs += [pl.BlockSpec(memory_space=pltpu.VMEM)] * (len(operands) - smem)
        return pl.pallas_call(
            body,
            out_shape=out_shape,
            in_specs=specs,
            out_specs=jax.tree.map(lambda _: pl.BlockSpec(memory_space=pltpu.VMEM), out_shape),
            scratch_shapes=list(scratch),
            compiler_params=pltpu.CompilerParams(vmem_limit_bytes=VMEM_BYTES),
            **options,
        )(*operands)

    return run


def struct(shape, dtype):
    return jax.ShapeDtypeStruct(shape, dtype)


def cut(position):
    return slice(position * LANES, (position + 1) * LANES)


def sides(row):
    lane = lax.broadcasted_iota(jnp.int32, row.shape, 1)
    before = jnp.where(lane == 0, 0.0, pltpu.roll(row, 1, axis=1))
    after = jnp.where(lane == LANES - 1, 0.0, pltpu.roll(row, LANES - 1, axis=1))
    return before, after


def column_sums(parts):
    return jnp.concatenate([jnp.sum(part.T, axis=0, keepdims=True) for part in parts], axis=0)


def to_columns(rows):
    channels = rows[0].shape[1]
    rest = jnp.zeros((LANES - len(rows), channels), f32)
    return jnp.concatenate(list(rows) + [rest], axis=0).T


def matmul(left, right):
    return lax.dot_general(left, right, (((1,), (0,)), ((), ())), preferred_element_type=f32)


def matmul_nt(left, right):
    return lax.dot_general(left, right, (((1,), (1,)), ((), ())), preferred_element_type=f32)


def sigmoid(values):
    return 1.0 / (1.0 + jnp.exp(-values))


def moments(received, pixel_count):
    total = jnp.sum(received, axis=0)
    mean = total[0:1] / pixel_count
    variance = total[1:2] / pixel_count - mean * mean
    return mean, lax.rsqrt(variance + norm_eps)


def pool_body(grids, cells, chans, index_ref, feat_ref, out_ref, acc_ref):
    step = pl.program_id(0)
    rows = round_up(chans, 8)
    index = index_ref[...]
    high, low = index // cells, index % cells
    count = index.shape[1]
    feat = feat_ref[...].astype(f32)
    feat = jnp.concatenate([feat, jnp.zeros((rows - chans, count), f32)], axis=0)
    spread = jnp.concatenate(
        [jnp.where(high == grid, feat, 0.0) for grid in range(grids)], axis=0
    ).astype(bf16)
    table = (lax.broadcasted_iota(jnp.int32, (cells, count), 0) == low).astype(f32).astype(bf16)
    added = matmul_nt(spread, table)

    @pl.when(step == 0)
    def _():
        acc_ref[...] = added

    @pl.when(step > 0)
    def _():
        acc_ref[...] += added

    @pl.when(step == pl.num_programs(0) - 1)
    def _():
        out_ref[...] = acc_ref[...].reshape(grids, rows, cells)[:, :chans].astype(bf16)


def spread_body(grids, cells, chans, first, index_ref, grad_ref, out_ref):
    rows = round_up(chans, 8)
    index = index_ref[...]
    high, low = index // cells, index % cells
    count = index.shape[1]
    table = (lax.broadcasted_iota(jnp.int32, (cells, count), 0) == low).astype(f32).astype(bf16)
    grad = grad_ref[:, first : first + chans, :].astype(f32)
    grad = jnp.concatenate([grad, jnp.zeros((grids, rows - chans, cells), f32)], axis=1)
    picked = matmul(grad.reshape(grids * rows, cells).astype(bf16), table)
    total = jnp.zeros((rows, count), f32)
    for grid in range(grids):
        total = jnp.where(high == grid, picked[grid * rows : (grid + 1) * rows], total)
    out_ref[...] = total[:chans]


def pack_body(lid, cam, mid, one_width, lidar_ref, cam_ref, mid_ref, norm_ref, out_ref):
    rows = lidar_ref.shape[2]
    for a in range(3):
        base = a * one_width
        for b in range(3):
            out_ref[:, base + b * lid : base + (b + 1) * lid] = lidar_ref[a, b].astype(bf16)
        used = 3 * lid + 3 * cam
        rest = [cam_ref[a, b] for b in range(3)]
        if one_width > used:
            rest.append(jnp.zeros((rows, one_width - used), f32))
        out_ref[:, base + 3 * lid : base + one_width] = jnp.concatenate(rest, axis=1).astype(bf16)
        for b in range(3):
            start = 3 * one_width + (3 * a + b) * mid
            out_ref[:, start : start + mid] = mid_ref[a, b].astype(bf16)
    norm = norm_ref[...]
    high = norm.astype(bf16)
    left = norm - high.astype(f32)
    middle = left.astype(bf16)
    low = (left - middle.astype(f32)).astype(bf16)
    tail = jnp.concatenate(
        [high.astype(f32), middle.astype(f32), low.astype(f32), jnp.zeros((rows, LANES - 12), f32)],
        axis=1,
    )
    out_ref[:, 3 * one_width + 9 * mid :] = tail.astype(bf16)


def unpack_body(own, lid, cam, one_width, mid, masks, where_ref, *refs):
    parts, (one_ref, two_ref, one_t_ref, two_t_ref, norm_ref, all_ref) = refs[:-6], refs[-6:]
    chan = where_ref[0]
    place = 0
    for part in parts:
        for j in range(part.shape[0]):
            row = pl.multiple_of((chan ^ masks[place]) * own, own)
            all_ref[pl.ds(row, own), :] = part[j]
            place += 1
    one_ref[...] = all_ref[:, : 3 * one_width]
    two_t_ref[...] = all_ref[:, 3 * one_width : 3 * one_width + 9 * mid]
    tail = all_ref[:, 3 * one_width + 9 * mid :].astype(f32)
    norm = tail[:, 0:4] + tail[:, 4:8] + tail[:, 8:12]
    norm_ref[...] = jnp.concatenate([norm, jnp.zeros((norm.shape[0], LANES - 4), f32)], axis=1)
    outs = mid
    for a in range(3):
        for b in range(3):
            to = slice((3 * a + b) * outs, (3 * a + b + 1) * outs)
            start = a * one_width + b * lid
            one_t_ref[0:lid, to] = all_ref[:, start : start + lid].T
            start = 3 * one_width + (3 * a + b) * mid
            two_ref[:, to] = all_ref[:, start : start + mid].T
        start = a * one_width + 3 * lid
        turned = all_ref[:, start : start + one_width - 3 * lid].T
        for b in range(3):
            to = slice((3 * a + b) * outs, (3 * a + b + 1) * outs)
            one_t_ref[lid : lid + cam, to] = turned[b * cam : (b + 1) * cam]


def edge_rows(edge_ref, place_ref, groups, first, last):
    if groups == 2:
        edge_ref[0] = jnp.where(place_ref[1] == 0, last, first)
    else:
        edge_ref[0] = last
        edge_ref[1] = first


def first_body(
    cfg, place_ref, got_ref, above_ref, below_ref, kernel_ref,
    stack_ref, cot_ref, out_ref, sums_ref, edge_ref,
):
    nc, spg, rows, lid, cam, lid_own, cam_own, one_width, groups = cfg
    per_strip = rows // spg
    has_above = place_ref[1] > 0
    has_below = place_ref[1] < groups - 1
    cam_at = 2 * lid_own

    def take(p, first, count):
        if p == 0:
            pieces = [above_ref[c, first : first + count, :] for c in range(nc)]
        elif p == rows + 1:
            pieces = [below_ref[c, first : first + count, :] for c in range(nc)]
        else:
            s, r = (p - 1) // per_strip, (p - 1) % per_strip
            pieces = [got_ref[s * nc + c, first : first + count, cut(r)] for c in range(nc)]
        row = jnp.concatenate([piece.astype(f32) for piece in pieces], axis=0)
        if p == 0:
            row = jnp.where(has_above, row, 0.0)
        if p == rows + 1:
            row = jnp.where(has_below, row, 0.0)
        return row

    used = 3 * lid + 3 * cam
    if one_width > used:
        stack_ref[used:, :] = jnp.zeros((one_width - used, (rows + 2) * LANES), bf16)
    for p in range(rows + 2):
        row = take(p, 0, lid_own)
        for b, shifted in zip((0, 2, 1), (*sides(row), row), strict=True):
            stack_ref[b * lid : (b + 1) * lid, cut(p)] = shifted.astype(bf16)
        row = take(p, cam_at, cam_own)
        for b, shifted in zip((0, 2, 1), (*sides(row), row), strict=True):
            start = 3 * lid + b * cam
            stack_ref[start : start + cam, cut(p)] = shifted.astype(bf16)
        cot_ref[:, cut(p)] = take(p, lid_own, lid_own).astype(bf16)
    total = None
    for a in range(3):
        term = matmul(
            kernel_ref[:, a * one_width : (a + 1) * one_width],
            stack_ref[:, a * LANES : (a + rows) * LANES],
        )
        total = term if total is None else total + term
    finish_sums(total, rows, out_ref, sums_ref, edge_ref, place_ref, groups)


def finish_sums(total, rows, out_ref, sums_ref, edge_ref, place_ref, groups):
    out_ref[...] = total
    sums = squares = None
    for q in range(rows):
        row = total[:, cut(q)]
        sums = row if sums is None else sums + row
        squares = row * row if squares is None else squares + row * row
    sums_ref[...] = column_sums([sums, squares])
    edge_rows(edge_ref, place_ref, groups, total[:, cut(0)], total[:, cut(rows - 1)])


def second_body(
    cfg, place_ref, raw_ref, above_ref, below_ref, stats_ref, norm_ref, kernel_ref,
    out_ref, sums_ref, edge_ref, hidden_ref, means_ref, stack_ref,
):
    rows, chans, groups, pixel_count = cfg
    mean, inv = moments(stats_ref[...], pixel_count)
    columns = to_columns([mean, inv])
    means_ref[...] = columns
    mean, inv = columns[:, 0:1], columns[:, 1:2]
    gain, shift = norm_ref[:, 0:1], norm_ref[:, 1:2]
    for p in range(rows + 2):
        if p == 0:
            raw = above_ref[...]
        elif p == rows + 1:
            raw = below_ref[...]
        else:
            raw = raw_ref[:, cut(p - 1)]
        act = gain * ((raw - mean) * inv) + shift
        hidden = act * sigmoid(act)
        if p == 0:
            hidden = jnp.where(place_ref[1] > 0, hidden, 0.0)
        elif p == rows + 1:
            hidden = jnp.where(place_ref[1] < groups - 1, hidden, 0.0)
        else:
            hidden_ref[:, cut(p - 1)] = hidden
        for b, shifted in zip((0, 2, 1), (*sides(hidden), hidden), strict=True):
            stack_ref[b * chans : (b + 1) * chans, cut(p)] = shifted.astype(bf16)
    total = None
    for a in range(3):
        term = matmul(
            kernel_ref[:, a * 3 * chans : (a + 1) * 3 * chans],
            stack_ref[:, a * LANES : (a + rows) * LANES],
        )
        total = term if total is None else total + term
    finish_sums(total, rows, out_ref, sums_ref, edge_ref, place_ref, groups)


def slope_body(
    cfg, place_ref, raw_ref, above_ref, below_ref, stats_ref, norm_ref, cot_ref, hidden_ref,
    slope_ref, sums_ref, mixed_ref, means_ref,
):
    rows, chans, own, spg, nc, groups, pixel_count = cfg
    per_strip = rows // spg
    mean, inv = moments(stats_ref[...], pixel_count)
    columns = to_columns([mean, inv])
    means_ref[...] = columns
    mean, inv = columns[:, 0:1], columns[:, 1:2]
    gain, shift = norm_ref[:, 2:3], norm_ref[:, 3:4]
    shift_sum = gain_sum = None
    for p in range(rows + 2):
        if p == 0:
            raw = above_ref[...]
        elif p == rows + 1:
            raw = below_ref[...]
        else:
            raw = raw_ref[:, cut(p - 1)]
        centred = (raw - mean) * inv
        act = gain * centred + shift
        gate = sigmoid(act)
        slope = cot_ref[:, cut(p)].astype(f32) * (gate * (1.0 + act * (1.0 - gate)))
        slope_ref[:, cut(p)] = slope
        if 0 < p <= rows:
            shift_sum = slope if shift_sum is None else shift_sum + slope
            term = slope * centred
            gain_sum = term if gain_sum is None else gain_sum + term
            mixed = (hidden_ref[:, cut(p - 1)] + act * gate).astype(bf16)
            s, r = (p - 1) // per_strip, (p - 1) % per_strip
            for c in range(nc):
                mixed_ref[s * nc + c, :, cut(r)] = mixed[c * own : (c + 1) * own]
    sums_ref[...] = column_sums([shift_sum, gain_sum])


def mid_back_body(
    cfg, place_ref, slope_ref, raw_ref, above_ref, below_ref, means_two_ref, stats_ref, norm_ref,
    kernel_ref, raw_one_ref, means_one_ref, cot_ref, hidden_ref,
    out_ref, sums_ref, edge_ref, keep_ref, send_ref, grads_ref, stack_ref, order_ref,
):
    rows, chans, own, nc, groups, pixel_count = cfg
    total = jnp.sum(stats_ref[...], axis=0)
    grads_ref[...] = total
    columns = to_columns([total[0:1] / pixel_count, total[1:2] / pixel_count])
    shift_mean, gain_mean = columns[:, 0:1], columns[:, 1:2]
    mean, inv = means_two_ref[:, 0:1], means_two_ref[:, 1:2]
    scale = norm_ref[:, 2:3] * inv
    for p in range(rows + 2):
        if p == 0:
            raw = above_ref[...]
        elif p == rows + 1:
            raw = below_ref[...]
        else:
            raw = raw_ref[:, cut(p - 1)]
        centred = (raw - mean) * inv
        grad = scale * (slope_ref[:, cut(p)] - shift_mean - centred * gain_mean)
        if p == 0:
            grad = jnp.where(place_ref[1] > 0, grad, 0.0)
        elif p == rows + 1:
            grad = jnp.where(place_ref[1] < groups - 1, grad, 0.0)
        for b, shifted in zip((2, 0, 1), (*sides(grad), grad), strict=True):
            stack_ref[b * chans : (b + 1) * chans, cut(p)] = shifted.astype(bf16)
    back = None
    for a in range(3):
        term = matmul(
            kernel_ref[:, a * 3 * chans : (a + 1) * 3 * chans],
            stack_ref[:, (2 - a) * LANES : (2 - a + rows) * LANES],
        )
        back = term if back is None else back + term
    mean, inv = means_one_ref[:, 0:1], means_one_ref[:, 1:2]
    gain, shift = norm_ref[:, 0:1], norm_ref[:, 1:2]
    shift_sum = gain_sum = None
    slopes = []
    for q in range(rows):
        centred = (raw_one_ref[:, cut(q)] - mean) * inv
        act = gain * centred + shift
        gate = sigmoid(act)
        grad = back[:, cut(q)] + cot_ref[:, cut(q + 1)].astype(f32)
        slope = grad * (gate * (1.0 + act * (1.0 - gate)))
        out_ref[:, cut(q)] = slope
        if q in (0, rows - 1):
            slopes.append(slope)
        shift_sum = slope if shift_sum is None else shift_sum + slope
        term = slope * centred
        gain_sum = term if gain_sum is None else gain_sum + term
    sums_ref[...] = column_sums([shift_sum, gain_sum])
    edge_rows(edge_ref, place_ref, groups, slopes[0], slopes[-1])
    order_ref[...] = hidden_ref[...].astype(bf16)
    low = place_ref[0] & 1
    halves = []
    for side in (low, 1 - low):
        for pair in range(nc // 2):
            start = pl.multiple_of((2 * pair + side) * own, own)
            halves.append(order_ref[pl.ds(start, own), :])
    ordered = jnp.concatenate(halves, axis=0)
    half = chans // 2
    for a in range(3):
        grad = matmul_nt(ordered, stack_ref[:, (2 - a) * LANES : (2 - a + rows) * LANES])
        grad = grad.astype(bf16)
        to = slice(a * 3 * chans, (a + 1) * 3 * chans)
        keep_ref[:, to] = grad[:half]
        send_ref[:, to] = grad[half:]


def first_back_body(
    cfg, place_ref, slope_ref, slope_above_ref, slope_below_ref, raw_ref, above_ref, below_ref,
    means_ref, stats_ref, norm_ref, kernel_ref, cells_ref, mixed_ref, grads_two_ref,
    keep_ref, send_ref, back_ref, grads_ref, stack_ref,
):
    rows, chans, own, lid, cam, lid_own, cam_own, one_width, spg, nc, groups, pixel_count = cfg
    per_strip = rows // spg
    total = jnp.sum(stats_ref[...], axis=0)
    grads_ref[...] = jnp.concatenate(
        [total[1:2], total[0:1], grads_two_ref[1:2], grads_two_ref[0:1]], axis=0
    )
    columns = to_columns([total[0:1] / pixel_count, total[1:2] / pixel_count])
    shift_mean, gain_mean = columns[:, 0:1], columns[:, 1:2]
    mean, inv = means_ref[:, 0:1], means_ref[:, 1:2]
    scale = norm_ref[:, 0:1] * inv
    for p in range(rows + 2):
        if p == 0:
            raw, slope = above_ref[...], slope_above_ref[...]
        elif p == rows + 1:
            raw, slope = below_ref[...], slope_below_ref[...]
        else:
            raw, slope = raw_ref[:, cut(p - 1)], slope_ref[:, cut(p - 1)]
        grad = scale * (slope - shift_mean - (raw - mean) * inv * gain_mean)
        if p == 0:
            grad = jnp.where(place_ref[1] > 0, grad, 0.0)
        elif p == rows + 1:
            grad = jnp.where(place_ref[1] < groups - 1, grad, 0.0)
        for b, shifted in zip((2, 0, 1), (*sides(grad), grad), strict=True):
            stack_ref[b * chans : (b + 1) * chans, cut(p)] = shifted.astype(bf16)
    low = place_ref[0] & 1
    halves = []
    for side in (low, 1 - low):
        for pair in range(nc // 2):
            start = pl.multiple_of(chans + (2 * pair + side) * own, own)
            halves.append(stack_ref[pl.ds(start, own), LANES : (rows + 1) * LANES])
    ordered = jnp.concatenate(halves, axis=0)
    half = chans // 2
    for a in range(3):
        grad = matmul_nt(ordered, cells_ref[:, a * LANES : (a + rows) * LANES]).astype(bf16)
        to = slice(a * one_width, (a + 1) * one_width)
        keep_ref[:, to] = grad[:half]
        send_ref[:, to] = grad[half:]
    back = None
    for a in range(3):
        term = matmul(
            kernel_ref[:, a * 3 * chans : (a + 1) * 3 * chans],
            stack_ref[:, (2 - a) * LANES : (2 - a + rows) * LANES],
        )
        back = term if back is None else back + term
    for s in range(spg):
        cells = slice(s * per_strip * LANES, (s + 1) * per_strip * LANES)
        for c in range(nc):
            block = s * nc + c
            back_ref[block, 0:lid_own, :] = back[c * lid_own : (c + 1) * lid_own, cells].astype(bf16)
            back_ref[block, lid_own : 2 * lid_own, :] = mixed_ref[block]
            start = lid + c * cam_own
            back_ref[block, 2 * lid_own : 2 * lid_own + cam_own, :] = back[
                start : start + cam_own, cells
            ].astype(bf16)


def adam(weight, gradient, first, second, rate):
    first = beta_one * first + (1.0 - beta_one) * gradient
    second = beta_two * second + (1.0 - beta_two) * gradient * gradient
    fix_one = 1.0 - beta_one**STEP
    fix_two = 1.0 - beta_two**STEP
    stepped = first / fix_one / (jnp.sqrt(second / fix_two) + adam_eps)
    return weight - rate * (stepped + weight_decay * weight), first, second


def adam_body(lid, cam, mid, factor_ref, one_ref, two_ref, grad_ref, *refs):
    factor = factor_ref[0]
    ins, outs = refs[:12], refs[12:]
    (wc, mc, vc), (wl, ml, vl), (wm, mm, vm), (wb, mb, vb) = (ins[3 * i : 3 * i + 3] for i in range(4))
    oc, ol, om, ob = (outs[3 * i : 3 * i + 3] for i in range(4))

    def step(reads, writes, at, gradient, rate):
        weight, first, second = (ref[at] for ref in reads)
        for ref, value in zip(writes, adam(weight, factor * gradient, first, second, rate), strict=True):
            ref[at] = value

    for b in range(3):
        at = (0, b)
        step((wl, ml, vl), ol, at, one_ref[:, b * lid : (b + 1) * lid].astype(f32), learn_rate)
        step((wm, mm, vm), om, at, two_ref[:, b * mid : (b + 1) * mid].astype(f32), learn_rate)
    tail = one_ref[:, 3 * lid :].astype(f32)
    for b in range(3):
        step((wc, mc, vc), oc, (0, b), tail[:, b * cam : (b + 1) * cam], learn_rate)

    @pl.when(pl.program_id(0) == 0)
    def _():
        step((wb, mb, vb), ob, ..., grad_ref[...], norm_rate)


def shards(
    cam_feats,
    cell_index,
    lidar_bev,
    w_cam,
    w_lidar,
    w_mid,
    bn_params,
    cotangent,
    m_cam,
    v_cam,
    m_lidar,
    v_lidar,
    m_mid,
    v_mid,
    m_bn,
    v_bn,
):
    grids, lid_own, strip_rows, width = lidar_bev.shape
    cam_own, points = cam_feats.shape
    own = bn_params.shape[1]
    nc = lax.axis_size("chan")
    ns = lax.axis_size("strip")
    lid, cam, chans = nc * lid_own, nc * cam_own, nc * own
    spg = grids // nc
    groups = ns // spg
    members = spg * nc
    rows = spg * strip_rows
    cells = strip_rows * width
    pixel_count = float(grids * cells * ns)
    devices = ns * nc
    one_width = round_up(3 * lid + 3 * cam, 256)
    two_width = 3 * chans
    total_width = 3 * one_width + 3 * two_width
    chan = lax.axis_index("chan")
    group = lax.axis_index("strip") // spg
    place = jnp.stack([chan, group]).astype(jnp.int32)

    def within(member_of):
        return [member for g in range(groups) for member in member_of(g)]

    tile_groups = [[g * members + r for r in range(members)] for g in range(groups)]
    half_groups = [
        [(g * spg + s) * nc + 2 * pair + low for pair in range(nc // 2) for s in range(spg)]
        for g in range(groups)
        for low in range(2)
    ]
    strip_groups = [
        [(g * spg + s) * nc + c for s in range(spg)] for g in range(groups) for c in range(nc)
    ]

    def exchange(blocks, parts):
        return lax.all_to_all(blocks, AXES, 0, 0, axis_index_groups=parts, tiled=True)

    def everywhere(values):
        return lax.all_to_all(
            jnp.broadcast_to(values[None], (devices, *values.shape)), AXES, 0, 0, tiled=True
        )

    def chan_swap(values, bit):
        return lax.ppermute(values, "chan", [(c, c ^ bit) for c in range(nc)])

    def neighbours(edges):
        if groups == 1:
            return edges[0], edges[0]
        if groups == 2:
            pairs = [(i, (i + members) % devices) for i in range(devices)]
            other = lax.ppermute(edges[0], AXES, pairs)
            return other, other
        down = [(i, i + members) for i in range(devices - members)]
        up = [(i + members, i) for i in range(devices - members)]
        return lax.ppermute(edges[0], AXES, down), lax.ppermute(edges[1], AXES, up)

    edge_count = 2 if groups > 2 else 1

    turn = (0, 1, 3, 2)
    packed = call(
        functools.partial(pack_body, lid, cam, chans, one_width),
        struct((own, total_width + LANES), bf16),
    )(w_lidar.transpose(turn), w_cam.transpose(turn), w_mid, bn_params.T)
    parts, masks = [packed[None]], [0]
    bit = nc // 2
    while bit:
        stacked = parts[0] if len(parts) == 1 else jnp.concatenate(parts, axis=0)
        parts.append(chan_swap(stacked, bit))
        masks += [mask ^ bit for mask in masks]
        bit //= 2

    index_row = cell_index.reshape(1, points)
    block = math.gcd(points, 2048)
    pooled = pl.pallas_call(
        functools.partial(pool_body, grids, cells, cam_own),
        grid=(points // block,),
        in_specs=[
            pl.BlockSpec((1, block), lambda i: (0, i)),
            pl.BlockSpec((cam_own, block), lambda i: (0, i)),
        ],
        out_specs=pl.BlockSpec((grids, cam_own, cells), lambda i: (0, 0, 0)),
        out_shape=struct((grids, cam_own, cells), bf16),
        scratch_shapes=[pltpu.VMEM((grids * round_up(cam_own, 8), cells), f32)],
        compiler_params=pltpu.CompilerParams(vmem_limit_bytes=VMEM_BYTES),
    )(index_row, cam_feats)
    joined = jnp.concatenate(
        [
            lidar_bev.reshape(grids, lid_own, cells),
            cotangent.reshape(grids, own, cells),
            pooled,
        ],
        axis=1,
    )
    got = exchange(joined, tile_groups)
    depth = joined.shape[1]
    last = got[members - nc :, :, cells - width :]
    first = got[:nc, :, :width]
    if groups == 2:
        edges = jnp.where(group == 0, last, first)[None]
    else:
        edges = jnp.stack([last, first])
    above, below = neighbours(edges)

    kernel_one, kernel_two, kernel_one_t, kernel_two_t, norm = call(
        functools.partial(unpack_body, own, lid, cam, one_width, chans, masks),
        [
            struct((chans, 3 * one_width), bf16),
            struct((chans, 3 * two_width), bf16),
            struct((lid + cam, 3 * two_width), bf16),
            struct((chans, 3 * two_width), bf16),
            struct((chans, LANES), f32),
        ],
        scratch=[pltpu.VMEM((chans, total_width + LANES), bf16)],
        smem=1,
    )(place, *parts)

    area = rows * LANES
    wide = (rows + 2) * LANES
    cells_stack, cot, raw_one, sums_one, edges_one = call(
        functools.partial(
            first_body, (nc, spg, rows, lid, cam, lid_own, cam_own, one_width, groups)
        ),
        [
            struct((one_width, wide), bf16),
            struct((chans, wide), bf16),
            struct((chans, area), f32),
            struct((2, chans), f32),
            struct((edge_count, chans, LANES), f32),
        ],
        smem=1,
    )(place, got, above, below, kernel_one)

    above_one, below_one = neighbours(edges_one)
    stats_one = everywhere(sums_one)
    raw_two, sums_two, edges_two, hidden, means_one = call(
        functools.partial(second_body, (rows, chans, groups, pixel_count)),
        [
            struct((chans, area), f32),
            struct((2, chans), f32),
            struct((edge_count, chans, LANES), f32),
            struct((chans, area), f32),
            struct((chans, LANES), f32),
        ],
        scratch=[pltpu.VMEM((two_width, wide), bf16)],
        smem=1,
    )(place, raw_one, above_one, below_one, stats_one, norm, kernel_two)

    above_two, below_two = neighbours(edges_two)
    stats_two = everywhere(sums_two)
    slope_two, sums_three, mixed_blocks, means_two = call(
        functools.partial(slope_body, (rows, chans, own, spg, nc, groups, pixel_count)),
        [
            struct((chans, wide), f32),
            struct((2, chans), f32),
            struct((members, own, cells), bf16),
            struct((chans, LANES), f32),
        ],
        smem=1,
    )(place, raw_two, above_two, below_two, stats_two, norm, cot, hidden)

    stats_three = everywhere(sums_three)
    slope_one, sums_four, edges_four, keep_two, send_two, grads_two = call(
        functools.partial(mid_back_body, (rows, chans, own, nc, groups, pixel_count)),
        [
            struct((chans, area), f32),
            struct((2, chans), f32),
            struct((edge_count, chans, LANES), f32),
            struct((chans // 2, 3 * two_width), bf16),
            struct((chans // 2, 3 * two_width), bf16),
            struct((2, chans), f32),
        ],
        scratch=[pltpu.VMEM((two_width, wide), bf16), pltpu.VMEM((chans, area), bf16)],
        smem=1,
    )(
        place, slope_two, raw_two, above_two, below_two, means_two, stats_three, norm,
        kernel_two_t, raw_one, means_one, cot, hidden,
    )

    above_four, below_four = neighbours(edges_four)
    got_two = chan_swap(send_two, 1)
    stats_four = everywhere(sums_four)
    keep_one, send_one, back_blocks, grad_bn_all = call(
        functools.partial(
            first_back_body,
            (rows, chans, own, lid, cam, lid_own, cam_own, one_width, spg, nc, groups, pixel_count),
        ),
        [
            struct((chans // 2, 3 * one_width), bf16),
            struct((chans // 2, 3 * one_width), bf16),
            struct((members, depth, cells), bf16),
            struct((4, chans), f32),
        ],
        scratch=[pltpu.VMEM((two_width, wide), bf16)],
        smem=1,
    )(
        place, slope_one, above_four, below_four, raw_one, above_one, below_one, means_one,
        stats_four, norm, kernel_one_t, cells_stack, mixed_blocks, grads_two,
    )

    got_one = chan_swap(send_one, 1)
    halved = jnp.concatenate(
        [
            (keep_one.astype(f32) + got_one.astype(f32)).astype(bf16),
            (keep_two.astype(f32) + got_two.astype(f32)).astype(bf16),
        ],
        axis=1,
    )
    piece_rows = own // spg
    pieces = exchange(halved.reshape(members // 2, piece_rows, total_width), half_groups)
    piece = jnp.sum(pieces.astype(f32), axis=0)
    shift = members
    while shift < devices:
        pairs = [(i, i ^ shift) for i in range(devices)]
        sent = piece.astype(bf16)
        piece = sent.astype(f32) + lax.ppermute(sent, AXES, pairs).astype(f32)
        shift *= 2
    piece = piece.astype(bf16)
    own_grads = exchange(
        jnp.broadcast_to(piece[None], (spg, piece_rows, total_width)), strip_groups
    ).reshape(own, total_width)
    grad_bn = lax.dynamic_slice(grad_bn_all, (0, chan * own), (4, own))
    squares = jnp.sum(jnp.square(own_grads.astype(f32))) + jnp.sum(grad_bn * grad_bn)
    bit = 1
    while bit < nc:
        squares = squares + chan_swap(squares, bit)
        bit *= 2
    grad_norm = jnp.sqrt(squares)
    factor = jnp.minimum(1.0, clip_norm / (grad_norm + 1e-06))

    home = exchange(back_blocks, tile_groups)
    grad_lidar = home[:, :lid_own].astype(f32).reshape(lidar_bev.shape)
    mixed = home[:, lid_own : lid_own + own].astype(f32).reshape(cotangent.shape)
    grad_cam = pl.pallas_call(
        functools.partial(spread_body, grids, cells, cam_own, lid_own + own),
        grid=(points // block,),
        in_specs=[
            pl.BlockSpec((1, block), lambda i: (0, i)),
            pl.BlockSpec((grids, depth, cells), lambda i: (0, 0, 0)),
        ],
        out_specs=pl.BlockSpec((cam_own, block), lambda i: (0, i)),
        out_shape=struct((cam_own, points), f32),
        compiler_params=pltpu.CompilerParams(vmem_limit_bytes=VMEM_BYTES),
    )(index_row, home)

    tall = lambda array: array.transpose(turn)
    state = [
        *(tall(array) for array in (w_cam, m_cam, v_cam)),
        *(tall(array) for array in (w_lidar, m_lidar, v_lidar)),
        w_mid, m_mid, v_mid, bn_params, m_bn, v_bn,
    ]
    state_specs = [
        pl.BlockSpec((1, *array.shape[1:]), lambda a: (a, 0, 0, 0))
        if array.ndim == 4
        else pl.BlockSpec(array.shape, lambda a: (0, 0))
        for array in state
    ]
    updated = pl.pallas_call(
        functools.partial(adam_body, lid, cam, chans),
        grid=(3,),
        in_specs=[
            pl.BlockSpec(memory_space=pltpu.SMEM),
            pl.BlockSpec((own, one_width), lambda a: (0, a)),
            pl.BlockSpec((own, two_width), lambda a: (0, a)),
            pl.BlockSpec((4, own), lambda a: (0, 0)),
            *state_specs,
        ],
        out_specs=state_specs,
        out_shape=[struct(array.shape, f32) for array in state],
        compiler_params=pltpu.CompilerParams(vmem_limit_bytes=VMEM_BYTES),
    )(
        factor.reshape(1), own_grads[:, : 3 * one_width], own_grads[:, 3 * one_width :], grad_bn, *state
    )
    turned = [tall(array) for array in updated[:6]]
    return (mixed, grad_cam, grad_lidar, grad_norm, *turned, *updated[6:])


def solution(mesh):
    return jax.shard_map(
        shards,
        mesh=mesh,
        in_specs=(
            P("chan", "strip"),
            P("strip"),
            P(None, "chan", "strip", None),
            P(None, None, None, "chan"),
            P(None, None, None, "chan"),
            P(None, None, "chan", None),
            P(None, "chan"),
            P(None, "chan", "strip", None),
            P(None, None, None, "chan"),
            P(None, None, None, "chan"),
            P(None, None, None, "chan"),
            P(None, None, None, "chan"),
            P(None, None, "chan", None),
            P(None, None, "chan", None),
            P(None, "chan"),
            P(None, "chan"),
        ),
        out_specs=(
            P(None, "chan", "strip", None),
            P("chan", "strip"),
            P(None, "chan", "strip", None),
            P(),
            P(None, None, None, "chan"),
            P(None, None, None, "chan"),
            P(None, None, None, "chan"),
            P(None, None, None, "chan"),
            P(None, None, None, "chan"),
            P(None, None, None, "chan"),
            P(None, None, "chan", None),
            P(None, None, "chan", None),
            P(None, None, "chan", None),
            P(None, "chan"),
            P(None, "chan"),
            P(None, "chan"),
        ),
        check_vma=False,
    )
```

```python
import functools
import math

import jax
import jax.numpy as jnp
from jax import lax
from jax.experimental import pallas as pl
from jax.experimental.pallas import tpu as pltpu
from jax.sharding import PartitionSpec as P

STEP = 10


beta_one = 0.9
beta_two = 0.999
adam_eps = 1e-08
learn_rate = 0.02
norm_rate = 1.5
weight_decay = 0.01
norm_eps = 1e-05
clip_norm = 1.0

AXES = ("strip", "chan")
LANES = 128
VMEM_BYTES = 24 * 1024 * 1024
VMEM_MOST = 60 * 1024 * 1024

f32 = jnp.float32
bf16 = jnp.bfloat16


def round_up(value, step):
    return (value + step - 1) // step * step


def call(body, out_shape, scratch=(), smem=0, after=(), **options):
    waits = len(after)

    def run(*operands):
        specs = [pl.BlockSpec(memory_space=pltpu.SMEM)] * smem
        specs += [pl.BlockSpec(memory_space=pltpu.VMEM)] * (len(operands) - smem)
        specs = [pl.BlockSpec(memory_space=pl.ANY)] * waits + specs
        return pl.pallas_call(
            lambda *refs: body(*refs[waits:]),
            out_shape=out_shape,
            in_specs=specs,
            out_specs=jax.tree.map(lambda _: pl.BlockSpec(memory_space=pltpu.VMEM), out_shape),
            scratch_shapes=list(scratch),
            compiler_params=pltpu.CompilerParams(vmem_limit_bytes=VMEM_BYTES),
            **options,
        )(*after, *operands)

    return run


def struct(shape, dtype):
    return jax.ShapeDtypeStruct(shape, dtype)


def cut(position):
    return slice(position * LANES, (position + 1) * LANES)


def sides(row):
    lane = lax.broadcasted_iota(jnp.int32, row.shape, 1)
    before = jnp.where(lane == 0, 0.0, pltpu.roll(row, 1, axis=1))
    after = jnp.where(lane == LANES - 1, 0.0, pltpu.roll(row, LANES - 1, axis=1))
    return before, after


def column_sums(parts):
    return jnp.concatenate([jnp.sum(part.T, axis=0, keepdims=True) for part in parts], axis=0)


def for_all(ref, values):
    ref[...] = jnp.broadcast_to(values[None], ref.shape)


def to_columns(rows):
    channels = rows[0].shape[1]
    rest = jnp.zeros((LANES - len(rows), channels), f32)
    return jnp.concatenate(list(rows) + [rest], axis=0).T


def matmul(left, right):
    return lax.dot_general(left, right, (((1,), (0,)), ((), ())), preferred_element_type=f32)


def matmul_nt(left, right):
    return lax.dot_general(left, right, (((1,), (1,)), ((), ())), preferred_element_type=f32)


def sigmoid(values):
    return 1.0 / (1.0 + jnp.exp(-values))


def moments(received, pixel_count):
    total = jnp.sum(received, axis=0)
    mean = total[0:1] / pixel_count
    variance = total[1:2] / pixel_count - mean * mean
    return mean, lax.rsqrt(variance + norm_eps)


def pool_body(grids, cells, chans, index_ref, feat_ref, out_ref, acc_ref):
    step = pl.program_id(0)
    rows = round_up(chans, 8)
    index = index_ref[...]
    high, low = index // cells, index % cells
    count = index.shape[1]
    feat = feat_ref[...].astype(f32)
    feat = jnp.concatenate([feat, jnp.zeros((rows - chans, count), f32)], axis=0)
    spread = jnp.concatenate(
        [jnp.where(high == grid, feat, 0.0) for grid in range(grids)], axis=0
    ).astype(bf16)
    table = (lax.broadcasted_iota(jnp.int32, (cells, count), 0) == low).astype(f32).astype(bf16)
    added = matmul_nt(spread, table)

    @pl.when(step == 0)
    def _():
        acc_ref[...] = added

    @pl.when(step > 0)
    def _():
        acc_ref[...] += added

    @pl.when(step == pl.num_programs(0) - 1)
    def _():
        out_ref[...] = acc_ref[...].reshape(grids, rows, cells)[:, :chans].astype(bf16)


def spread_body(grids, cells, chans, first, index_ref, grad_ref, out_ref):
    rows = round_up(chans, 8)
    index = index_ref[...]
    high, low = index // cells, index % cells
    count = index.shape[1]
    table = (lax.broadcasted_iota(jnp.int32, (cells, count), 0) == low).astype(f32).astype(bf16)
    grad = grad_ref[:, first : first + chans, :].astype(f32)
    grad = jnp.concatenate([grad, jnp.zeros((grids, rows - chans, cells), f32)], axis=1)
    picked = matmul(grad.reshape(grids * rows, cells).astype(bf16), table)
    total = jnp.zeros((rows, count), f32)
    for grid in range(grids):
        total = jnp.where(high == grid, picked[grid * rows : (grid + 1) * rows], total)
    out_ref[...] = total[:chans]


def pack_body(
    lid, cam, mid, one_width, norm_ref, lidar_far, cam_far, mid_far, out_ref,
    lidar_ref, cam_ref, mid_ref, sems,
):
    rows = lidar_ref.shape[2]
    pairs = ((lidar_far, lidar_ref), (cam_far, cam_ref), (mid_far, mid_ref))
    copies = [
        [pltpu.make_async_copy(far.at[a], near.at[a], sems.at[i, a]) for i, (far, near) in enumerate(pairs)]
        for a in range(3)
    ]
    for group in copies:
        for copy in group:
            copy.start()
    for a in range(3):
        for copy in copies[a]:
            copy.wait()
        base = a * one_width
        for b in range(3):
            out_ref[:, base + b * lid : base + (b + 1) * lid] = lidar_ref[a, b].astype(bf16)
        used = 3 * lid + 3 * cam
        rest = [cam_ref[a, b] for b in range(3)]
        if one_width > used:
            rest.append(jnp.zeros((rows, one_width - used), f32))
        out_ref[:, base + 3 * lid : base + one_width] = jnp.concatenate(rest, axis=1).astype(bf16)
        for b in range(3):
            start = 3 * one_width + (3 * a + b) * mid
            out_ref[:, start : start + mid] = mid_ref[a, b].astype(bf16)
    norm = norm_ref[...]
    norm = jnp.concatenate([norm, jnp.zeros((LANES - norm.shape[0], rows), f32)], axis=0)
    norm = jnp.concatenate([norm, jnp.zeros((LANES, LANES - rows), f32)], axis=1).T[:rows, :4]
    high = norm.astype(bf16)
    left = norm - high.astype(f32)
    middle = left.astype(bf16)
    low = (left - middle.astype(f32)).astype(bf16)
    tail = jnp.concatenate(
        [high.astype(f32), middle.astype(f32), low.astype(f32), jnp.zeros((rows, LANES - 12), f32)],
        axis=1,
    )
    out_ref[:, 3 * one_width + 9 * mid :] = tail.astype(bf16)


def place_rows(own, masks, chan, parts, all_ref):
    place = 0
    for part in parts:
        for j in range(part.shape[0]):
            row = pl.multiple_of((chan ^ masks[place]) * own, own)
            all_ref[pl.ds(row, own), :] = part[j]
            place += 1


def unpack_body(own, one_width, two_width, masks, place_ref, *refs):
    parts, (one_ref, two_ref, norm_ref, all_ref) = refs[:-4], refs[-4:]
    place_rows(own, masks, place_ref[0], parts, all_ref)
    one_ref[...] = all_ref[:, : 3 * one_width]
    two_ref[...] = all_ref[:, 3 * one_width : 3 * (one_width + two_width)]
    tail = all_ref[:, 3 * (one_width + two_width) :].astype(f32)
    norm = tail[:, 0:4] + tail[:, 4:8] + tail[:, 8:12]
    norm_ref[...] = jnp.concatenate([norm, jnp.zeros((norm.shape[0], LANES - 4), f32)], axis=1)


def turn_body(lid, cam, one_width, outs, one_ref, two_t_ref, one_t_ref, two_ref):
    for t in range(9):
        at = slice(t * outs, (t + 1) * outs)
        two_ref[:, at] = two_t_ref[:, at].T
    for a in range(3):
        for b in range(3):
            to = slice((3 * a + b) * outs, (3 * a + b + 1) * outs)
            start = a * one_width + b * lid
            one_t_ref[0:lid, to] = one_ref[:, start : start + lid].T
        start = a * one_width + 3 * lid
        turned = one_ref[:, start : start + one_width - 3 * lid].T
        for b in range(3):
            to = slice((3 * a + b) * outs, (3 * a + b + 1) * outs)
            one_t_ref[lid : lid + cam, to] = turned[b * cam : (b + 1) * cam]


def edge_rows(edge_ref, place_ref, groups, first, last):
    if groups == 2:
        edge_ref[0] = jnp.where(place_ref[1] == 0, last, first)
    else:
        edge_ref[0] = last
        edge_ref[1] = first


def fill_stack(stack_ref, base, order, p, row):
    count = row.shape[0]
    for b, shifted in zip(order, (*sides(row), row), strict=True):
        start = base + b * count
        stack_ref[start : start + count, cut(p)] = shifted.astype(bf16)


FORWARD = (0, 2, 1)
BACKWARD = (2, 0, 1)


def first_body(cfg, got_ref, kernel_ref, stack_ref, cot_ref, part_ref):
    nc, spg, rows, lid, cam, lid_own, cam_own, one_width = cfg
    per_strip = rows // spg

    def take(q, first, count):
        s, r = q // per_strip, q % per_strip
        pieces = [got_ref[s * nc + c, first : first + count, cut(r)] for c in range(nc)]
        return jnp.concatenate([piece.astype(f32) for piece in pieces], axis=0)

    used = 3 * (lid + cam)
    stack_ref[:, cut(0)] = jnp.zeros((one_width, LANES), bf16)
    stack_ref[:, cut(rows + 1)] = jnp.zeros((one_width, LANES), bf16)
    if one_width > used:
        stack_ref[used:, :] = jnp.zeros((one_width - used, (rows + 2) * LANES), bf16)
    for q in range(rows):
        fill_stack(stack_ref, 0, FORWARD, q + 1, take(q, 0, lid_own))
        fill_stack(stack_ref, 3 * lid, FORWARD, q + 1, take(q, 2 * lid_own, cam_own))
        cot_ref[:, cut(q)] = take(q, lid_own, lid_own).astype(bf16)
    total = None
    for a in range(3):
        term = matmul(
            kernel_ref[:, a * one_width : (a + 1) * one_width],
            stack_ref[:, a * LANES : (a + rows) * LANES],
        )
        total = term if total is None else total + term
    part_ref[...] = total


def first_halo_body(
    cfg, place_ref, part_ref, above_ref, below_ref, kernel_ref,
    halo_ref, cot_ref, out_ref, sums_ref, edge_ref,
):
    nc, rows, lid, cam, lid_own, cam_own, one_width, groups = cfg
    has_above = place_ref[1] > 0
    has_below = place_ref[1] < groups - 1
    used = 3 * (lid + cam)
    if one_width > used:
        halo_ref[used:, :] = jnp.zeros((one_width - used, 2 * LANES), bf16)
    for side, (ref, given) in enumerate(((above_ref, has_above), (below_ref, has_below))):
        row = jnp.concatenate([ref[c, :lid_own].astype(f32) for c in range(nc)], axis=0)
        fill_stack(halo_ref, 0, FORWARD, side, jnp.where(given, row, 0.0))
        row = jnp.concatenate([ref[c, 2 * lid_own :].astype(f32) for c in range(nc)], axis=0)
        fill_stack(halo_ref, 3 * lid, FORWARD, side, jnp.where(given, row, 0.0))
        cot_ref[:, cut(side)] = jnp.concatenate([ref[c, lid_own : 2 * lid_own] for c in range(nc)], axis=0)
    lines = [part_ref[:, cut(q)] for q in range(rows)]
    lines[0] = lines[0] + matmul(kernel_ref[:, :one_width], halo_ref[:, cut(0)])
    lines[-1] = lines[-1] + matmul(kernel_ref[:, 2 * one_width :], halo_ref[:, cut(1)])
    finish_sums(lines, out_ref, sums_ref, edge_ref, place_ref, groups)


def finish_sums(lines, out_ref, sums_ref, edge_ref, place_ref, groups):
    sums = squares = None
    for q, row in enumerate(lines):
        out_ref[:, cut(q)] = row
        sums = row if sums is None else sums + row
        squares = row * row if squares is None else squares + row * row
    for_all(sums_ref, column_sums([sums, squares]))
    edge_rows(edge_ref, place_ref, groups, lines[0], lines[-1])


def second_body(
    cfg, place_ref, raw_ref, above_ref, below_ref, stats_ref, norm_ref, kernel_ref,
    out_ref, sums_ref, edge_ref, hidden_ref, means_ref, stack_ref,
):
    rows, chans, groups, pixel_count = cfg
    mean, inv = moments(stats_ref[...], pixel_count)
    columns = to_columns([mean, inv])
    means_ref[...] = columns
    mean, inv = columns[:, 0:1], columns[:, 1:2]
    gain, shift = norm_ref[:, 0:1], norm_ref[:, 1:2]
    for p in range(rows + 2):
        if p == 0:
            raw = above_ref[...]
        elif p == rows + 1:
            raw = below_ref[...]
        else:
            raw = raw_ref[:, cut(p - 1)]
        act = gain * ((raw - mean) * inv) + shift
        hidden = act * sigmoid(act)
        if p == 0:
            hidden = jnp.where(place_ref[1] > 0, hidden, 0.0)
        elif p == rows + 1:
            hidden = jnp.where(place_ref[1] < groups - 1, hidden, 0.0)
        else:
            hidden_ref[:, cut(p - 1)] = hidden
        fill_stack(stack_ref, 0, FORWARD, p, hidden)
    total = None
    for a in range(3):
        term = matmul(
            kernel_ref[:, a * 3 * chans : (a + 1) * 3 * chans],
            stack_ref[:, a * LANES : (a + rows) * LANES],
        )
        total = term if total is None else total + term
    lines = [total[:, cut(q)] for q in range(rows)]
    finish_sums(lines, out_ref, sums_ref, edge_ref, place_ref, groups)


def slope_body(
    cfg, place_ref, raw_ref, above_ref, below_ref, stats_ref, norm_ref, cot_ref, cot_halo_ref, hidden_ref,
    slope_ref, sums_ref, means_ref, mixed_ref,
):
    rows, own, spg, nc, pixel_count = cfg
    per_strip = rows // spg
    mean, inv = moments(stats_ref[...], pixel_count)
    columns = to_columns([mean, inv])
    means_ref[...] = columns
    mean, inv = columns[:, 0:1], columns[:, 1:2]
    gain, shift = norm_ref[:, 2:3], norm_ref[:, 3:4]
    shift_sum = gain_sum = None
    for p in range(rows + 2):
        if p == 0:
            raw, cot = above_ref[...], cot_halo_ref[:, cut(0)]
        elif p == rows + 1:
            raw, cot = below_ref[...], cot_halo_ref[:, cut(1)]
        else:
            raw, cot = raw_ref[:, cut(p - 1)], cot_ref[:, cut(p - 1)]
        centred = (raw - mean) * inv
        act = gain * centred + shift
        gate = sigmoid(act)
        slope = cot.astype(f32) * (gate * (1.0 + act * (1.0 - gate)))
        slope_ref[:, cut(p)] = slope
        if 0 < p <= rows:
            shift_sum = slope if shift_sum is None else shift_sum + slope
            term = slope * centred
            gain_sum = term if gain_sum is None else gain_sum + term
            mixed = (hidden_ref[:, cut(p - 1)] + act * gate).astype(bf16)
            s, r = (p - 1) // per_strip, (p - 1) % per_strip
            for c in range(nc):
                mixed_ref[s * nc + c, :, cut(r)] = mixed[c * own : (c + 1) * own]
    for_all(sums_ref, column_sums([shift_sum, gain_sum]))


def mid_back_body(
    cfg, place_ref, slope_ref, raw_ref, above_ref, below_ref, means_two_ref, stats_ref, norm_ref,
    kernel_ref, raw_one_ref, means_one_ref, cot_ref,
    out_ref, sums_ref, edge_ref, stack_ref, grads_ref,
):
    rows, chans, groups, pixel_count = cfg
    total = jnp.sum(stats_ref[...], axis=0)
    grads_ref[...] = total
    columns = to_columns([total[0:1] / pixel_count, total[1:2] / pixel_count])
    shift_mean, gain_mean = columns[:, 0:1], columns[:, 1:2]
    mean, inv = means_two_ref[:, 0:1], means_two_ref[:, 1:2]
    scale = norm_ref[:, 2:3] * inv
    for p in range(rows + 2):
        if p == 0:
            raw = above_ref[...]
        elif p == rows + 1:
            raw = below_ref[...]
        else:
            raw = raw_ref[:, cut(p - 1)]
        centred = (raw - mean) * inv
        grad = scale * (slope_ref[:, cut(p)] - shift_mean - centred * gain_mean)
        if p == 0:
            grad = jnp.where(place_ref[1] > 0, grad, 0.0)
        elif p == rows + 1:
            grad = jnp.where(place_ref[1] < groups - 1, grad, 0.0)
        fill_stack(stack_ref, 0, BACKWARD, p, grad)
    back = None
    for a in range(3):
        term = matmul(
            kernel_ref[:, a * 3 * chans : (a + 1) * 3 * chans],
            stack_ref[:, (2 - a) * LANES : (2 - a + rows) * LANES],
        )
        back = term if back is None else back + term
    mean, inv = means_one_ref[:, 0:1], means_one_ref[:, 1:2]
    gain, shift = norm_ref[:, 0:1], norm_ref[:, 1:2]
    shift_sum = gain_sum = None
    slopes = []
    for q in range(rows):
        centred = (raw_one_ref[:, cut(q)] - mean) * inv
        act = gain * centred + shift
        gate = sigmoid(act)
        grad = back[:, cut(q)] + cot_ref[:, cut(q)].astype(f32)
        slope = grad * (gate * (1.0 + act * (1.0 - gate)))
        out_ref[:, cut(q)] = slope
        if q in (0, rows - 1):
            slopes.append(slope)
        shift_sum = slope if shift_sum is None else shift_sum + slope
        term = slope * centred
        gain_sum = term if gain_sum is None else gain_sum + term
    for_all(sums_ref, column_sums([shift_sum, gain_sum]))
    edge_rows(edge_ref, place_ref, groups, slopes[0], slopes[-1])


def halves(place_ref, own, nc, rows_at):
    low = place_ref[0] & 1
    found = []
    for side in (low, 1 - low):
        for pair in range(nc // 2):
            found.append(rows_at(pl.multiple_of((2 * pair + side) * own, own)))
    return jnp.concatenate(found, axis=0)


def first_back_body(
    cfg, place_ref, slope_ref, slope_above_ref, slope_below_ref, raw_ref, above_ref, below_ref,
    means_ref, stats_ref, norm_ref, grads_two_ref, own_ref, halo_ref, hidden_ref, stack_two_ref,
    keep_ref, send_ref, stack_ref, grads_ref, squares_ref, cells_ref,
):
    rows, chans, own, nc, one_width, groups, pixel_count = cfg
    wide = (rows + 2) * LANES
    total = jnp.sum(stats_ref[...], axis=0)
    grads = jnp.concatenate(
        [total[1:2], total[0:1], grads_two_ref[1:2], grads_two_ref[0:1]], axis=0
    )
    grads_ref[...] = grads
    squares_ref[...] = jnp.sum(grads * grads).reshape(1, 1)
    columns = to_columns([total[0:1] / pixel_count, total[1:2] / pixel_count])
    shift_mean, gain_mean = columns[:, 0:1], columns[:, 1:2]
    mean, inv = means_ref[:, 0:1], means_ref[:, 1:2]
    scale = norm_ref[:, 0:1] * inv
    for p in range(rows + 2):
        if p == 0:
            raw, slope = above_ref[...], slope_above_ref[...]
        elif p == rows + 1:
            raw, slope = below_ref[...], slope_below_ref[...]
        else:
            raw, slope = raw_ref[:, cut(p - 1)], slope_ref[:, cut(p - 1)]
        grad = scale * (slope - shift_mean - (raw - mean) * inv * gain_mean)
        if p == 0:
            grad = jnp.where(place_ref[1] > 0, grad, 0.0)
        elif p == rows + 1:
            grad = jnp.where(place_ref[1] < groups - 1, grad, 0.0)
        fill_stack(stack_ref, 0, BACKWARD, p, grad)
    cells_ref[:, :LANES] = halo_ref[:, :LANES]
    cells_ref[:, LANES : wide - LANES] = own_ref[:, LANES : wide - LANES]
    cells_ref[:, wide - LANES :] = halo_ref[:, LANES:]
    half = chans // 2
    ordered = halves(
        place_ref, own, nc,
        lambda start: stack_ref[pl.ds(chans + start, own), LANES : (rows + 1) * LANES],
    )
    hidden = halves(place_ref, own, nc, lambda start: hidden_ref[pl.ds(start, own), :]).astype(bf16)
    for a in range(3):
        grad = matmul_nt(ordered, cells_ref[:, a * LANES : (a + rows) * LANES]).astype(bf16)
        to = slice(a * one_width, (a + 1) * one_width)
        keep_ref[:, to] = grad[:half]
        send_ref[:, to] = grad[half:]
        grad = matmul_nt(hidden, stack_two_ref[:, (2 - a) * LANES : (2 - a + rows) * LANES]).astype(bf16)
        start = 3 * one_width + a * 3 * chans
        keep_ref[:, start : start + 3 * chans] = grad[:half]
        send_ref[:, start : start + 3 * chans] = grad[half:]


def inputs_back_body(cfg, stack_ref, kernel_ref, mixed_ref, back_ref):
    rows, chans, lid, lid_own, cam_own, spg, nc = cfg
    per_strip = rows // spg
    back = None
    for a in range(3):
        term = matmul(
            kernel_ref[:, a * 3 * chans : (a + 1) * 3 * chans],
            stack_ref[:, (2 - a) * LANES : (2 - a + rows) * LANES],
        )
        back = term if back is None else back + term
    for s in range(spg):
        cells = slice(s * per_strip * LANES, (s + 1) * per_strip * LANES)
        for c in range(nc):
            block = s * nc + c
            back_ref[block, 0:lid_own, :] = back[c * lid_own : (c + 1) * lid_own, cells].astype(bf16)
            back_ref[block, lid_own : 2 * lid_own, :] = mixed_ref[block]
            start = lid + c * cam_own
            back_ref[block, 2 * lid_own : 2 * lid_own + cam_own, :] = back[
                start : start + cam_own, cells
            ].astype(bf16)


def adam(weight, gradient, first, second, rate):
    first = beta_one * first + (1.0 - beta_one) * gradient
    second = beta_two * second + (1.0 - beta_two) * gradient * gradient
    fix_one = 1.0 - beta_one**STEP
    fix_two = 1.0 - beta_two**STEP
    stepped = first / fix_one / (jnp.sqrt(second / fix_two) + adam_eps)
    return weight - rate * (stepped + weight_decay * weight), first, second


def add_body(mine_ref, other_ref, out_ref):
    out_ref[...] = (mine_ref[...].astype(f32) + other_ref[...].astype(f32)).astype(bf16)


def sum_body(pieces_ref, out_ref):
    out_ref[...] = jnp.sum(pieces_ref[...].astype(f32), axis=0).astype(bf16)


def merge_body(copies, mine_ref, other_ref, out_ref):
    width = mine_ref.shape[1]
    piece = (mine_ref[...].astype(f32) + other_ref[...].astype(f32)).astype(bf16)
    values = piece.astype(f32)
    squares = jnp.sum(values * values).reshape(1, 1)
    high = squares.astype(bf16).astype(f32)
    middle = (squares - high).astype(bf16).astype(f32)
    low = squares - high - middle
    shape = (piece.shape[0], LANES)
    row = lax.broadcasted_iota(jnp.int32, shape, 0)
    lane = lax.broadcasted_iota(jnp.int32, shape, 1)
    terms = jnp.where(lane == 0, high, jnp.where(lane == 1, middle, jnp.where(lane == 2, low, 0.0)))
    terms = jnp.where(row == 0, terms, 0.0).astype(bf16)
    for copy in range(copies):
        out_ref[copy, :, :width] = piece
        out_ref[copy, :, width:] = terms


def adam_body(lid, cam, mid, squares_ref, norm_squares_ref, grads_ref, norm_grad_ref, *refs):
    norm_ins, fars, refs = refs[:3], refs[3:12], refs[12:]
    norm_outs, far_outs, norm_ref, refs = refs[:3], refs[3:12], refs[12], refs[13:]
    nears, ins, outs = refs[:9], refs[9], refs[10]
    one_width = round_up(3 * lid + 3 * cam, 256)
    reads = [
        [pltpu.make_async_copy(fars[i].at[a], nears[i].at[a], ins.at[i, a]) for i in range(9)]
        for a in range(3)
    ]
    writes = [
        [pltpu.make_async_copy(nears[i].at[a], far_outs[i].at[a], outs.at[i, a]) for i in range(9)]
        for a in range(3)
    ]
    for group in reads:
        for copy in group:
            copy.start()
    norm = jnp.sqrt(squares_ref[...] + norm_squares_ref[...])
    norm_ref[...] = norm
    factor = jnp.minimum(1.0, clip_norm / (norm + 1e-06))

    def step(refs, results, at, gradient, rate):
        weight, first, second = (ref[at] for ref in refs)
        for ref, value in zip(results, adam(weight, factor * gradient, first, second, rate), strict=True):
            ref[at] = value

    step(norm_ins, norm_outs, ..., norm_grad_ref[...], norm_rate)
    for a in range(3):
        for copy in reads[a]:
            copy.wait()
        base = a * one_width
        tail = grads_ref[:, base + 3 * lid : base + one_width].astype(f32)
        for b in range(3):
            given = (
                tail[:, b * cam : (b + 1) * cam],
                grads_ref[:, base + b * lid : base + (b + 1) * lid].astype(f32),
                grads_ref[
                    :, 3 * one_width + (3 * a + b) * mid : 3 * one_width + (3 * a + b + 1) * mid
                ].astype(f32),
            )
            for i, gradient in enumerate(given):
                state = nears[3 * i : 3 * i + 3]
                step(state, state, (a, b), gradient, learn_rate)
        for copy in writes[a]:
            copy.start()
    for group in writes:
        for copy in group:
            copy.wait()


def shards(
    cam_feats,
    cell_index,
    lidar_bev,
    w_cam,
    w_lidar,
    w_mid,
    bn_params,
    cotangent,
    m_cam,
    v_cam,
    m_lidar,
    v_lidar,
    m_mid,
    v_mid,
    m_bn,
    v_bn,
):
    grids, lid_own, strip_rows, width = lidar_bev.shape
    cam_own, points = cam_feats.shape
    own = bn_params.shape[1]
    nc = lax.axis_size("chan")
    ns = lax.axis_size("strip")
    lid, cam, chans = nc * lid_own, nc * cam_own, nc * own
    spg = grids // nc
    groups = ns // spg
    members = spg * nc
    rows = spg * strip_rows
    cells = strip_rows * width
    pixel_count = float(grids * cells * ns)
    devices = ns * nc
    one_width = round_up(3 * lid + 3 * cam, 256)
    two_width = 3 * chans
    total_width = 3 * one_width + 3 * two_width
    chan = lax.axis_index("chan")
    group = lax.axis_index("strip") // spg
    place = jnp.stack([chan, group]).astype(jnp.int32)

    tile_groups = [[g * members + r for r in range(members)] for g in range(groups)]
    half_groups = [
        [(g * spg + s) * nc + 2 * pair + low for pair in range(nc // 2) for s in range(spg)]
        for g in range(groups)
        for low in range(2)
    ]
    strip_groups = [
        [(g * spg + s) * nc + c for s in range(spg)] for g in range(groups) for c in range(nc)
    ]

    def exchange(blocks, parts):
        return lax.all_to_all(blocks, AXES, 0, 0, axis_index_groups=parts, tiled=True)

    def everywhere(copies):
        return lax.all_to_all(copies, AXES, 0, 0, tiled=True)

    def chan_swap(values, bit):
        return lax.ppermute(values, "chan", [(c, c ^ bit) for c in range(nc)])

    def neighbours(edges):
        if groups == 1:
            return edges[0], edges[0]
        if groups == 2:
            pairs = [(i, (i + members) % devices) for i in range(devices)]
            other = lax.ppermute(edges[0], AXES, pairs)
            return other, other
        down = [(i, i + members) for i in range(devices - members)]
        up = [(i + members, i) for i in range(devices - members)]
        return lax.ppermute(edges[0], AXES, down), lax.ppermute(edges[1], AXES, up)

    edge_count = 2 if groups > 2 else 1

    area = rows * LANES
    wide = (rows + 2) * LANES
    def from_all_channels(packed):
        parts, masks = [packed[None]], [0]
        bit = nc // 2
        while bit:
            stacked = parts[0] if len(parts) == 1 else jnp.concatenate(parts, axis=0)
            parts.append(chan_swap(stacked, bit))
            masks += [mask ^ bit for mask in masks]
            bit //= 2
        return parts, masks

    def edge_cells(got):
        last = got[members - nc :, :, cells - width :]
        first = got[:nc, :, :width]
        if groups == 2:
            return jnp.where(group == 0, last, first)[None]
        return jnp.stack([last, first])

    sums_struct = struct((devices, 2, chans), f32)
    packed_width = total_width + LANES

    index_row = cell_index.reshape(1, points)
    block = math.gcd(points, 2048)
    pooled = pl.pallas_call(
        functools.partial(pool_body, grids, cells, cam_own),
        grid=(points // block,),
        in_specs=[
            pl.BlockSpec((1, block), lambda i: (0, i)),
            pl.BlockSpec((cam_own, block), lambda i: (0, i)),
        ],
        out_specs=pl.BlockSpec((grids, cam_own, cells), lambda i: (0, 0, 0)),
        out_shape=struct((grids, cam_own, cells), bf16),
        scratch_shapes=[pltpu.VMEM((grids * round_up(cam_own, 8), cells), f32)],
        compiler_params=pltpu.CompilerParams(vmem_limit_bytes=VMEM_BYTES),
    )(index_row, cam_feats)
    joined = jnp.concatenate(
        [
            lidar_bev.reshape(grids, lid_own, cells),
            cotangent.reshape(grids, own, cells),
            pooled,
        ],
        axis=1,
    )
    got = exchange(joined, tile_groups)
    above, below = neighbours(edge_cells(got))

    turn = (0, 1, 3, 2)
    far = pl.BlockSpec(memory_space=pltpu.HBM)
    near = pl.BlockSpec(memory_space=pltpu.VMEM)
    weights = [w_lidar.transpose(turn), w_cam.transpose(turn), w_mid]
    packed = pl.pallas_call(
        functools.partial(pack_body, lid, cam, chans, one_width),
        in_specs=[near, far, far, far],
        out_specs=near,
        out_shape=struct((own, packed_width), bf16),
        scratch_shapes=[
            *(pltpu.VMEM(weight.shape, f32) for weight in weights),
            pltpu.SemaphoreType.DMA((3, 3)),
        ],
        compiler_params=pltpu.CompilerParams(vmem_limit_bytes=VMEM_MOST),
    )(bn_params, *weights)
    parts, masks = from_all_channels(packed)
    kernel_one, kernel_two_t, norm = call(
        functools.partial(unpack_body, own, one_width, two_width, masks),
        [
            struct((chans, 3 * one_width), bf16),
            struct((chans, 3 * two_width), bf16),
            struct((chans, LANES), f32),
        ],
        scratch=[pltpu.VMEM((chans, packed_width), bf16)],
        smem=1,
    )(place, *parts)

    kernel_one_t, kernel_two = call(
        functools.partial(turn_body, lid, cam, one_width, chans),
        [struct((lid + cam, 3 * two_width), bf16), struct((chans, 3 * two_width), bf16)],
    )(kernel_one, kernel_two_t)
    own_stack, cot, part_one = call(
        functools.partial(first_body, (nc, spg, rows, lid, cam, lid_own, cam_own, one_width)),
        [
            struct((one_width, wide), bf16),
            struct((chans, area), bf16),
            struct((chans, area), f32),
        ],
    )(got, kernel_one)
    halo_stack, cot_halo, raw_one, sums_one, edges_one = call(
        functools.partial(
            first_halo_body, (nc, rows, lid, cam, lid_own, cam_own, one_width, groups)
        ),
        [
            struct((one_width, 2 * LANES), bf16),
            struct((chans, 2 * LANES), bf16),
            struct((chans, area), f32),
            sums_struct,
            struct((edge_count, chans, LANES), f32),
        ],
        smem=1,
        after=(kernel_one_t, kernel_two),
    )(place, part_one, above, below, kernel_one)

    above_one, below_one = neighbours(edges_one)
    stats_one = everywhere(sums_one)
    raw_two, sums_two, edges_two, hidden, means_one = call(
        functools.partial(second_body, (rows, chans, groups, pixel_count)),
        [
            struct((chans, area), f32),
            sums_struct,
            struct((edge_count, chans, LANES), f32),
            struct((chans, area), f32),
            struct((chans, LANES), f32),
        ],
        scratch=[pltpu.VMEM((two_width, wide), bf16)],
        smem=1,
    )(place, raw_one, above_one, below_one, stats_one, norm, kernel_two)

    above_two, below_two = neighbours(edges_two)
    stats_two = everywhere(sums_two)
    slope_two, sums_three, means_two, mixed_blocks = call(
        functools.partial(slope_body, (rows, own, spg, nc, pixel_count)),
        [
            struct((chans, wide), f32),
            sums_struct,
            struct((chans, LANES), f32),
            struct((members, own, cells), bf16),
        ],
        smem=1,
    )(place, raw_two, above_two, below_two, stats_two, norm, cot, cot_halo, hidden)

    stats_three = everywhere(sums_three)
    slope_one, sums_four, edges_four, grad_stack, grads_two = call(
        functools.partial(mid_back_body, (rows, chans, groups, pixel_count)),
        [
            struct((chans, area), f32),
            sums_struct,
            struct((edge_count, chans, LANES), f32),
            struct((two_width, wide), bf16),
            struct((2, chans), f32),
        ],
        smem=1,
    )(
        place, slope_two, raw_two, above_two, below_two, means_two, stats_three, norm,
        kernel_two_t, raw_one, means_one, cot,
    )

    above_four, below_four = neighbours(edges_four)
    stats_four = everywhere(sums_four)
    keep, send, grad_stack_one, grad_bn_all, norm_squares = call(
        functools.partial(
            first_back_body, (rows, chans, own, nc, one_width, groups, pixel_count)
        ),
        [
            struct((chans // 2, total_width), bf16),
            struct((chans // 2, total_width), bf16),
            struct((two_width, wide), bf16),
            struct((4, chans), f32),
            struct((1, 1), f32),
        ],
        scratch=[pltpu.VMEM((one_width, wide), bf16)],
        smem=1,
    )(
        place, slope_one, above_four, below_four, raw_one, above_one, below_one, means_one,
        stats_four, norm, grads_two, own_stack, halo_stack, hidden, grad_stack,
    )
    back_blocks = call(
        functools.partial(inputs_back_body, (rows, chans, lid, lid_own, cam_own, spg, nc)),
        struct((members, lid_own + own + cam_own, cells), bf16),
    )(grad_stack_one, kernel_one_t, mixed_blocks)
    home = exchange(back_blocks, tile_groups)

    halved = call(add_body, struct(keep.shape, bf16), after=(back_blocks,))(keep, chan_swap(send, 1))
    piece_rows = own // spg
    pieces = exchange(halved.reshape(members // 2, piece_rows, total_width), half_groups)
    piece = call(sum_body, struct((piece_rows, total_width), bf16))(pieces)
    other = jnp.zeros_like(piece)
    shift = members
    while shift < devices:
        if shift > members:
            piece = (piece.astype(f32) + other.astype(f32)).astype(bf16)
        other = lax.ppermute(piece, AXES, [(i, i ^ shift) for i in range(devices)])
        shift *= 2
    merged = call(
        functools.partial(merge_body, spg), struct((spg, piece_rows, packed_width), bf16)
    )(piece, other)
    merged = exchange(merged, strip_groups)
    squares = jnp.sum(merged[:, 0, total_width : total_width + 3].astype(f32)).reshape(1, 1)
    own_grads = merged.reshape(own, packed_width)
    bit = 1
    while bit < nc:
        squares = squares + chan_swap(squares, bit)
        bit *= 2
    grad_bn = lax.dynamic_slice(grad_bn_all, (0, chan * own), (4, own))

    depth = back_blocks.shape[1]
    grad_lidar = home[:, :lid_own].astype(f32).reshape(lidar_bev.shape)
    mixed = home[:, lid_own : lid_own + own].astype(f32).reshape(cotangent.shape)
    grad_cam = pl.pallas_call(
        functools.partial(spread_body, grids, cells, cam_own, lid_own + own),
        grid=(points // block,),
        in_specs=[
            pl.BlockSpec((1, block), lambda i: (0, i)),
            pl.BlockSpec((grids, depth, cells), lambda i: (0, 0, 0)),
        ],
        out_specs=pl.BlockSpec((cam_own, block), lambda i: (0, i)),
        out_shape=struct((cam_own, points), f32),
        compiler_params=pltpu.CompilerParams(vmem_limit_bytes=VMEM_BYTES),
    )(index_row, home)

    tall = lambda array: array.transpose(turn)
    state = [
        *(tall(array) for array in (w_cam, m_cam, v_cam)),
        *(tall(array) for array in (w_lidar, m_lidar, v_lidar)),
        w_mid, m_mid, v_mid,
    ]
    norm_state = [bn_params, m_bn, v_bn]
    *updated, grad_norm = pl.pallas_call(
        functools.partial(adam_body, lid, cam, chans),
        in_specs=[near] * 7 + [far] * 9,
        out_specs=[near] * 3 + [far] * 9 + [near],
        out_shape=[struct(array.shape, f32) for array in norm_state + state] + [struct((1, 1), f32)],
        scratch_shapes=[
            *(pltpu.VMEM(array.shape, f32) for array in state),
            pltpu.SemaphoreType.DMA((9, 3)),
            pltpu.SemaphoreType.DMA((9, 3)),
        ],
        compiler_params=pltpu.CompilerParams(vmem_limit_bytes=VMEM_MOST),
    )(squares, norm_squares, own_grads, grad_bn, *norm_state, *state)
    turned = [tall(array) for array in updated[3:9]]
    return (mixed, grad_cam, grad_lidar, grad_norm.reshape(()), *turned, *updated[9:], *updated[:3])


def solution(mesh):
    return jax.shard_map(
        shards,
        mesh=mesh,
        in_specs=(
            P("chan", "strip"),
            P("strip"),
            P(None, "chan", "strip", None),
            P(None, None, None, "chan"),
            P(None, None, None, "chan"),
            P(None, None, "chan", None),
            P(None, "chan"),
            P(None, "chan", "strip", None),
            P(None, None, None, "chan"),
            P(None, None, None, "chan"),
            P(None, None, None, "chan"),
            P(None, None, None, "chan"),
            P(None, None, "chan", None),
            P(None, None, "chan", None),
            P(None, "chan"),
            P(None, "chan"),
        ),
        out_specs=(
            P(None, "chan", "strip", None),
            P("chan", "strip"),
            P(None, "chan", "strip", None),
            P(),
            P(None, None, None, "chan"),
            P(None, None, None, "chan"),
            P(None, None, None, "chan"),
            P(None, None, None, "chan"),
            P(None, None, None, "chan"),
            P(None, None, None, "chan"),
            P(None, None, "chan", None),
            P(None, None, "chan", None),
            P(None, None, "chan", None),
            P(None, "chan"),
            P(None, "chan"),
            P(None, "chan"),
        ),
        check_vma=False,
    )
```

```python
import functools
import math

import jax
import jax.numpy as jnp
from jax import lax
from jax.experimental import pallas as pl
from jax.experimental.pallas import tpu as pltpu
from jax.sharding import PartitionSpec as P

STEP = 10


beta_one = 0.9
beta_two = 0.999
adam_eps = 1e-08
learn_rate = 0.02
norm_rate = 1.5
weight_decay = 0.01
norm_eps = 1e-05
clip_norm = 1.0

AXES = ("strip", "chan")
LANES = 128
VMEM_BYTES = 24 * 1024 * 1024
VMEM_MOST = 60 * 1024 * 1024

f32 = jnp.float32
bf16 = jnp.bfloat16


def round_up(value, step):
    return (value + step - 1) // step * step


def call(body, out_shape, scratch=(), smem=0, after=()):
    waits = len(after)

    def run(*operands):
        specs = [pl.BlockSpec(memory_space=pltpu.SMEM)] * smem
        specs += [pl.BlockSpec(memory_space=pltpu.VMEM)] * (len(operands) - smem)
        specs = [pl.BlockSpec(memory_space=pl.ANY)] * waits + specs
        return pl.pallas_call(
            lambda *refs: body(*refs[waits:]),
            out_shape=out_shape,
            in_specs=specs,
            out_specs=jax.tree.map(lambda _: pl.BlockSpec(memory_space=pltpu.VMEM), out_shape),
            scratch_shapes=list(scratch),
            compiler_params=pltpu.CompilerParams(vmem_limit_bytes=VMEM_BYTES),
        )(*after, *operands)

    return run


def struct(shape, dtype):
    return jax.ShapeDtypeStruct(shape, dtype)


def cut(position):
    return slice(position * LANES, (position + 1) * LANES)


def sides(row):
    lane = lax.broadcasted_iota(jnp.int32, row.shape, 1)
    before = jnp.where(lane == 0, 0.0, pltpu.roll(row, 1, axis=1))
    after = jnp.where(lane == LANES - 1, 0.0, pltpu.roll(row, LANES - 1, axis=1))
    return before, after


def column_sums(parts):
    return jnp.concatenate([jnp.sum(part.T, axis=0, keepdims=True) for part in parts], axis=0)


def for_all(ref, values):
    ref[...] = jnp.broadcast_to(values[None], ref.shape)


def to_columns(rows):
    channels = rows[0].shape[1]
    rest = jnp.zeros((LANES - len(rows), channels), f32)
    return jnp.concatenate(list(rows) + [rest], axis=0).T


def matmul(left, right):
    return lax.dot_general(left, right, (((1,), (0,)), ((), ())), preferred_element_type=f32)


def matmul_nt(left, right):
    return lax.dot_general(left, right, (((1,), (1,)), ((), ())), preferred_element_type=f32)


def sigmoid(values):
    return 1.0 / (1.0 + jnp.exp(-values))


def moments(received, pixel_count):
    total = jnp.sum(received, axis=0)
    mean = total[0:1] / pixel_count
    variance = total[1:2] / pixel_count - mean * mean
    return mean, lax.rsqrt(variance + norm_eps)


def one_hot(low, cells):
    count = low.shape[1]
    tile = 16
    given = jnp.broadcast_to(low.astype(f32), (tile, count)).astype(bf16)
    row = lax.broadcasted_iota(jnp.int32, (tile, count), 0).astype(f32).astype(bf16)
    one, zero = jnp.ones((), bf16), jnp.zeros((), bf16)
    return jnp.concatenate(
        [
            jnp.where(given - jnp.asarray(start, bf16) == row, one, zero)
            for start in range(0, cells, tile)
        ],
        axis=0,
    )


def pool_body(block, index_ref, feat_ref, lidar_ref, cot_ref, out_ref):
    grids, own, cells = lidar_ref.shape
    chans, points = feat_ref.shape
    out_ref[:, :own] = lidar_ref[...]
    out_ref[:, own : 2 * own] = cot_ref[...]
    rows = round_up(chans, 8)
    total = None
    for start in range(0, points, block):
        at = slice(start, start + block)
        index = index_ref[:, at]
        high, low = index // cells, index % cells
        feat = feat_ref[:, at].astype(f32)
        feat = jnp.concatenate([feat, jnp.zeros((rows - chans, block), f32)], axis=0)
        spread = jnp.concatenate([jnp.where(high == grid, feat, 0.0) for grid in range(grids)], axis=0)
        term = matmul_nt(spread.astype(bf16), one_hot(low, cells))
        total = term if total is None else total + term
    out_ref[:, 2 * own :] = total.reshape(grids, rows, cells)[:, :chans].astype(bf16)


def home_body(
    block, index_ref, home_ref, lidar_far, mixed_far, cam_far, token_ref,
    lidar_ref, mixed_ref, cam_ref, sems,
):
    grids, own, _, _ = lidar_ref.shape
    cells = home_ref.shape[2]
    chans, points = cam_ref.shape
    token_ref[...] = jnp.zeros(token_ref.shape, f32)
    copies = []
    for i, (near, far) in enumerate(((lidar_ref, lidar_far), (mixed_ref, mixed_far))):
        near[...] = home_ref[:, i * own : (i + 1) * own, :].astype(f32).reshape(near.shape)
        copies.append(pltpu.make_async_copy(near, far, sems.at[i]))
        copies[-1].start()
    rows = round_up(chans, 8)
    grad = home_ref[:, 2 * own : 2 * own + chans, :].astype(f32)
    grad = jnp.concatenate([grad, jnp.zeros((grids, rows - chans, cells), f32)], axis=1)
    grad = grad.reshape(grids * rows, cells).astype(bf16)
    for start in range(0, points, block):
        at = slice(start, start + block)
        index = index_ref[:, at]
        high, low = index // cells, index % cells
        picked = matmul(grad, one_hot(low, cells))
        total = jnp.zeros((rows, block), f32)
        for grid in range(grids):
            total = jnp.where(high == grid, picked[grid * rows : (grid + 1) * rows], total)
        cam_ref[:, at] = total[:chans]
    copies.append(pltpu.make_async_copy(cam_ref, cam_far, sems.at[2]))
    copies[-1].start()
    for copy in copies:
        copy.wait()


def pack_body(
    lid, cam, mid, one_width, norm_ref, lidar_far, cam_far, mid_far, out_ref,
    near_ref, lidar_ref, cam_ref, mid_ref, norm_sem, sems,
):
    rows = lidar_ref.shape[2]
    norm_copy = pltpu.make_async_copy(norm_ref, near_ref, norm_sem)
    norm_copy.start()
    pairs = ((lidar_far, lidar_ref), (cam_far, cam_ref), (mid_far, mid_ref))
    copies = [
        [pltpu.make_async_copy(far.at[a], near.at[a], sems.at[i, a]) for i, (far, near) in enumerate(pairs)]
        for a in range(3)
    ]
    for group in copies:
        for copy in group:
            copy.start()
    for a in range(3):
        for copy in copies[a]:
            copy.wait()
        base = a * one_width
        for b in range(3):
            out_ref[:, base + b * lid : base + (b + 1) * lid] = lidar_ref[a, b].astype(bf16)
        used = 3 * lid + 3 * cam
        rest = [cam_ref[a, b] for b in range(3)]
        if one_width > used:
            rest.append(jnp.zeros((rows, one_width - used), f32))
        out_ref[:, base + 3 * lid : base + one_width] = jnp.concatenate(rest, axis=1).astype(bf16)
        for b in range(3):
            start = 3 * one_width + (3 * a + b) * mid
            out_ref[:, start : start + mid] = mid_ref[a, b].astype(bf16)
    norm_copy.wait()
    norm = near_ref[...]
    norm = jnp.concatenate([norm, jnp.zeros((LANES - norm.shape[0], rows), f32)], axis=0)
    norm = jnp.concatenate([norm, jnp.zeros((LANES, LANES - rows), f32)], axis=1).T[:rows, :4]
    high = norm.astype(bf16)
    left = norm - high.astype(f32)
    middle = left.astype(bf16)
    low = (left - middle.astype(f32)).astype(bf16)
    tail = jnp.concatenate(
        [high.astype(f32), middle.astype(f32), low.astype(f32), jnp.zeros((rows, LANES - 12), f32)],
        axis=1,
    )
    out_ref[:, 3 * one_width + 9 * mid :] = tail.astype(bf16)


def place_rows(own, masks, chan, parts, all_ref):
    place = 0
    for part in parts:
        for j in range(part.shape[0]):
            row = pl.multiple_of((chan ^ masks[place]) * own, own)
            all_ref[pl.ds(row, own), :] = part[j]
            place += 1


def unpack_body(own, one_width, two_width, masks, place_ref, *refs):
    parts, (one_ref, two_ref, norm_ref, all_ref) = refs[:-4], refs[-4:]
    place_rows(own, masks, place_ref[0], parts, all_ref)
    one_ref[...] = all_ref[:, : 3 * one_width]
    two_ref[...] = all_ref[:, 3 * one_width : 3 * (one_width + two_width)]
    tail = all_ref[:, 3 * (one_width + two_width) :].astype(f32)
    norm = tail[:, 0:4] + tail[:, 4:8] + tail[:, 8:12]
    norm_ref[...] = jnp.concatenate([norm, jnp.zeros((norm.shape[0], LANES - 4), f32)], axis=1)


def turn_body(lid, cam, one_width, outs, one_ref, two_t_ref, one_t_ref, two_ref):
    for t in range(9):
        at = slice(t * outs, (t + 1) * outs)
        two_ref[:, at] = two_t_ref[:, at].T
    for a in range(3):
        for b in range(3):
            to = slice((3 * a + b) * outs, (3 * a + b + 1) * outs)
            start = a * one_width + b * lid
            one_t_ref[0:lid, to] = one_ref[:, start : start + lid].T
        start = a * one_width + 3 * lid
        turned = one_ref[:, start : start + one_width - 3 * lid].T
        for b in range(3):
            to = slice((3 * a + b) * outs, (3 * a + b + 1) * outs)
            one_t_ref[lid : lid + cam, to] = turned[b * cam : (b + 1) * cam]


def edge_rows(edge_ref, place_ref, groups, first, last):
    if groups == 2:
        edge_ref[0] = jnp.where(place_ref[1] == 0, last, first)
    else:
        edge_ref[0] = last
        edge_ref[1] = first


def fill_stack(stack_ref, base, order, p, row):
    count = row.shape[0]
    for b, shifted in zip(order, (*sides(row), row), strict=True):
        start = base + b * count
        stack_ref[start : start + count, cut(p)] = shifted.astype(bf16)


FORWARD = (0, 2, 1)
BACKWARD = (2, 0, 1)


def first_body(cfg, got_ref, kernel_ref, stack_ref, cot_ref, part_ref):
    nc, spg, rows, lid, cam, lid_own, cam_own, one_width = cfg
    per_strip = rows // spg

    def take(q, first, count):
        s, r = q // per_strip, q % per_strip
        pieces = [got_ref[s * nc + c, first : first + count, cut(r)] for c in range(nc)]
        return jnp.concatenate([piece.astype(f32) for piece in pieces], axis=0)

    used = 3 * (lid + cam)
    stack_ref[:, cut(0)] = jnp.zeros((one_width, LANES), bf16)
    stack_ref[:, cut(rows + 1)] = jnp.zeros((one_width, LANES), bf16)
    if one_width > used:
        stack_ref[used:, :] = jnp.zeros((one_width - used, (rows + 2) * LANES), bf16)
    for q in range(rows):
        fill_stack(stack_ref, 0, FORWARD, q + 1, take(q, 0, lid_own))
        fill_stack(stack_ref, 3 * lid, FORWARD, q + 1, take(q, 2 * lid_own, cam_own))
        cot_ref[:, cut(q)] = take(q, lid_own, lid_own).astype(bf16)
    total = None
    for a in range(3):
        term = matmul(
            kernel_ref[:, a * one_width : (a + 1) * one_width],
            stack_ref[:, a * LANES : (a + rows) * LANES],
        )
        total = term if total is None else total + term
    part_ref[...] = total


def first_halo_body(
    cfg, place_ref, part_ref, above_ref, below_ref, kernel_ref,
    halo_ref, cot_ref, out_ref, sums_ref, edge_ref,
):
    nc, rows, lid, cam, lid_own, cam_own, one_width, groups = cfg
    has_above = place_ref[1] > 0
    has_below = place_ref[1] < groups - 1
    used = 3 * (lid + cam)
    if one_width > used:
        halo_ref[used:, :] = jnp.zeros((one_width - used, 2 * LANES), bf16)
    for side, (ref, given) in enumerate(((above_ref, has_above), (below_ref, has_below))):
        row = jnp.concatenate([ref[c, :lid_own].astype(f32) for c in range(nc)], axis=0)
        fill_stack(halo_ref, 0, FORWARD, side, jnp.where(given, row, 0.0))
        row = jnp.concatenate([ref[c, 2 * lid_own :].astype(f32) for c in range(nc)], axis=0)
        fill_stack(halo_ref, 3 * lid, FORWARD, side, jnp.where(given, row, 0.0))
        cot_ref[:, cut(side)] = jnp.concatenate([ref[c, lid_own : 2 * lid_own] for c in range(nc)], axis=0)
    lines = [part_ref[:, cut(q)] for q in range(rows)]
    lines[0] = lines[0] + matmul(kernel_ref[:, :one_width], halo_ref[:, cut(0)])
    lines[-1] = lines[-1] + matmul(kernel_ref[:, 2 * one_width :], halo_ref[:, cut(1)])
    finish_sums(lines, out_ref, sums_ref, edge_ref, place_ref, groups)


def finish_sums(lines, out_ref, sums_ref, edge_ref, place_ref, groups):
    sums = squares = None
    for q, row in enumerate(lines):
        out_ref[:, cut(q)] = row
        sums = row if sums is None else sums + row
        squares = row * row if squares is None else squares + row * row
    for_all(sums_ref, column_sums([sums, squares]))
    edge_rows(edge_ref, place_ref, groups, lines[0], lines[-1])


def second_body(
    cfg, place_ref, raw_ref, above_ref, below_ref, stats_ref, norm_ref, kernel_ref,
    out_ref, sums_ref, edge_ref, hidden_ref, means_ref, stack_ref,
):
    rows, chans, groups, pixel_count = cfg
    mean, inv = moments(stats_ref[...], pixel_count)
    columns = to_columns([mean, inv])
    means_ref[...] = columns
    mean, inv = columns[:, 0:1], columns[:, 1:2]
    gain, shift = norm_ref[:, 0:1], norm_ref[:, 1:2]
    for p in range(rows + 2):
        if p == 0:
            raw = above_ref[...]
        elif p == rows + 1:
            raw = below_ref[...]
        else:
            raw = raw_ref[:, cut(p - 1)]
        act = gain * ((raw - mean) * inv) + shift
        hidden = act * sigmoid(act)
        if p == 0:
            hidden = jnp.where(place_ref[1] > 0, hidden, 0.0)
        elif p == rows + 1:
            hidden = jnp.where(place_ref[1] < groups - 1, hidden, 0.0)
        else:
            hidden_ref[:, cut(p - 1)] = hidden
        fill_stack(stack_ref, 0, FORWARD, p, hidden)
    total = None
    for a in range(3):
        term = matmul(
            kernel_ref[:, a * 3 * chans : (a + 1) * 3 * chans],
            stack_ref[:, a * LANES : (a + rows) * LANES],
        )
        total = term if total is None else total + term
    lines = [total[:, cut(q)] for q in range(rows)]
    finish_sums(lines, out_ref, sums_ref, edge_ref, place_ref, groups)


def slope_body(
    cfg, place_ref, raw_ref, above_ref, below_ref, stats_ref, norm_ref, cot_ref, cot_halo_ref, hidden_ref,
    slope_ref, sums_ref, means_ref, mixed_ref,
):
    rows, own, spg, nc, pixel_count = cfg
    per_strip = rows // spg
    mean, inv = moments(stats_ref[...], pixel_count)
    columns = to_columns([mean, inv])
    means_ref[...] = columns
    mean, inv = columns[:, 0:1], columns[:, 1:2]
    gain, shift = norm_ref[:, 2:3], norm_ref[:, 3:4]
    shift_sum = gain_sum = None
    for p in range(rows + 2):
        if p == 0:
            raw, cot = above_ref[...], cot_halo_ref[:, cut(0)]
        elif p == rows + 1:
            raw, cot = below_ref[...], cot_halo_ref[:, cut(1)]
        else:
            raw, cot = raw_ref[:, cut(p - 1)], cot_ref[:, cut(p - 1)]
        centred = (raw - mean) * inv
        act = gain * centred + shift
        gate = sigmoid(act)
        slope = cot.astype(f32) * (gate * (1.0 + act * (1.0 - gate)))
        slope_ref[:, cut(p)] = slope
        if 0 < p <= rows:
            shift_sum = slope if shift_sum is None else shift_sum + slope
            term = slope * centred
            gain_sum = term if gain_sum is None else gain_sum + term
            mixed = (hidden_ref[:, cut(p - 1)] + act * gate).astype(bf16)
            s, r = (p - 1) // per_strip, (p - 1) % per_strip
            for c in range(nc):
                mixed_ref[s * nc + c, :, cut(r)] = mixed[c * own : (c + 1) * own]
    for_all(sums_ref, column_sums([shift_sum, gain_sum]))


def mid_back_body(
    cfg, place_ref, slope_ref, raw_ref, above_ref, below_ref, means_two_ref, stats_ref, norm_ref,
    kernel_ref, raw_one_ref, means_one_ref, cot_ref,
    out_ref, sums_ref, edge_ref, stack_ref, grads_ref,
):
    rows, chans, groups, pixel_count = cfg
    total = jnp.sum(stats_ref[...], axis=0)
    grads_ref[...] = total
    columns = to_columns([total[0:1] / pixel_count, total[1:2] / pixel_count])
    shift_mean, gain_mean = columns[:, 0:1], columns[:, 1:2]
    mean, inv = means_two_ref[:, 0:1], means_two_ref[:, 1:2]
    scale = norm_ref[:, 2:3] * inv
    for p in range(rows + 2):
        if p == 0:
            raw = above_ref[...]
        elif p == rows + 1:
            raw = below_ref[...]
        else:
            raw = raw_ref[:, cut(p - 1)]
        centred = (raw - mean) * inv
        grad = scale * (slope_ref[:, cut(p)] - shift_mean - centred * gain_mean)
        if p == 0:
            grad = jnp.where(place_ref[1] > 0, grad, 0.0)
        elif p == rows + 1:
            grad = jnp.where(place_ref[1] < groups - 1, grad, 0.0)
        fill_stack(stack_ref, 0, BACKWARD, p, grad)
    back = None
    for a in range(3):
        term = matmul(
            kernel_ref[:, a * 3 * chans : (a + 1) * 3 * chans],
            stack_ref[:, (2 - a) * LANES : (2 - a + rows) * LANES],
        )
        back = term if back is None else back + term
    mean, inv = means_one_ref[:, 0:1], means_one_ref[:, 1:2]
    gain, shift = norm_ref[:, 0:1], norm_ref[:, 1:2]
    shift_sum = gain_sum = None
    slopes = []
    for q in range(rows):
        centred = (raw_one_ref[:, cut(q)] - mean) * inv
        act = gain * centred + shift
        gate = sigmoid(act)
        grad = back[:, cut(q)] + cot_ref[:, cut(q)].astype(f32)
        slope = grad * (gate * (1.0 + act * (1.0 - gate)))
        out_ref[:, cut(q)] = slope
        if q in (0, rows - 1):
            slopes.append(slope)
        shift_sum = slope if shift_sum is None else shift_sum + slope
        term = slope * centred
        gain_sum = term if gain_sum is None else gain_sum + term
    for_all(sums_ref, column_sums([shift_sum, gain_sum]))
    edge_rows(edge_ref, place_ref, groups, slopes[0], slopes[-1])


def halves(place_ref, own, nc, rows_at):
    low = place_ref[0] & 1
    found = []
    for side in (low, 1 - low):
        for pair in range(nc // 2):
            found.append(rows_at(pl.multiple_of((2 * pair + side) * own, own)))
    return jnp.concatenate(found, axis=0)


def first_back_body(
    cfg, place_ref, slope_ref, slope_above_ref, slope_below_ref, raw_ref, above_ref, below_ref,
    means_ref, stats_ref, norm_ref, grads_two_ref, own_ref, halo_ref, hidden_ref, stack_two_ref,
    keep_ref, send_ref, stack_ref, grads_ref, squares_ref, cells_ref,
):
    rows, chans, own, nc, one_width, groups, pixel_count = cfg
    wide = (rows + 2) * LANES
    total = jnp.sum(stats_ref[...], axis=0)
    grads = jnp.concatenate(
        [total[1:2], total[0:1], grads_two_ref[1:2], grads_two_ref[0:1]], axis=0
    )
    grads_ref[...] = grads
    squares_ref[...] = jnp.sum(grads * grads).reshape(1, 1)
    columns = to_columns([total[0:1] / pixel_count, total[1:2] / pixel_count])
    shift_mean, gain_mean = columns[:, 0:1], columns[:, 1:2]
    mean, inv = means_ref[:, 0:1], means_ref[:, 1:2]
    scale = norm_ref[:, 0:1] * inv
    for p in range(rows + 2):
        if p == 0:
            raw, slope = above_ref[...], slope_above_ref[...]
        elif p == rows + 1:
            raw, slope = below_ref[...], slope_below_ref[...]
        else:
            raw, slope = raw_ref[:, cut(p - 1)], slope_ref[:, cut(p - 1)]
        grad = scale * (slope - shift_mean - (raw - mean) * inv * gain_mean)
        if p == 0:
            grad = jnp.where(place_ref[1] > 0, grad, 0.0)
        elif p == rows + 1:
            grad = jnp.where(place_ref[1] < groups - 1, grad, 0.0)
        fill_stack(stack_ref, 0, BACKWARD, p, grad)
    cells_ref[:, :LANES] = halo_ref[:, :LANES]
    cells_ref[:, LANES : wide - LANES] = own_ref[:, LANES : wide - LANES]
    cells_ref[:, wide - LANES :] = halo_ref[:, LANES:]
    half = chans // 2
    ordered = halves(
        place_ref, own, nc,
        lambda start: stack_ref[pl.ds(chans + start, own), LANES : (rows + 1) * LANES],
    )
    hidden = halves(place_ref, own, nc, lambda start: hidden_ref[pl.ds(start, own), :]).astype(bf16)
    for a in range(3):
        grad = matmul_nt(ordered, cells_ref[:, a * LANES : (a + rows) * LANES]).astype(bf16)
        to = slice(a * one_width, (a + 1) * one_width)
        keep_ref[:, to] = grad[:half]
        send_ref[:, to] = grad[half:]
        grad = matmul_nt(hidden, stack_two_ref[:, (2 - a) * LANES : (2 - a + rows) * LANES]).astype(bf16)
        start = 3 * one_width + a * 3 * chans
        keep_ref[:, start : start + 3 * chans] = grad[:half]
        send_ref[:, start : start + 3 * chans] = grad[half:]


def inputs_back_body(cfg, stack_ref, kernel_ref, mixed_ref, back_ref):
    rows, chans, lid, lid_own, cam_own, spg, nc = cfg
    per_strip = rows // spg
    back = None
    for a in range(3):
        term = matmul(
            kernel_ref[:, a * 3 * chans : (a + 1) * 3 * chans],
            stack_ref[:, (2 - a) * LANES : (2 - a + rows) * LANES],
        )
        back = term if back is None else back + term
    for s in range(spg):
        cells = slice(s * per_strip * LANES, (s + 1) * per_strip * LANES)
        for c in range(nc):
            block = s * nc + c
            back_ref[block, 0:lid_own, :] = back[c * lid_own : (c + 1) * lid_own, cells].astype(bf16)
            back_ref[block, lid_own : 2 * lid_own, :] = mixed_ref[block]
            start = lid + c * cam_own
            back_ref[block, 2 * lid_own : 2 * lid_own + cam_own, :] = back[
                start : start + cam_own, cells
            ].astype(bf16)


def adam(weight, gradient, first, second, rate):
    first = beta_one * first + (1.0 - beta_one) * gradient
    second = beta_two * second + (1.0 - beta_two) * gradient * gradient
    fix_one = 1.0 - beta_one**STEP
    fix_two = 1.0 - beta_two**STEP
    stepped = first / fix_one / (jnp.sqrt(second / fix_two) + adam_eps)
    return weight - rate * (stepped + weight_decay * weight), first, second


def add_body(mine_ref, other_ref, out_ref):
    out_ref[...] = (mine_ref[...].astype(f32) + other_ref[...].astype(f32)).astype(bf16)


def sum_body(pieces_ref, out_ref):
    out_ref[...] = jnp.sum(pieces_ref[...].astype(f32), axis=0).astype(bf16)


def merge_body(copies, mine_ref, other_ref, out_ref):
    width = mine_ref.shape[1]
    piece = (mine_ref[...].astype(f32) + other_ref[...].astype(f32)).astype(bf16)
    values = piece.astype(f32)
    squares = jnp.sum(values * values).reshape(1, 1)
    high = squares.astype(bf16).astype(f32)
    middle = (squares - high).astype(bf16).astype(f32)
    low = squares - high - middle
    shape = (piece.shape[0], LANES)
    row = lax.broadcasted_iota(jnp.int32, shape, 0)
    lane = lax.broadcasted_iota(jnp.int32, shape, 1)
    terms = jnp.where(lane == 0, high, jnp.where(lane == 1, middle, jnp.where(lane == 2, low, 0.0)))
    terms = jnp.where(row == 0, terms, 0.0).astype(bf16)
    for copy in range(copies):
        out_ref[copy, :, :width] = piece
        out_ref[copy, :, width:] = terms


def tail_body(width, pieces_ref, out_ref):
    out_ref[...] = jnp.broadcast_to(jnp.sum(pieces_ref[:, :, width:].astype(f32)), out_ref.shape)


def adam_body(lid, cam, mid, chans, smalls, *refs):
    square_refs, grads_ref, refs = refs[:chans], refs[chans], refs[chans + 1 :]
    small_fars, fars, refs = refs[:smalls], refs[smalls : smalls + 9], refs[smalls + 9 :]
    small_outs, far_outs, refs = refs[:4], refs[4:13], refs[13:]
    small_nears, nears, refs = refs[:smalls], refs[smalls : smalls + 9], refs[smalls + 9 :]
    small_ins, ins, outs, norm_ref = refs
    one_width = round_up(3 * lid + 3 * cam, 256)
    first = [
        pltpu.make_async_copy(far, near, small_ins.at[i])
        for i, (far, near) in enumerate(zip(small_fars, small_nears, strict=True))
    ]
    reads = [
        [pltpu.make_async_copy(fars[i].at[a], nears[i].at[a], ins.at[i, a]) for i in range(9)]
        for a in range(3)
    ]
    for group in (first, *reads):
        for copy in group:
            copy.start()
    for copy in first:
        copy.wait()
    squares = [ref[0:1, 0:1] for ref in square_refs]
    norm_squares_ref, norm_grad_ref, *norm_state = small_nears
    while len(squares) > 1:
        squares = [squares[i] + squares[i + 1] for i in range(0, len(squares), 2)]
    norm = jnp.sqrt(squares[0] + norm_squares_ref[...])
    norm_ref[...] = norm
    factor = jnp.minimum(1.0, clip_norm / (norm + 1e-06))

    def step(state, at, gradient, rate):
        weight, first, second = (ref[at] for ref in state)
        for ref, value in zip(state, adam(weight, factor * gradient, first, second, rate), strict=True):
            ref[at] = value

    step(norm_state, ..., norm_grad_ref[...], norm_rate)
    writes = [
        [
            pltpu.make_async_copy(near, far, small_ins.at[i])
            for i, (near, far) in enumerate(zip((*norm_state, norm_ref), small_outs, strict=True))
        ]
    ]
    for copy in writes[0]:
        copy.start()
    for a in range(3):
        for copy in reads[a]:
            copy.wait()
        base = a * one_width
        tail = grads_ref[:, base + 3 * lid : base + one_width].astype(f32)
        for b in range(3):
            start = 3 * one_width + (3 * a + b) * mid
            given = (
                tail[:, b * cam : (b + 1) * cam],
                grads_ref[:, base + b * lid : base + (b + 1) * lid].astype(f32),
                grads_ref[:, start : start + mid].astype(f32),
            )
            for i, gradient in enumerate(given):
                step(nears[3 * i : 3 * i + 3], (a, b), gradient, learn_rate)
        writes.append(
            [pltpu.make_async_copy(nears[i].at[a], far_outs[i].at[a], outs.at[i, a]) for i in range(9)]
        )
        for copy in writes[-1]:
            copy.start()
    for group in writes:
        for copy in group:
            copy.wait()


def shards(
    cam_feats,
    cell_index,
    lidar_bev,
    w_cam,
    w_lidar,
    w_mid,
    bn_params,
    cotangent,
    m_cam,
    v_cam,
    m_lidar,
    v_lidar,
    m_mid,
    v_mid,
    m_bn,
    v_bn,
):
    grids, lid_own, strip_rows, width = lidar_bev.shape
    cam_own, points = cam_feats.shape
    own = bn_params.shape[1]
    nc = lax.axis_size("chan")
    ns = lax.axis_size("strip")
    lid, cam, chans = nc * lid_own, nc * cam_own, nc * own
    spg = grids // nc
    groups = ns // spg
    members = spg * nc
    rows = spg * strip_rows
    cells = strip_rows * width
    pixel_count = float(grids * cells * ns)
    devices = ns * nc
    one_width = round_up(3 * lid + 3 * cam, 256)
    two_width = 3 * chans
    total_width = 3 * one_width + 3 * two_width
    chan = lax.axis_index("chan")
    group = lax.axis_index("strip") // spg
    place = jnp.stack([chan, group]).astype(jnp.int32)

    tile_groups = [[g * members + r for r in range(members)] for g in range(groups)]
    half_groups = [
        [(g * spg + s) * nc + 2 * pair + low for pair in range(nc // 2) for s in range(spg)]
        for g in range(groups)
        for low in range(2)
    ]
    strip_groups = [
        [(g * spg + s) * nc + c for s in range(spg)] for g in range(groups) for c in range(nc)
    ]

    def exchange(blocks, parts):
        return lax.all_to_all(blocks, AXES, 0, 0, axis_index_groups=parts, tiled=True)

    def everywhere(copies):
        return lax.all_to_all(copies, AXES, 0, 0, tiled=True)

    def chan_swap(values, bit):
        return lax.ppermute(values, "chan", [(c, c ^ bit) for c in range(nc)])

    def neighbours(edges):
        if groups == 1:
            return edges[0], edges[0]
        if groups == 2:
            pairs = [(i, (i + members) % devices) for i in range(devices)]
            other = lax.ppermute(edges[0], AXES, pairs)
            return other, other
        down = [(i, i + members) for i in range(devices - members)]
        up = [(i + members, i) for i in range(devices - members)]
        return lax.ppermute(edges[0], AXES, down), lax.ppermute(edges[1], AXES, up)

    edge_count = 2 if groups > 2 else 1

    area = rows * LANES
    wide = (rows + 2) * LANES
    def from_all_channels(packed):
        parts, masks = [packed[None]], [0]
        bit = nc // 2
        while bit:
            stacked = parts[0] if len(parts) == 1 else jnp.concatenate(parts, axis=0)
            parts.append(chan_swap(stacked, bit))
            masks += [mask ^ bit for mask in masks]
            bit //= 2
        return parts, masks

    def edge_cells(got):
        last = got[members - nc :, :, cells - width :]
        first = got[:nc, :, :width]
        if groups == 2:
            return jnp.where(group == 0, last, first)[None]
        return jnp.stack([last, first])

    sums_struct = struct((devices, 2, chans), f32)
    packed_width = total_width + LANES

    index_row = cell_index.reshape(1, points)
    block = math.gcd(points, 1024)
    joined = call(
        functools.partial(pool_body, block), struct((grids, lid_own + own + cam_own, cells), bf16)
    )(
        index_row, cam_feats, lidar_bev.reshape(grids, lid_own, cells),
        cotangent.reshape(grids, own, cells),
    )
    got = exchange(joined, tile_groups)
    above, below = neighbours(edge_cells(got))

    turn = (0, 1, 3, 2)
    far = pl.BlockSpec(memory_space=pltpu.HBM)
    near = pl.BlockSpec(memory_space=pltpu.VMEM)
    weights = [w_lidar.transpose(turn), w_cam.transpose(turn), w_mid]
    packed = pl.pallas_call(
        functools.partial(pack_body, lid, cam, chans, one_width),
        in_specs=[far] * 4,
        out_specs=near,
        out_shape=struct((own, packed_width), bf16),
        scratch_shapes=[
            *(pltpu.VMEM(weight.shape, f32) for weight in (bn_params, *weights)),
            pltpu.SemaphoreType.DMA,
            pltpu.SemaphoreType.DMA((3, 3)),
        ],
        compiler_params=pltpu.CompilerParams(vmem_limit_bytes=VMEM_MOST),
    )(bn_params, *weights)
    parts, masks = from_all_channels(packed)
    kernel_one, kernel_two_t, norm = call(
        functools.partial(unpack_body, own, one_width, two_width, masks),
        [
            struct((chans, 3 * one_width), bf16),
            struct((chans, 3 * two_width), bf16),
            struct((chans, LANES), f32),
        ],
        scratch=[pltpu.VMEM((chans, packed_width), bf16)],
        smem=1,
    )(place, *parts)

    kernel_one_t, kernel_two = call(
        functools.partial(turn_body, lid, cam, one_width, chans),
        [struct((lid + cam, 3 * two_width), bf16), struct((chans, 3 * two_width), bf16)],
    )(kernel_one, kernel_two_t)
    own_stack, cot, part_one = call(
        functools.partial(first_body, (nc, spg, rows, lid, cam, lid_own, cam_own, one_width)),
        [
            struct((one_width, wide), bf16),
            struct((chans, area), bf16),
            struct((chans, area), f32),
        ],
    )(got, kernel_one)
    halo_stack, cot_halo, raw_one, sums_one, edges_one = call(
        functools.partial(
            first_halo_body, (nc, rows, lid, cam, lid_own, cam_own, one_width, groups)
        ),
        [
            struct((one_width, 2 * LANES), bf16),
            struct((chans, 2 * LANES), bf16),
            struct((chans, area), f32),
            sums_struct,
            struct((edge_count, chans, LANES), f32),
        ],
        smem=1,
        after=(kernel_one_t, kernel_two),
    )(place, part_one, above, below, kernel_one)

    above_one, below_one = neighbours(edges_one)
    stats_one = everywhere(sums_one)
    raw_two, sums_two, edges_two, hidden, means_one = call(
        functools.partial(second_body, (rows, chans, groups, pixel_count)),
        [
            struct((chans, area), f32),
            sums_struct,
            struct((edge_count, chans, LANES), f32),
            struct((chans, area), f32),
            struct((chans, LANES), f32),
        ],
        scratch=[pltpu.VMEM((two_width, wide), bf16)],
        smem=1,
    )(place, raw_one, above_one, below_one, stats_one, norm, kernel_two)

    above_two, below_two = neighbours(edges_two)
    stats_two = everywhere(sums_two)
    slope_two, sums_three, means_two, mixed_blocks = call(
        functools.partial(slope_body, (rows, own, spg, nc, pixel_count)),
        [
            struct((chans, wide), f32),
            sums_struct,
            struct((chans, LANES), f32),
            struct((members, own, cells), bf16),
        ],
        smem=1,
    )(place, raw_two, above_two, below_two, stats_two, norm, cot, cot_halo, hidden)

    stats_three = everywhere(sums_three)
    slope_one, sums_four, edges_four, grad_stack, grads_two = call(
        functools.partial(mid_back_body, (rows, chans, groups, pixel_count)),
        [
            struct((chans, area), f32),
            sums_struct,
            struct((edge_count, chans, LANES), f32),
            struct((two_width, wide), bf16),
            struct((2, chans), f32),
        ],
        smem=1,
    )(
        place, slope_two, raw_two, above_two, below_two, means_two, stats_three, norm,
        kernel_two_t, raw_one, means_one, cot,
    )

    above_four, below_four = neighbours(edges_four)
    stats_four = everywhere(sums_four)
    keep, send, grad_stack_one, grad_bn_all, norm_squares = call(
        functools.partial(
            first_back_body, (rows, chans, own, nc, one_width, groups, pixel_count)
        ),
        [
            struct((chans // 2, total_width), bf16),
            struct((chans // 2, total_width), bf16),
            struct((two_width, wide), bf16),
            struct((4, chans), f32),
            struct((1, 1), f32),
        ],
        scratch=[pltpu.VMEM((one_width, wide), bf16)],
        smem=1,
    )(
        place, slope_one, above_four, below_four, raw_one, above_one, below_one, means_one,
        stats_four, norm, grads_two, own_stack, halo_stack, hidden, grad_stack,
    )
    back_blocks = call(
        functools.partial(inputs_back_body, (rows, chans, lid, lid_own, cam_own, spg, nc)),
        struct((members, lid_own + own + cam_own, cells), bf16),
    )(grad_stack_one, kernel_one_t, mixed_blocks)
    home = exchange(back_blocks, tile_groups)

    halved = call(add_body, struct(keep.shape, bf16), after=(back_blocks,))(keep, chan_swap(send, 1))
    piece_rows = own // spg
    pieces = exchange(halved.reshape(members // 2, piece_rows, total_width), half_groups)
    piece = call(sum_body, struct((piece_rows, total_width), bf16))(pieces)
    other = jnp.zeros_like(piece)
    shift = members
    while shift < devices:
        if shift > members:
            piece = (piece.astype(f32) + other.astype(f32)).astype(bf16)
        other = lax.ppermute(piece, AXES, [(i, i ^ shift) for i in range(devices)])
        shift *= 2
    merged = call(
        functools.partial(merge_body, spg), struct((spg, piece_rows, packed_width), bf16), after=(home,)
    )(piece, other)
    merged = exchange(merged, strip_groups)
    own_grads = merged.reshape(own, packed_width)
    images = [struct(lidar_bev.shape, f32), struct(cotangent.shape, f32), struct((cam_own, points), f32)]
    grad_lidar, mixed, grad_cam, token = pl.pallas_call(
        functools.partial(home_body, block),
        in_specs=[near] * 2,
        out_specs=[far] * 3 + [near],
        out_shape=[*images, struct((8, LANES), f32)],
        scratch_shapes=[
            *(pltpu.VMEM(image.shape, f32) for image in images),
            pltpu.SemaphoreType.DMA((3,)),
        ],
        compiler_params=pltpu.CompilerParams(vmem_limit_bytes=VMEM_BYTES),
    )(index_row, home)
    tall = lambda array: array.transpose(turn)
    state = [
        *(tall(array) for array in (w_cam, m_cam, v_cam)),
        *(tall(array) for array in (w_lidar, m_lidar, v_lidar)),
        w_mid, m_mid, v_mid,
    ]
    squares = call(
        functools.partial(tail_body, total_width),
        struct((8, LANES), f32),
        after=(token,),
    )(merged)
    squares = [squares] + [
        lax.ppermute(squares, "chan", [(c, c ^ mask) for c in range(nc)]) for mask in range(1, nc)
    ]
    grad_bn = lax.dynamic_slice(grad_bn_all, (0, chan * own), (4, own))
    norm_state = [bn_params, m_bn, v_bn]
    small = [norm_squares, grad_bn, *norm_state]
    results = [*norm_state, norm_squares, *state]
    updated = pl.pallas_call(
        functools.partial(adam_body, lid, cam, chans, nc, len(small)),
        in_specs=[near] * (nc + 1) + [far] * (len(small) + 9),
        out_specs=[far] * 13,
        out_shape=[struct(array.shape, f32) for array in results],
        scratch_shapes=[
            *(pltpu.VMEM(array.shape, f32) for array in small + state),
            pltpu.SemaphoreType.DMA((len(small),)),
            pltpu.SemaphoreType.DMA((9, 3)),
            pltpu.SemaphoreType.DMA((9, 3)),
            pltpu.VMEM((1, 1), f32),
        ],
        compiler_params=pltpu.CompilerParams(vmem_limit_bytes=VMEM_MOST),
    )(*squares, own_grads, *small, *state)
    turned = [tall(array) for array in updated[4:10]]
    return (mixed, grad_cam, grad_lidar, updated[3].reshape(()), *turned, *updated[10:], *updated[:3])


def solution(mesh):
    return jax.shard_map(
        shards,
        mesh=mesh,
        in_specs=(
            P("chan", "strip"),
            P("strip"),
            P(None, "chan", "strip", None),
            P(None, None, None, "chan"),
            P(None, None, None, "chan"),
            P(None, None, "chan", None),
            P(None, "chan"),
            P(None, "chan", "strip", None),
            P(None, None, None, "chan"),
            P(None, None, None, "chan"),
            P(None, None, None, "chan"),
            P(None, None, None, "chan"),
            P(None, None, "chan", None),
            P(None, None, "chan", None),
            P(None, "chan"),
            P(None, "chan"),
        ),
        out_specs=(
            P(None, "chan", "strip", None),
            P("chan", "strip"),
            P(None, "chan", "strip", None),
            P(),
            P(None, None, None, "chan"),
            P(None, None, None, "chan"),
            P(None, None, None, "chan"),
            P(None, None, None, "chan"),
            P(None, None, None, "chan"),
            P(None, None, None, "chan"),
            P(None, None, "chan", None),
            P(None, None, "chan", None),
            P(None, None, "chan", None),
            P(None, "chan"),
            P(None, "chan"),
            P(None, "chan"),
        ),
        check_vma=False,
    )
```

```python
import functools
import math

import jax
import jax.numpy as jnp
from jax import lax
from jax.experimental import pallas as pl
from jax.experimental.pallas import tpu as pltpu
from jax.sharding import PartitionSpec as P

STEP = 10


beta_one = 0.9
beta_two = 0.999
adam_eps = 1e-08
learn_rate = 0.02
norm_rate = 1.5
weight_decay = 0.01
norm_eps = 1e-05
clip_norm = 1.0

AXES = ("strip", "chan")
LANES = 128
VMEM_BYTES = 24 * 1024 * 1024
VMEM_MOST = 60 * 1024 * 1024

f32 = jnp.float32
bf16 = jnp.bfloat16


def round_up(value, step):
    return (value + step - 1) // step * step


def call(body, out_shape, scratch=(), smem=0, after=()):
    waits = len(after)

    def run(*operands):
        specs = [pl.BlockSpec(memory_space=pltpu.SMEM)] * smem
        specs += [pl.BlockSpec(memory_space=pltpu.VMEM)] * (len(operands) - smem)
        specs = [pl.BlockSpec(memory_space=pl.ANY)] * waits + specs
        return pl.pallas_call(
            lambda *refs: body(*refs[waits:]),
            out_shape=out_shape,
            in_specs=specs,
            out_specs=jax.tree.map(lambda _: pl.BlockSpec(memory_space=pltpu.VMEM), out_shape),
            scratch_shapes=list(scratch),
            compiler_params=pltpu.CompilerParams(vmem_limit_bytes=VMEM_BYTES),
        )(*after, *operands)

    return run


def struct(shape, dtype):
    return jax.ShapeDtypeStruct(shape, dtype)


def cut(position):
    return slice(position * LANES, (position + 1) * LANES)


def sides(row):
    lane = lax.broadcasted_iota(jnp.int32, row.shape, 1)
    before = jnp.where(lane == 0, 0.0, pltpu.roll(row, 1, axis=1))
    after = jnp.where(lane == LANES - 1, 0.0, pltpu.roll(row, LANES - 1, axis=1))
    return before, after


def column_sums(parts):
    return jnp.concatenate([jnp.sum(part.T, axis=0, keepdims=True) for part in parts], axis=0)


def for_all(ref, values):
    ref[...] = jnp.broadcast_to(values[None], ref.shape)


def to_columns(rows):
    channels = rows[0].shape[1]
    rest = jnp.zeros((LANES - len(rows), channels), f32)
    return jnp.concatenate(list(rows) + [rest], axis=0).T


def matmul(left, right):
    return lax.dot_general(left, right, (((1,), (0,)), ((), ())), preferred_element_type=f32)


def matmul_nt(left, right):
    return lax.dot_general(left, right, (((1,), (1,)), ((), ())), preferred_element_type=f32)


def sigmoid(values):
    return 1.0 / (1.0 + jnp.exp(-values))


def moments(received, pixel_count):
    total = jnp.sum(received, axis=0)
    mean = total[0:1] / pixel_count
    variance = total[1:2] / pixel_count - mean * mean
    return mean, lax.rsqrt(variance + norm_eps)


def one_hot(low, cells):
    count = low.shape[1]
    tile = 16
    given = jnp.broadcast_to(low.astype(f32), (tile, count)).astype(bf16)
    row = lax.broadcasted_iota(jnp.int32, (tile, count), 0).astype(f32).astype(bf16)
    one, zero = jnp.ones((), bf16), jnp.zeros((), bf16)
    return jnp.concatenate(
        [
            jnp.where(given - jnp.asarray(start, bf16) == row, one, zero)
            for start in range(0, cells, tile)
        ],
        axis=0,
    )


def split_body(place_ref, got_ref, keep_ref, send_ref):
    low = place_ref[0] & 1
    for pair in range(keep_ref.shape[0]):
        keep_ref[pair] = got_ref[2 * pair + low]
        send_ref[pair] = got_ref[2 * pair + 1 - low]


def pool_body(block, index_ref, feat_ref, lidar_ref, cot_ref, out_ref):
    grids, own, cells = lidar_ref.shape
    chans, points = feat_ref.shape
    out_ref[:, :own] = lidar_ref[...]
    out_ref[:, own : 2 * own] = cot_ref[...]
    rows = round_up(chans, 8)
    total = None
    for start in range(0, points, block):
        at = slice(start, start + block)
        index = index_ref[:, at]
        high, low = index // cells, index % cells
        feat = feat_ref[:, at].astype(f32)
        feat = jnp.concatenate([feat, jnp.zeros((rows - chans, block), f32)], axis=0)
        spread = jnp.concatenate([jnp.where(high == grid, feat, 0.0) for grid in range(grids)], axis=0)
        term = matmul_nt(spread.astype(bf16), one_hot(low, cells))
        total = term if total is None else total + term
    out_ref[:, 2 * own :] = total.reshape(grids, rows, cells)[:, :chans].astype(bf16)


def home_body(
    block, place_ref, index_ref, keep_ref, got_ref, lidar_far, mixed_far, cam_far, token_ref,
    lidar_ref, mixed_ref, cam_ref, sems,
):
    grids, own, _, _ = lidar_ref.shape
    cells = keep_ref.shape[2]
    chans, points = cam_ref.shape
    low = place_ref[0] & 1
    blocks = [(ref, pair, 2 * pair + parity) for ref, parity in ((keep_ref, low), (got_ref, 1 - low)) for pair in range(grids // 2)]
    token_ref[...] = jnp.zeros(token_ref.shape, f32)
    copies = []
    for i, (near, far) in enumerate(((lidar_ref, lidar_far), (mixed_ref, mixed_far))):
        for ref, pair, grid in blocks:
            near[grid] = ref[pair, i * own : (i + 1) * own, :].astype(f32).reshape(near.shape[1:])
        copies.append(pltpu.make_async_copy(near, far, sems.at[i]))
        copies[-1].start()
    rows = round_up(chans, 8)
    grad = jnp.concatenate([ref[:, 2 * own : 2 * own + chans, :] for ref in (keep_ref, got_ref)], axis=0)
    grad = jnp.concatenate([grad.astype(f32), jnp.zeros((grids, rows - chans, cells), f32)], axis=1)
    grad = grad.reshape(grids * rows, cells).astype(bf16)
    for start in range(0, points, block):
        at = slice(start, start + block)
        index = index_ref[:, at]
        high, low_part = index // cells, index % cells
        picked = matmul(grad, one_hot(low_part, cells))
        total = jnp.zeros((rows, block), f32)
        for i, (_, _, grid) in enumerate(blocks):
            total = jnp.where(high == grid, picked[i * rows : (i + 1) * rows], total)
        cam_ref[:, at] = total[:chans]
    copies.append(pltpu.make_async_copy(cam_ref, cam_far, sems.at[2]))
    copies[-1].start()
    for copy in copies:
        copy.wait()


def pack_body(
    lid, cam, mid, one_width, norm_ref, lidar_far, cam_far, mid_far, out_ref,
    near_ref, lidar_ref, cam_ref, mid_ref, norm_sem, sems,
):
    rows = lidar_ref.shape[2]
    norm_copy = pltpu.make_async_copy(norm_ref, near_ref, norm_sem)
    norm_copy.start()
    pairs = ((lidar_far, lidar_ref), (cam_far, cam_ref), (mid_far, mid_ref))
    copies = [
        [pltpu.make_async_copy(far.at[a], near.at[a], sems.at[i, a]) for i, (far, near) in enumerate(pairs)]
        for a in range(3)
    ]
    for group in copies:
        for copy in group:
            copy.start()
    for a in range(3):
        for copy in copies[a]:
            copy.wait()
        base = a * one_width
        for b in range(3):
            out_ref[:, base + b * lid : base + (b + 1) * lid] = lidar_ref[a, b].astype(bf16)
        used = 3 * lid + 3 * cam
        rest = [cam_ref[a, b] for b in range(3)]
        if one_width > used:
            rest.append(jnp.zeros((rows, one_width - used), f32))
        out_ref[:, base + 3 * lid : base + one_width] = jnp.concatenate(rest, axis=1).astype(bf16)
        for b in range(3):
            start = 3 * one_width + (3 * a + b) * mid
            out_ref[:, start : start + mid] = mid_ref[a, b].astype(bf16)
    norm_copy.wait()
    norm = near_ref[...]
    norm = jnp.concatenate([norm, jnp.zeros((LANES - norm.shape[0], rows), f32)], axis=0)
    norm = jnp.concatenate([norm, jnp.zeros((LANES, LANES - rows), f32)], axis=1).T[:rows, :4]
    high = norm.astype(bf16)
    left = norm - high.astype(f32)
    middle = left.astype(bf16)
    low = (left - middle.astype(f32)).astype(bf16)
    tail = jnp.concatenate(
        [high.astype(f32), middle.astype(f32), low.astype(f32), jnp.zeros((rows, LANES - 12), f32)],
        axis=1,
    )
    out_ref[:, 3 * one_width + 9 * mid :] = tail.astype(bf16)


def place_rows(own, masks, chan, parts, all_ref):
    place = 0
    for part in parts:
        for j in range(part.shape[0]):
            row = pl.multiple_of((chan ^ masks[place]) * own, own)
            all_ref[pl.ds(row, own), :] = part[j]
            place += 1


def unpack_body(own, one_width, two_width, masks, place_ref, *refs):
    parts, (one_ref, two_ref, norm_ref, all_ref) = refs[:-4], refs[-4:]
    place_rows(own, masks, place_ref[0], parts, all_ref)
    one_ref[...] = all_ref[:, : 3 * one_width]
    two_ref[...] = all_ref[:, 3 * one_width : 3 * (one_width + two_width)]
    tail = all_ref[:, 3 * (one_width + two_width) :].astype(f32)
    norm = tail[:, 0:4] + tail[:, 4:8] + tail[:, 8:12]
    norm_ref[...] = jnp.concatenate([norm, jnp.zeros((norm.shape[0], LANES - 4), f32)], axis=1)


def turn_body(lid, cam, one_width, outs, one_ref, two_t_ref, one_t_ref, two_ref):
    for t in range(9):
        at = slice(t * outs, (t + 1) * outs)
        two_ref[:, at] = two_t_ref[:, at].T
    for a in range(3):
        for b in range(3):
            to = slice((3 * a + b) * outs, (3 * a + b + 1) * outs)
            start = a * one_width + b * lid
            one_t_ref[0:lid, to] = one_ref[:, start : start + lid].T
        start = a * one_width + 3 * lid
        turned = one_ref[:, start : start + one_width - 3 * lid].T
        for b in range(3):
            to = slice((3 * a + b) * outs, (3 * a + b + 1) * outs)
            one_t_ref[lid : lid + cam, to] = turned[b * cam : (b + 1) * cam]


def edge_rows(edge_ref, place_ref, groups, first, last):
    if groups == 2:
        edge_ref[0] = jnp.where(place_ref[1] == 0, last, first)
    else:
        edge_ref[0] = last
        edge_ref[1] = first


def fill_stack(stack_ref, base, order, p, row):
    count = row.shape[0]
    for b, shifted in zip(order, (*sides(row), row), strict=True):
        start = base + b * count
        stack_ref[start : start + count, cut(p)] = shifted.astype(bf16)


FORWARD = (0, 2, 1)
BACKWARD = (2, 0, 1)


def first_body(cfg, got_ref, kernel_ref, stack_ref, cot_ref, part_ref):
    nc, spg, rows, lid, cam, lid_own, cam_own, one_width = cfg
    per_strip = rows // spg

    def take(q, first, count):
        s, r = q // per_strip, q % per_strip
        pieces = [got_ref[s * nc + c, first : first + count, cut(r)] for c in range(nc)]
        return jnp.concatenate([piece.astype(f32) for piece in pieces], axis=0)

    used = 3 * (lid + cam)
    stack_ref[:, cut(0)] = jnp.zeros((one_width, LANES), bf16)
    stack_ref[:, cut(rows + 1)] = jnp.zeros((one_width, LANES), bf16)
    if one_width > used:
        stack_ref[used:, :] = jnp.zeros((one_width - used, (rows + 2) * LANES), bf16)
    for q in range(rows):
        fill_stack(stack_ref, 0, FORWARD, q + 1, take(q, 0, lid_own))
        fill_stack(stack_ref, 3 * lid, FORWARD, q + 1, take(q, 2 * lid_own, cam_own))
        cot_ref[:, cut(q)] = take(q, lid_own, lid_own).astype(bf16)
    total = None
    for a in range(3):
        term = matmul(
            kernel_ref[:, a * one_width : (a + 1) * one_width],
            stack_ref[:, a * LANES : (a + rows) * LANES],
        )
        total = term if total is None else total + term
    part_ref[...] = total


def first_halo_body(
    cfg, place_ref, part_ref, above_ref, below_ref, kernel_ref,
    halo_ref, cot_ref, out_ref, sums_ref, edge_ref,
):
    nc, rows, lid, cam, lid_own, cam_own, one_width, groups = cfg
    has_above = place_ref[1] > 0
    has_below = place_ref[1] < groups - 1
    used = 3 * (lid + cam)
    if one_width > used:
        halo_ref[used:, :] = jnp.zeros((one_width - used, 2 * LANES), bf16)
    for side, (ref, given) in enumerate(((above_ref, has_above), (below_ref, has_below))):
        row = jnp.concatenate([ref[c, :lid_own].astype(f32) for c in range(nc)], axis=0)
        fill_stack(halo_ref, 0, FORWARD, side, jnp.where(given, row, 0.0))
        row = jnp.concatenate([ref[c, 2 * lid_own :].astype(f32) for c in range(nc)], axis=0)
        fill_stack(halo_ref, 3 * lid, FORWARD, side, jnp.where(given, row, 0.0))
        cot_ref[:, cut(side)] = jnp.concatenate([ref[c, lid_own : 2 * lid_own] for c in range(nc)], axis=0)
    lines = [part_ref[:, cut(q)] for q in range(rows)]
    lines[0] = lines[0] + matmul(kernel_ref[:, :one_width], halo_ref[:, cut(0)])
    lines[-1] = lines[-1] + matmul(kernel_ref[:, 2 * one_width :], halo_ref[:, cut(1)])
    finish_sums(lines, out_ref, sums_ref, edge_ref, place_ref, groups)


def finish_sums(lines, out_ref, sums_ref, edge_ref, place_ref, groups):
    sums = squares = None
    for q, row in enumerate(lines):
        out_ref[:, cut(q)] = row
        sums = row if sums is None else sums + row
        squares = row * row if squares is None else squares + row * row
    for_all(sums_ref, column_sums([sums, squares]))
    edge_rows(edge_ref, place_ref, groups, lines[0], lines[-1])


def second_body(
    cfg, place_ref, raw_ref, above_ref, below_ref, stats_ref, norm_ref, kernel_ref,
    out_ref, sums_ref, edge_ref, hidden_ref, means_ref, stack_ref,
):
    rows, chans, groups, pixel_count = cfg
    mean, inv = moments(stats_ref[...], pixel_count)
    columns = to_columns([mean, inv])
    means_ref[...] = columns
    mean, inv = columns[:, 0:1], columns[:, 1:2]
    gain, shift = norm_ref[:, 0:1], norm_ref[:, 1:2]
    for p in range(rows + 2):
        if p == 0:
            raw = above_ref[...]
        elif p == rows + 1:
            raw = below_ref[...]
        else:
            raw = raw_ref[:, cut(p - 1)]
        act = gain * ((raw - mean) * inv) + shift
        hidden = act * sigmoid(act)
        if p == 0:
            hidden = jnp.where(place_ref[1] > 0, hidden, 0.0)
        elif p == rows + 1:
            hidden = jnp.where(place_ref[1] < groups - 1, hidden, 0.0)
        else:
            hidden_ref[:, cut(p - 1)] = hidden
        fill_stack(stack_ref, 0, FORWARD, p, hidden)
    total = None
    for a in range(3):
        term = matmul(
            kernel_ref[:, a * 3 * chans : (a + 1) * 3 * chans],
            stack_ref[:, a * LANES : (a + rows) * LANES],
        )
        total = term if total is None else total + term
    lines = [total[:, cut(q)] for q in range(rows)]
    finish_sums(lines, out_ref, sums_ref, edge_ref, place_ref, groups)


def slope_body(
    cfg, place_ref, raw_ref, above_ref, below_ref, stats_ref, norm_ref, cot_ref, cot_halo_ref, hidden_ref,
    slope_ref, sums_ref, means_ref, mixed_ref,
):
    rows, own, spg, nc, pixel_count = cfg
    per_strip = rows // spg
    mean, inv = moments(stats_ref[...], pixel_count)
    columns = to_columns([mean, inv])
    means_ref[...] = columns
    mean, inv = columns[:, 0:1], columns[:, 1:2]
    gain, shift = norm_ref[:, 2:3], norm_ref[:, 3:4]
    shift_sum = gain_sum = None
    for p in range(rows + 2):
        if p == 0:
            raw, cot = above_ref[...], cot_halo_ref[:, cut(0)]
        elif p == rows + 1:
            raw, cot = below_ref[...], cot_halo_ref[:, cut(1)]
        else:
            raw, cot = raw_ref[:, cut(p - 1)], cot_ref[:, cut(p - 1)]
        centred = (raw - mean) * inv
        act = gain * centred + shift
        gate = sigmoid(act)
        slope = cot.astype(f32) * (gate * (1.0 + act * (1.0 - gate)))
        slope_ref[:, cut(p)] = slope
        if 0 < p <= rows:
            shift_sum = slope if shift_sum is None else shift_sum + slope
            term = slope * centred
            gain_sum = term if gain_sum is None else gain_sum + term
            mixed = (hidden_ref[:, cut(p - 1)] + act * gate).astype(bf16)
            s, r = (p - 1) // per_strip, (p - 1) % per_strip
            for c in range(nc):
                mixed_ref[s * nc + c, :, cut(r)] = mixed[c * own : (c + 1) * own]
    for_all(sums_ref, column_sums([shift_sum, gain_sum]))


def mid_back_body(
    cfg, place_ref, slope_ref, raw_ref, above_ref, below_ref, means_two_ref, stats_ref, norm_ref,
    kernel_ref, raw_one_ref, means_one_ref, cot_ref,
    out_ref, sums_ref, edge_ref, stack_ref, grads_ref,
):
    rows, chans, groups, pixel_count = cfg
    total = jnp.sum(stats_ref[...], axis=0)
    grads_ref[...] = total
    columns = to_columns([total[0:1] / pixel_count, total[1:2] / pixel_count])
    shift_mean, gain_mean = columns[:, 0:1], columns[:, 1:2]
    mean, inv = means_two_ref[:, 0:1], means_two_ref[:, 1:2]
    scale = norm_ref[:, 2:3] * inv
    for p in range(rows + 2):
        if p == 0:
            raw = above_ref[...]
        elif p == rows + 1:
            raw = below_ref[...]
        else:
            raw = raw_ref[:, cut(p - 1)]
        centred = (raw - mean) * inv
        grad = scale * (slope_ref[:, cut(p)] - shift_mean - centred * gain_mean)
        if p == 0:
            grad = jnp.where(place_ref[1] > 0, grad, 0.0)
        elif p == rows + 1:
            grad = jnp.where(place_ref[1] < groups - 1, grad, 0.0)
        fill_stack(stack_ref, 0, BACKWARD, p, grad)
    back = None
    for a in range(3):
        term = matmul(
            kernel_ref[:, a * 3 * chans : (a + 1) * 3 * chans],
            stack_ref[:, (2 - a) * LANES : (2 - a + rows) * LANES],
        )
        back = term if back is None else back + term
    mean, inv = means_one_ref[:, 0:1], means_one_ref[:, 1:2]
    gain, shift = norm_ref[:, 0:1], norm_ref[:, 1:2]
    shift_sum = gain_sum = None
    slopes = []
    for q in range(rows):
        centred = (raw_one_ref[:, cut(q)] - mean) * inv
        act = gain * centred + shift
        gate = sigmoid(act)
        grad = back[:, cut(q)] + cot_ref[:, cut(q)].astype(f32)
        slope = grad * (gate * (1.0 + act * (1.0 - gate)))
        out_ref[:, cut(q)] = slope
        if q in (0, rows - 1):
            slopes.append(slope)
        shift_sum = slope if shift_sum is None else shift_sum + slope
        term = slope * centred
        gain_sum = term if gain_sum is None else gain_sum + term
    for_all(sums_ref, column_sums([shift_sum, gain_sum]))
    edge_rows(edge_ref, place_ref, groups, slopes[0], slopes[-1])


def halves(place_ref, own, nc, rows_at):
    low = place_ref[0] & 1
    found = []
    for side in (low, 1 - low):
        for pair in range(nc // 2):
            found.append(rows_at(pl.multiple_of((2 * pair + side) * own, own)))
    return jnp.concatenate(found, axis=0)


def first_back_body(
    cfg, place_ref, slope_ref, slope_above_ref, slope_below_ref, raw_ref, above_ref, below_ref,
    means_ref, stats_ref, norm_ref, grads_two_ref, own_ref, halo_ref, hidden_ref, stack_two_ref,
    keep_ref, send_ref, stack_ref, grads_ref, squares_ref, cells_ref,
):
    rows, chans, own, nc, one_width, groups, pixel_count = cfg
    wide = (rows + 2) * LANES
    total = jnp.sum(stats_ref[...], axis=0)
    grads = jnp.concatenate(
        [total[1:2], total[0:1], grads_two_ref[1:2], grads_two_ref[0:1]], axis=0
    )
    grads_ref[...] = grads
    squares_ref[...] = jnp.sum(grads * grads).reshape(1, 1)
    columns = to_columns([total[0:1] / pixel_count, total[1:2] / pixel_count])
    shift_mean, gain_mean = columns[:, 0:1], columns[:, 1:2]
    mean, inv = means_ref[:, 0:1], means_ref[:, 1:2]
    scale = norm_ref[:, 0:1] * inv
    for p in range(rows + 2):
        if p == 0:
            raw, slope = above_ref[...], slope_above_ref[...]
        elif p == rows + 1:
            raw, slope = below_ref[...], slope_below_ref[...]
        else:
            raw, slope = raw_ref[:, cut(p - 1)], slope_ref[:, cut(p - 1)]
        grad = scale * (slope - shift_mean - (raw - mean) * inv * gain_mean)
        if p == 0:
            grad = jnp.where(place_ref[1] > 0, grad, 0.0)
        elif p == rows + 1:
            grad = jnp.where(place_ref[1] < groups - 1, grad, 0.0)
        fill_stack(stack_ref, 0, BACKWARD, p, grad)
    cells_ref[:, :LANES] = halo_ref[:, :LANES]
    cells_ref[:, LANES : wide - LANES] = own_ref[:, LANES : wide - LANES]
    cells_ref[:, wide - LANES :] = halo_ref[:, LANES:]
    half = chans // 2
    ordered = halves(
        place_ref, own, nc,
        lambda start: stack_ref[pl.ds(chans + start, own), LANES : (rows + 1) * LANES],
    )
    hidden = halves(place_ref, own, nc, lambda start: hidden_ref[pl.ds(start, own), :]).astype(bf16)
    for a in range(3):
        grad = matmul_nt(ordered, cells_ref[:, a * LANES : (a + rows) * LANES]).astype(bf16)
        to = slice(a * one_width, (a + 1) * one_width)
        keep_ref[:, to] = grad[:half]
        send_ref[:, to] = grad[half:]
        grad = matmul_nt(hidden, stack_two_ref[:, (2 - a) * LANES : (2 - a + rows) * LANES]).astype(bf16)
        start = 3 * one_width + a * 3 * chans
        keep_ref[:, start : start + 3 * chans] = grad[:half]
        send_ref[:, start : start + 3 * chans] = grad[half:]


def inputs_back_body(cfg, stack_ref, kernel_ref, mixed_ref, back_ref):
    rows, chans, lid, lid_own, cam_own, spg, nc = cfg
    per_strip = rows // spg
    back = None
    for a in range(3):
        term = matmul(
            kernel_ref[:, a * 3 * chans : (a + 1) * 3 * chans],
            stack_ref[:, (2 - a) * LANES : (2 - a + rows) * LANES],
        )
        back = term if back is None else back + term
    for s in range(spg):
        cells = slice(s * per_strip * LANES, (s + 1) * per_strip * LANES)
        for c in range(nc):
            block = s * nc + c
            back_ref[block, 0:lid_own, :] = back[c * lid_own : (c + 1) * lid_own, cells].astype(bf16)
            back_ref[block, lid_own : 2 * lid_own, :] = mixed_ref[block]
            start = lid + c * cam_own
            back_ref[block, 2 * lid_own : 2 * lid_own + cam_own, :] = back[
                start : start + cam_own, cells
            ].astype(bf16)


def adam(weight, gradient, first, second, rate):
    first = beta_one * first + (1.0 - beta_one) * gradient
    second = beta_two * second + (1.0 - beta_two) * gradient * gradient
    fix_one = 1.0 - beta_one**STEP
    fix_two = 1.0 - beta_two**STEP
    stepped = first / fix_one / (jnp.sqrt(second / fix_two) + adam_eps)
    return weight - rate * (stepped + weight_decay * weight), first, second


def add_body(mine_ref, other_ref, out_ref):
    out_ref[...] = (mine_ref[...].astype(f32) + other_ref[...].astype(f32)).astype(bf16)


def sum_body(pieces_ref, out_ref):
    out_ref[...] = jnp.sum(pieces_ref[...].astype(f32), axis=0).astype(bf16)


def merge_body(copies, mine_ref, other_ref, out_ref):
    width = mine_ref.shape[1]
    piece = (mine_ref[...].astype(f32) + other_ref[...].astype(f32)).astype(bf16)
    values = piece.astype(f32)
    squares = jnp.sum(values * values).reshape(1, 1)
    high = squares.astype(bf16).astype(f32)
    middle = (squares - high).astype(bf16).astype(f32)
    low = squares - high - middle
    shape = (piece.shape[0], LANES)
    row = lax.broadcasted_iota(jnp.int32, shape, 0)
    lane = lax.broadcasted_iota(jnp.int32, shape, 1)
    terms = jnp.where(lane == 0, high, jnp.where(lane == 1, middle, jnp.where(lane == 2, low, 0.0)))
    terms = jnp.where(row == 0, terms, 0.0).astype(bf16)
    for copy in range(copies):
        out_ref[copy, :, :width] = piece
        out_ref[copy, :, width:] = terms


def tail_body(width, pieces_ref, out_ref):
    out_ref[...] = jnp.broadcast_to(jnp.sum(pieces_ref[:, :, width:].astype(f32)), out_ref.shape)


def adam_body(lid, cam, mid, chans, smalls, *refs):
    square_refs, grads_ref, refs = refs[:chans], refs[chans], refs[chans + 1 :]
    small_fars, fars, refs = refs[:smalls], refs[smalls : smalls + 9], refs[smalls + 9 :]
    small_outs, far_outs, refs = refs[:4], refs[4:13], refs[13:]
    small_nears, nears, refs = refs[:smalls], refs[smalls : smalls + 9], refs[smalls + 9 :]
    small_ins, ins, outs, norm_ref = refs
    one_width = round_up(3 * lid + 3 * cam, 256)
    first = [
        pltpu.make_async_copy(far, near, small_ins.at[i])
        for i, (far, near) in enumerate(zip(small_fars, small_nears, strict=True))
    ]
    reads = [
        [pltpu.make_async_copy(fars[i].at[a], nears[i].at[a], ins.at[i, a]) for i in range(9)]
        for a in range(3)
    ]
    for group in (first, *reads):
        for copy in group:
            copy.start()
    for copy in first:
        copy.wait()
    squares = [ref[0:1, 0:1] for ref in square_refs]
    norm_squares_ref, norm_grad_ref, *norm_state = small_nears
    while len(squares) > 1:
        squares = [squares[i] + squares[i + 1] for i in range(0, len(squares), 2)]
    norm = jnp.sqrt(squares[0] + norm_squares_ref[...])
    norm_ref[...] = norm
    factor = jnp.minimum(1.0, clip_norm / (norm + 1e-06))

    def step(state, at, gradient, rate):
        weight, first, second = (ref[at] for ref in state)
        for ref, value in zip(state, adam(weight, factor * gradient, first, second, rate), strict=True):
            ref[at] = value

    step(norm_state, ..., norm_grad_ref[...], norm_rate)
    writes = [
        [
            pltpu.make_async_copy(near, far, small_ins.at[i])
            for i, (near, far) in enumerate(zip((*norm_state, norm_ref), small_outs, strict=True))
        ]
    ]
    for copy in writes[0]:
        copy.start()
    for a in range(3):
        for copy in reads[a]:
            copy.wait()
        base = a * one_width
        tail = grads_ref[:, base + 3 * lid : base + one_width].astype(f32)
        for b in range(3):
            start = 3 * one_width + (3 * a + b) * mid
            given = (
                tail[:, b * cam : (b + 1) * cam],
                grads_ref[:, base + b * lid : base + (b + 1) * lid].astype(f32),
                grads_ref[:, start : start + mid].astype(f32),
            )
            for i, gradient in enumerate(given):
                step(nears[3 * i : 3 * i + 3], (a, b), gradient, learn_rate)
        writes.append(
            [pltpu.make_async_copy(nears[i].at[a], far_outs[i].at[a], outs.at[i, a]) for i in range(9)]
        )
        for copy in writes[-1]:
            copy.start()
    for group in writes:
        for copy in group:
            copy.wait()


def shards(
    cam_feats,
    cell_index,
    lidar_bev,
    w_cam,
    w_lidar,
    w_mid,
    bn_params,
    cotangent,
    m_cam,
    v_cam,
    m_lidar,
    v_lidar,
    m_mid,
    v_mid,
    m_bn,
    v_bn,
):
    grids, lid_own, strip_rows, width = lidar_bev.shape
    cam_own, points = cam_feats.shape
    own = bn_params.shape[1]
    nc = lax.axis_size("chan")
    ns = lax.axis_size("strip")
    lid, cam, chans = nc * lid_own, nc * cam_own, nc * own
    spg = grids // nc
    groups = ns // spg
    members = spg * nc
    rows = spg * strip_rows
    cells = strip_rows * width
    pixel_count = float(grids * cells * ns)
    devices = ns * nc
    one_width = round_up(3 * lid + 3 * cam, 256)
    two_width = 3 * chans
    total_width = 3 * one_width + 3 * two_width
    chan = lax.axis_index("chan")
    group = lax.axis_index("strip") // spg
    place = jnp.stack([chan, group]).astype(jnp.int32)

    tile_groups = [[g * members + r for r in range(members)] for g in range(groups)]
    half_groups = [
        [(g * spg + s) * nc + 2 * pair + low for pair in range(nc // 2) for s in range(spg)]
        for g in range(groups)
        for low in range(2)
    ]
    core_groups = [
        [(g * spg + s) * nc + 2 * pair + low for s in range(spg) for pair in range(nc // 2)]
        for g in range(groups)
        for low in range(2)
    ]
    strip_groups = [
        [(g * spg + s) * nc + c for s in range(spg)] for g in range(groups) for c in range(nc)
    ]

    def exchange(blocks, parts):
        return lax.all_to_all(blocks, AXES, 0, 0, axis_index_groups=parts, tiled=True)

    def everywhere(copies):
        return lax.all_to_all(copies, AXES, 0, 0, tiled=True)

    def chan_swap(values, bit):
        return lax.ppermute(values, "chan", [(c, c ^ bit) for c in range(nc)])

    def neighbours(edges):
        if groups == 1:
            return edges[0], edges[0]
        if groups == 2:
            pairs = [(i, (i + members) % devices) for i in range(devices)]
            other = lax.ppermute(edges[0], AXES, pairs)
            return other, other
        down = [(i, i + members) for i in range(devices - members)]
        up = [(i + members, i) for i in range(devices - members)]
        return lax.ppermute(edges[0], AXES, down), lax.ppermute(edges[1], AXES, up)

    edge_count = 2 if groups > 2 else 1

    area = rows * LANES
    wide = (rows + 2) * LANES
    def from_all_channels(packed):
        parts, masks = [packed[None]], [0]
        bit = nc // 2
        while bit:
            stacked = parts[0] if len(parts) == 1 else jnp.concatenate(parts, axis=0)
            parts.append(chan_swap(stacked, bit))
            masks += [mask ^ bit for mask in masks]
            bit //= 2
        return parts, masks

    def edge_cells(got):
        last = got[members - nc :, :, cells - width :]
        first = got[:nc, :, :width]
        if groups == 2:
            return jnp.where(group == 0, last, first)[None]
        return jnp.stack([last, first])

    sums_struct = struct((devices, 2, chans), f32)
    packed_width = total_width + LANES

    index_row = cell_index.reshape(1, points)
    block = math.gcd(points, 1024)
    joined = call(
        functools.partial(pool_body, block), struct((grids, lid_own + own + cam_own, cells), bf16)
    )(
        index_row, cam_feats, lidar_bev.reshape(grids, lid_own, cells),
        cotangent.reshape(grids, own, cells),
    )
    got = exchange(joined, tile_groups)
    above, below = neighbours(edge_cells(got))

    turn = (0, 1, 3, 2)
    far = pl.BlockSpec(memory_space=pltpu.HBM)
    near = pl.BlockSpec(memory_space=pltpu.VMEM)
    weights = [w_lidar.transpose(turn), w_cam.transpose(turn), w_mid]
    packed = pl.pallas_call(
        functools.partial(pack_body, lid, cam, chans, one_width),
        in_specs=[far] * 4,
        out_specs=near,
        out_shape=struct((own, packed_width), bf16),
        scratch_shapes=[
            *(pltpu.VMEM(weight.shape, f32) for weight in (bn_params, *weights)),
            pltpu.SemaphoreType.DMA,
            pltpu.SemaphoreType.DMA((3, 3)),
        ],
        compiler_params=pltpu.CompilerParams(vmem_limit_bytes=VMEM_MOST),
    )(bn_params, *weights)
    parts, masks = from_all_channels(packed)
    kernel_one, kernel_two_t, norm = call(
        functools.partial(unpack_body, own, one_width, two_width, masks),
        [
            struct((chans, 3 * one_width), bf16),
            struct((chans, 3 * two_width), bf16),
            struct((chans, LANES), f32),
        ],
        scratch=[pltpu.VMEM((chans, packed_width), bf16)],
        smem=1,
    )(place, *parts)

    kernel_one_t, kernel_two = call(
        functools.partial(turn_body, lid, cam, one_width, chans),
        [struct((lid + cam, 3 * two_width), bf16), struct((chans, 3 * two_width), bf16)],
    )(kernel_one, kernel_two_t)
    own_stack, cot, part_one = call(
        functools.partial(first_body, (nc, spg, rows, lid, cam, lid_own, cam_own, one_width)),
        [
            struct((one_width, wide), bf16),
            struct((chans, area), bf16),
            struct((chans, area), f32),
        ],
    )(got, kernel_one)
    halo_stack, cot_halo, raw_one, sums_one, edges_one = call(
        functools.partial(
            first_halo_body, (nc, rows, lid, cam, lid_own, cam_own, one_width, groups)
        ),
        [
            struct((one_width, 2 * LANES), bf16),
            struct((chans, 2 * LANES), bf16),
            struct((chans, area), f32),
            sums_struct,
            struct((edge_count, chans, LANES), f32),
        ],
        smem=1,
        after=(kernel_one_t, kernel_two),
    )(place, part_one, above, below, kernel_one)

    above_one, below_one = neighbours(edges_one)
    stats_one = everywhere(sums_one)
    raw_two, sums_two, edges_two, hidden, means_one = call(
        functools.partial(second_body, (rows, chans, groups, pixel_count)),
        [
            struct((chans, area), f32),
            sums_struct,
            struct((edge_count, chans, LANES), f32),
            struct((chans, area), f32),
            struct((chans, LANES), f32),
        ],
        scratch=[pltpu.VMEM((two_width, wide), bf16)],
        smem=1,
    )(place, raw_one, above_one, below_one, stats_one, norm, kernel_two)

    above_two, below_two = neighbours(edges_two)
    stats_two = everywhere(sums_two)
    slope_two, sums_three, means_two, mixed_blocks = call(
        functools.partial(slope_body, (rows, own, spg, nc, pixel_count)),
        [
            struct((chans, wide), f32),
            sums_struct,
            struct((chans, LANES), f32),
            struct((members, own, cells), bf16),
        ],
        smem=1,
    )(place, raw_two, above_two, below_two, stats_two, norm, cot, cot_halo, hidden)

    stats_three = everywhere(sums_three)
    slope_one, sums_four, edges_four, grad_stack, grads_two = call(
        functools.partial(mid_back_body, (rows, chans, groups, pixel_count)),
        [
            struct((chans, area), f32),
            sums_struct,
            struct((edge_count, chans, LANES), f32),
            struct((two_width, wide), bf16),
            struct((2, chans), f32),
        ],
        smem=1,
    )(
        place, slope_two, raw_two, above_two, below_two, means_two, stats_three, norm,
        kernel_two_t, raw_one, means_one, cot,
    )

    above_four, below_four = neighbours(edges_four)
    stats_four = everywhere(sums_four)
    keep, send, grad_stack_one, grad_bn_all, norm_squares = call(
        functools.partial(
            first_back_body, (rows, chans, own, nc, one_width, groups, pixel_count)
        ),
        [
            struct((chans // 2, total_width), bf16),
            struct((chans // 2, total_width), bf16),
            struct((two_width, wide), bf16),
            struct((4, chans), f32),
            struct((1, 1), f32),
        ],
        scratch=[pltpu.VMEM((one_width, wide), bf16)],
        smem=1,
    )(
        place, slope_one, above_four, below_four, raw_one, above_one, below_one, means_one,
        stats_four, norm, grads_two, own_stack, halo_stack, hidden, grad_stack,
    )
    back_blocks = call(
        functools.partial(inputs_back_body, (rows, chans, lid, lid_own, cam_own, spg, nc)),
        struct((members, lid_own + own + cam_own, cells), bf16),
    )(grad_stack_one, kernel_one_t, mixed_blocks)
    home = exchange(back_blocks, core_groups)

    halved = call(add_body, struct(keep.shape, bf16), after=(back_blocks,))(keep, chan_swap(send, 1))
    piece_rows = own // spg
    pieces = exchange(halved.reshape(members // 2, piece_rows, total_width), half_groups)
    piece = call(sum_body, struct((piece_rows, total_width), bf16))(pieces)
    other = jnp.zeros_like(piece)
    shift = members
    while shift < devices:
        if shift > members:
            piece = (piece.astype(f32) + other.astype(f32)).astype(bf16)
        other = lax.ppermute(piece, AXES, [(i, i ^ shift) for i in range(devices)])
        shift *= 2
    merged = call(
        functools.partial(merge_body, spg), struct((spg, piece_rows, packed_width), bf16), after=(home,)
    )(piece, other)
    merged = exchange(merged, strip_groups)
    own_grads = merged.reshape(own, packed_width)
    keep_home, send_home = call(
        split_body, [struct((members // 2, *home.shape[1:]), bf16)] * 2, smem=1
    )(place, home)
    images = [struct(lidar_bev.shape, f32), struct(cotangent.shape, f32), struct((cam_own, points), f32)]
    grad_lidar, mixed, grad_cam, token = pl.pallas_call(
        functools.partial(home_body, block),
        in_specs=[pl.BlockSpec(memory_space=pltpu.SMEM)] + [near] * 3,
        out_specs=[far] * 3 + [near],
        out_shape=[*images, struct((8, LANES), f32)],
        scratch_shapes=[
            *(pltpu.VMEM(image.shape, f32) for image in images),
            pltpu.SemaphoreType.DMA((3,)),
        ],
        compiler_params=pltpu.CompilerParams(vmem_limit_bytes=VMEM_BYTES),
    )(place, index_row, keep_home, chan_swap(send_home, 1))
    tall = lambda array: array.transpose(turn)
    state = [
        *(tall(array) for array in (w_cam, m_cam, v_cam)),
        *(tall(array) for array in (w_lidar, m_lidar, v_lidar)),
        w_mid, m_mid, v_mid,
    ]
    squares = call(
        functools.partial(tail_body, total_width),
        struct((8, LANES), f32),
        after=(token,),
    )(merged)
    squares = [squares] + [
        lax.ppermute(squares, "chan", [(c, c ^ mask) for c in range(nc)]) for mask in range(1, nc)
    ]
    grad_bn = lax.dynamic_slice(grad_bn_all, (0, chan * own), (4, own))
    norm_state = [bn_params, m_bn, v_bn]
    small = [norm_squares, grad_bn, *norm_state]
    results = [*norm_state, norm_squares, *state]
    updated = pl.pallas_call(
        functools.partial(adam_body, lid, cam, chans, nc, len(small)),
        in_specs=[near] * (nc + 1) + [far] * (len(small) + 9),
        out_specs=[far] * 13,
        out_shape=[struct(array.shape, f32) for array in results],
        scratch_shapes=[
            *(pltpu.VMEM(array.shape, f32) for array in small + state),
            pltpu.SemaphoreType.DMA((len(small),)),
            pltpu.SemaphoreType.DMA((9, 3)),
            pltpu.SemaphoreType.DMA((9, 3)),
            pltpu.VMEM((1, 1), f32),
        ],
        compiler_params=pltpu.CompilerParams(vmem_limit_bytes=VMEM_MOST),
    )(*squares, own_grads, *small, *state)
    turned = [tall(array) for array in updated[4:10]]
    return (mixed, grad_cam, grad_lidar, updated[3].reshape(()), *turned, *updated[10:], *updated[:3])


def solution(mesh):
    return jax.shard_map(
        shards,
        mesh=mesh,
        in_specs=(
            P("chan", "strip"),
            P("strip"),
            P(None, "chan", "strip", None),
            P(None, None, None, "chan"),
            P(None, None, None, "chan"),
            P(None, None, "chan", None),
            P(None, "chan"),
            P(None, "chan", "strip", None),
            P(None, None, None, "chan"),
            P(None, None, None, "chan"),
            P(None, None, None, "chan"),
            P(None, None, None, "chan"),
            P(None, None, "chan", None),
            P(None, None, "chan", None),
            P(None, "chan"),
            P(None, "chan"),
        ),
        out_specs=(
            P(None, "chan", "strip", None),
            P("chan", "strip"),
            P(None, "chan", "strip", None),
            P(),
            P(None, None, None, "chan"),
            P(None, None, None, "chan"),
            P(None, None, None, "chan"),
            P(None, None, None, "chan"),
            P(None, None, None, "chan"),
            P(None, None, None, "chan"),
            P(None, None, "chan", None),
            P(None, None, "chan", None),
            P(None, None, "chan", None),
            P(None, "chan"),
            P(None, "chan"),
            P(None, "chan"),
        ),
        check_vma=False,
    )
```

```python
import functools
import math

import jax
import jax.numpy as jnp
from jax import lax
from jax.experimental import pallas as pl
from jax.experimental.pallas import tpu as pltpu
from jax.sharding import PartitionSpec as P

STEP = 10


beta_one = 0.9
beta_two = 0.999
adam_eps = 1e-08
learn_rate = 0.02
norm_rate = 1.5
weight_decay = 0.01
norm_eps = 1e-05
clip_norm = 1.0

AXES = ("strip", "chan")
LANES = 128
VMEM_BYTES = 24 * 1024 * 1024
VMEM_MOST = 60 * 1024 * 1024

f32 = jnp.float32
bf16 = jnp.bfloat16


def round_up(value, step):
    return (value + step - 1) // step * step


def call(body, out_shape, scratch=(), smem=0, after=()):
    waits = len(after)

    def run(*operands):
        specs = [pl.BlockSpec(memory_space=pltpu.SMEM)] * smem
        specs += [pl.BlockSpec(memory_space=pltpu.VMEM)] * (len(operands) - smem)
        specs = [pl.BlockSpec(memory_space=pl.ANY)] * waits + specs
        return pl.pallas_call(
            lambda *refs: body(*refs[waits:]),
            out_shape=out_shape,
            in_specs=specs,
            out_specs=jax.tree.map(lambda _: pl.BlockSpec(memory_space=pltpu.VMEM), out_shape),
            scratch_shapes=list(scratch),
            compiler_params=pltpu.CompilerParams(vmem_limit_bytes=VMEM_BYTES),
        )(*after, *operands)

    return run


def struct(shape, dtype):
    return jax.ShapeDtypeStruct(shape, dtype)


def cut(position):
    return slice(position * LANES, (position + 1) * LANES)


def sides(row):
    lane = lax.broadcasted_iota(jnp.int32, row.shape, 1)
    before = jnp.where(lane == 0, 0.0, pltpu.roll(row, 1, axis=1))
    after = jnp.where(lane == LANES - 1, 0.0, pltpu.roll(row, LANES - 1, axis=1))
    return before, after


def column_sums(parts):
    return jnp.concatenate([jnp.sum(part.T, axis=0, keepdims=True) for part in parts], axis=0)


def for_all(ref, values):
    ref[...] = jnp.broadcast_to(values[None], ref.shape)


def to_columns(rows):
    channels = rows[0].shape[1]
    rest = jnp.zeros((LANES - len(rows), channels), f32)
    return jnp.concatenate(list(rows) + [rest], axis=0).T


def matmul(left, right):
    return lax.dot_general(left, right, (((1,), (0,)), ((), ())), preferred_element_type=f32)


def matmul_nt(left, right):
    return lax.dot_general(left, right, (((1,), (1,)), ((), ())), preferred_element_type=f32)


def sigmoid(values):
    return 0.5 + 0.5 * jnp.tanh(0.5 * values)


def moments(received, pixel_count):
    total = jnp.sum(received, axis=0)
    mean = total[0:1] / pixel_count
    variance = total[1:2] / pixel_count - mean * mean
    return mean, lax.rsqrt(variance + norm_eps)


def one_hot(low, cells):
    count = low.shape[1]
    tile = 16
    given = jnp.broadcast_to(low.astype(f32), (tile, count)).astype(bf16)
    row = lax.broadcasted_iota(jnp.int32, (tile, count), 0).astype(f32).astype(bf16)
    one, zero = jnp.ones((), bf16), jnp.zeros((), bf16)
    return jnp.concatenate(
        [
            jnp.where(given - jnp.asarray(start, bf16) == row, one, zero)
            for start in range(0, cells, tile)
        ],
        axis=0,
    )


def split_body(place_ref, got_ref, keep_ref, send_ref):
    low = place_ref[0] & 1
    for pair in range(keep_ref.shape[0]):
        keep_ref[pair] = got_ref[2 * pair + low]
        send_ref[pair] = got_ref[2 * pair + 1 - low]


def pool_body(block, index_ref, feat_ref, lidar_ref, cot_ref, out_ref):
    grids, own, cells = lidar_ref.shape
    chans, points = feat_ref.shape
    out_ref[:, :own] = lidar_ref[...]
    out_ref[:, own : 2 * own] = cot_ref[...]
    rows = round_up(chans, 8)
    total = None
    for start in range(0, points, block):
        at = slice(start, start + block)
        index = index_ref[:, at]
        high, low = index // cells, index % cells
        feat = feat_ref[:, at].astype(f32)
        feat = jnp.concatenate([feat, jnp.zeros((rows - chans, block), f32)], axis=0)
        spread = jnp.concatenate([jnp.where(high == grid, feat, 0.0) for grid in range(grids)], axis=0)
        term = matmul_nt(spread.astype(bf16), one_hot(low, cells))
        total = term if total is None else total + term
    out_ref[:, 2 * own :] = total.reshape(grids, rows, cells)[:, :chans].astype(bf16)


def home_body(
    block, place_ref, index_ref, keep_ref, got_ref, lidar_far, mixed_far, cam_far, token_ref,
    lidar_ref, mixed_ref, cam_ref, sems,
):
    grids, own, _, _ = lidar_ref.shape
    cells = keep_ref.shape[2]
    chans, points = cam_ref.shape
    low = place_ref[0] & 1
    blocks = [(ref, pair, 2 * pair + parity) for ref, parity in ((keep_ref, low), (got_ref, 1 - low)) for pair in range(grids // 2)]
    token_ref[...] = jnp.zeros(token_ref.shape, f32)
    copies = []
    for i, (near, far) in enumerate(((lidar_ref, lidar_far), (mixed_ref, mixed_far))):
        for ref, pair, grid in blocks:
            near[grid] = ref[pair, i * own : (i + 1) * own, :].astype(f32).reshape(near.shape[1:])
        copies.append(pltpu.make_async_copy(near, far, sems.at[i]))
        copies[-1].start()
    rows = round_up(chans, 8)
    grad = jnp.concatenate([ref[:, 2 * own : 2 * own + chans, :] for ref in (keep_ref, got_ref)], axis=0)
    grad = jnp.concatenate([grad.astype(f32), jnp.zeros((grids, rows - chans, cells), f32)], axis=1)
    grad = grad.reshape(grids * rows, cells).astype(bf16)
    for start in range(0, points, block):
        at = slice(start, start + block)
        index = index_ref[:, at]
        high, low_part = index // cells, index % cells
        picked = matmul(grad, one_hot(low_part, cells))
        total = jnp.zeros((rows, block), f32)
        for i, (_, _, grid) in enumerate(blocks):
            total = jnp.where(high == grid, picked[i * rows : (i + 1) * rows], total)
        cam_ref[:, at] = total[:chans]
    copies.append(pltpu.make_async_copy(cam_ref, cam_far, sems.at[2]))
    copies[-1].start()
    for copy in copies:
        copy.wait()


def pack_body(
    lid, cam, mid, one_width, norm_ref, lidar_far, cam_far, mid_far, out_ref,
    near_ref, lidar_ref, cam_ref, mid_ref, norm_sem, sems,
):
    rows = lidar_ref.shape[2]
    norm_copy = pltpu.make_async_copy(norm_ref, near_ref, norm_sem)
    norm_copy.start()
    pairs = ((lidar_far, lidar_ref), (cam_far, cam_ref), (mid_far, mid_ref))
    copies = [
        [pltpu.make_async_copy(far.at[a], near.at[a], sems.at[i, a]) for i, (far, near) in enumerate(pairs)]
        for a in range(3)
    ]
    for group in copies:
        for copy in group:
            copy.start()
    for a in range(3):
        for copy in copies[a]:
            copy.wait()
        base = a * one_width
        for b in range(3):
            out_ref[:, base + b * lid : base + (b + 1) * lid] = lidar_ref[a, b].astype(bf16)
        used = 3 * lid + 3 * cam
        rest = [cam_ref[a, b] for b in range(3)]
        if one_width > used:
            rest.append(jnp.zeros((rows, one_width - used), f32))
        out_ref[:, base + 3 * lid : base + one_width] = jnp.concatenate(rest, axis=1).astype(bf16)
        for b in range(3):
            start = 3 * one_width + (3 * a + b) * mid
            out_ref[:, start : start + mid] = mid_ref[a, b].astype(bf16)
    norm_copy.wait()
    norm = near_ref[...]
    norm = jnp.concatenate([norm, jnp.zeros((LANES - norm.shape[0], rows), f32)], axis=0)
    norm = jnp.concatenate([norm, jnp.zeros((LANES, LANES - rows), f32)], axis=1).T[:rows, :4]
    high = norm.astype(bf16)
    left = norm - high.astype(f32)
    middle = left.astype(bf16)
    low = (left - middle.astype(f32)).astype(bf16)
    tail = jnp.concatenate(
        [high.astype(f32), middle.astype(f32), low.astype(f32), jnp.zeros((rows, LANES - 12), f32)],
        axis=1,
    )
    out_ref[:, 3 * one_width + 9 * mid :] = tail.astype(bf16)


def place_rows(own, masks, chan, parts, all_ref):
    place = 0
    for part in parts:
        for j in range(part.shape[0]):
            row = pl.multiple_of((chan ^ masks[place]) * own, own)
            all_ref[pl.ds(row, own), :] = part[j]
            place += 1


def unpack_body(own, one_width, two_width, masks, place_ref, *refs):
    parts, (one_ref, two_ref, norm_ref, all_ref) = refs[:-4], refs[-4:]
    place_rows(own, masks, place_ref[0], parts, all_ref)
    one_ref[...] = all_ref[:, : 3 * one_width]
    two_ref[...] = all_ref[:, 3 * one_width : 3 * (one_width + two_width)]
    tail = all_ref[:, 3 * (one_width + two_width) :].astype(f32)
    norm = tail[:, 0:4] + tail[:, 4:8] + tail[:, 8:12]
    norm_ref[...] = jnp.concatenate([norm, jnp.zeros((norm.shape[0], LANES - 4), f32)], axis=1)


def turn_body(lid, cam, one_width, outs, one_ref, two_t_ref, one_t_ref, two_ref):
    for t in range(9):
        at = slice(t * outs, (t + 1) * outs)
        two_ref[:, at] = two_t_ref[:, at].T
    for a in range(3):
        for b in range(3):
            to = slice((3 * a + b) * outs, (3 * a + b + 1) * outs)
            start = a * one_width + b * lid
            one_t_ref[0:lid, to] = one_ref[:, start : start + lid].T
        start = a * one_width + 3 * lid
        turned = one_ref[:, start : start + one_width - 3 * lid].T
        for b in range(3):
            to = slice((3 * a + b) * outs, (3 * a + b + 1) * outs)
            one_t_ref[lid : lid + cam, to] = turned[b * cam : (b + 1) * cam]


def edge_rows(edge_ref, place_ref, groups, first, last):
    if groups == 2:
        edge_ref[0] = jnp.where(place_ref[1] == 0, last, first)
    else:
        edge_ref[0] = last
        edge_ref[1] = first


def fill_stack(stack_ref, base, order, p, row):
    count = row.shape[0]
    for b, shifted in zip(order, (*sides(row), row), strict=True):
        start = base + b * count
        stack_ref[start : start + count, cut(p)] = shifted.astype(bf16)


FORWARD = (0, 2, 1)
BACKWARD = (2, 0, 1)


def first_body(cfg, got_ref, kernel_ref, stack_ref, cot_ref, part_ref):
    nc, spg, rows, lid, cam, lid_own, cam_own, one_width = cfg
    per_strip = rows // spg

    def take(q, first, count):
        s, r = q // per_strip, q % per_strip
        pieces = [got_ref[s * nc + c, first : first + count, cut(r)] for c in range(nc)]
        return jnp.concatenate([piece.astype(f32) for piece in pieces], axis=0)

    used = 3 * (lid + cam)
    stack_ref[:, cut(0)] = jnp.zeros((one_width, LANES), bf16)
    stack_ref[:, cut(rows + 1)] = jnp.zeros((one_width, LANES), bf16)
    if one_width > used:
        stack_ref[used:, :] = jnp.zeros((one_width - used, (rows + 2) * LANES), bf16)
    for q in range(rows):
        fill_stack(stack_ref, 0, FORWARD, q + 1, take(q, 0, lid_own))
        fill_stack(stack_ref, 3 * lid, FORWARD, q + 1, take(q, 2 * lid_own, cam_own))
        cot_ref[:, cut(q)] = take(q, lid_own, lid_own).astype(bf16)
    total = None
    for a in range(3):
        term = matmul(
            kernel_ref[:, a * one_width : (a + 1) * one_width],
            stack_ref[:, a * LANES : (a + rows) * LANES],
        )
        total = term if total is None else total + term
    part_ref[...] = total


def first_halo_body(
    cfg, place_ref, part_ref, above_ref, below_ref, kernel_ref,
    halo_ref, cot_ref, out_ref, sums_ref, edge_ref,
):
    nc, rows, lid, cam, lid_own, cam_own, one_width, groups = cfg
    has_above = place_ref[1] > 0
    has_below = place_ref[1] < groups - 1
    used = 3 * (lid + cam)
    if one_width > used:
        halo_ref[used:, :] = jnp.zeros((one_width - used, 2 * LANES), bf16)
    for side, (ref, given) in enumerate(((above_ref, has_above), (below_ref, has_below))):
        row = jnp.concatenate([ref[c, :lid_own].astype(f32) for c in range(nc)], axis=0)
        fill_stack(halo_ref, 0, FORWARD, side, jnp.where(given, row, 0.0))
        row = jnp.concatenate([ref[c, 2 * lid_own :].astype(f32) for c in range(nc)], axis=0)
        fill_stack(halo_ref, 3 * lid, FORWARD, side, jnp.where(given, row, 0.0))
        cot_ref[:, cut(side)] = jnp.concatenate([ref[c, lid_own : 2 * lid_own] for c in range(nc)], axis=0)
    lines = [part_ref[:, cut(q)] for q in range(rows)]
    lines[0] = lines[0] + matmul(kernel_ref[:, :one_width], halo_ref[:, cut(0)])
    lines[-1] = lines[-1] + matmul(kernel_ref[:, 2 * one_width :], halo_ref[:, cut(1)])
    finish_sums(lines, out_ref, sums_ref, edge_ref, place_ref, groups)


def finish_sums(lines, out_ref, sums_ref, edge_ref, place_ref, groups):
    sums = squares = None
    for q, row in enumerate(lines):
        out_ref[:, cut(q)] = row
        sums = row if sums is None else sums + row
        squares = row * row if squares is None else squares + row * row
    for_all(sums_ref, column_sums([sums, squares]))
    edge_rows(edge_ref, place_ref, groups, lines[0], lines[-1])


def second_body(
    cfg, place_ref, raw_ref, above_ref, below_ref, stats_ref, norm_ref, kernel_ref,
    out_ref, sums_ref, edge_ref, hidden_ref, means_ref, stack_ref,
):
    rows, chans, groups, pixel_count = cfg
    mean, inv = moments(stats_ref[...], pixel_count)
    columns = to_columns([mean, inv])
    means_ref[...] = columns
    mean, inv = columns[:, 0:1], columns[:, 1:2]
    gain, shift = norm_ref[:, 0:1], norm_ref[:, 1:2]
    for p in range(rows + 2):
        if p == 0:
            raw = above_ref[...]
        elif p == rows + 1:
            raw = below_ref[...]
        else:
            raw = raw_ref[:, cut(p - 1)]
        act = gain * ((raw - mean) * inv) + shift
        hidden = act * sigmoid(act)
        if p == 0:
            hidden = jnp.where(place_ref[1] > 0, hidden, 0.0)
        elif p == rows + 1:
            hidden = jnp.where(place_ref[1] < groups - 1, hidden, 0.0)
        else:
            hidden_ref[:, cut(p - 1)] = hidden
        fill_stack(stack_ref, 0, FORWARD, p, hidden)
    total = None
    for a in range(3):
        term = matmul(
            kernel_ref[:, a * 3 * chans : (a + 1) * 3 * chans],
            stack_ref[:, a * LANES : (a + rows) * LANES],
        )
        total = term if total is None else total + term
    lines = [total[:, cut(q)] for q in range(rows)]
    finish_sums(lines, out_ref, sums_ref, edge_ref, place_ref, groups)


def slope_body(
    cfg, place_ref, raw_ref, above_ref, below_ref, stats_ref, norm_ref, cot_ref, cot_halo_ref, hidden_ref,
    slope_ref, sums_ref, means_ref, mixed_ref,
):
    rows, own, spg, nc, pixel_count = cfg
    per_strip = rows // spg
    mean, inv = moments(stats_ref[...], pixel_count)
    columns = to_columns([mean, inv])
    means_ref[...] = columns
    mean, inv = columns[:, 0:1], columns[:, 1:2]
    gain, shift = norm_ref[:, 2:3], norm_ref[:, 3:4]
    shift_sum = gain_sum = None
    for p in range(rows + 2):
        if p == 0:
            raw, cot = above_ref[...], cot_halo_ref[:, cut(0)]
        elif p == rows + 1:
            raw, cot = below_ref[...], cot_halo_ref[:, cut(1)]
        else:
            raw, cot = raw_ref[:, cut(p - 1)], cot_ref[:, cut(p - 1)]
        centred = (raw - mean) * inv
        act = gain * centred + shift
        gate = sigmoid(act)
        slope = cot.astype(f32) * (gate * (1.0 + act * (1.0 - gate)))
        slope_ref[:, cut(p)] = slope
        if 0 < p <= rows:
            shift_sum = slope if shift_sum is None else shift_sum + slope
            term = slope * centred
            gain_sum = term if gain_sum is None else gain_sum + term
            mixed = (hidden_ref[:, cut(p - 1)] + act * gate).astype(bf16)
            s, r = (p - 1) // per_strip, (p - 1) % per_strip
            for c in range(nc):
                mixed_ref[s * nc + c, :, cut(r)] = mixed[c * own : (c + 1) * own]
    for_all(sums_ref, column_sums([shift_sum, gain_sum]))


def mid_back_body(
    cfg, place_ref, slope_ref, raw_ref, above_ref, below_ref, means_two_ref, stats_ref, norm_ref,
    kernel_ref, raw_one_ref, means_one_ref, cot_ref,
    out_ref, sums_ref, edge_ref, stack_ref, grads_ref,
):
    rows, chans, groups, pixel_count = cfg
    total = jnp.sum(stats_ref[...], axis=0)
    grads_ref[...] = total
    columns = to_columns([total[0:1] / pixel_count, total[1:2] / pixel_count])
    shift_mean, gain_mean = columns[:, 0:1], columns[:, 1:2]
    mean, inv = means_two_ref[:, 0:1], means_two_ref[:, 1:2]
    scale = norm_ref[:, 2:3] * inv
    for p in range(rows + 2):
        if p == 0:
            raw = above_ref[...]
        elif p == rows + 1:
            raw = below_ref[...]
        else:
            raw = raw_ref[:, cut(p - 1)]
        centred = (raw - mean) * inv
        grad = scale * (slope_ref[:, cut(p)] - shift_mean - centred * gain_mean)
        if p == 0:
            grad = jnp.where(place_ref[1] > 0, grad, 0.0)
        elif p == rows + 1:
            grad = jnp.where(place_ref[1] < groups - 1, grad, 0.0)
        fill_stack(stack_ref, 0, BACKWARD, p, grad)
    back = None
    for a in range(3):
        term = matmul(
            kernel_ref[:, a * 3 * chans : (a + 1) * 3 * chans],
            stack_ref[:, (2 - a) * LANES : (2 - a + rows) * LANES],
        )
        back = term if back is None else back + term
    mean, inv = means_one_ref[:, 0:1], means_one_ref[:, 1:2]
    gain, shift = norm_ref[:, 0:1], norm_ref[:, 1:2]
    shift_sum = gain_sum = None
    slopes = []
    for q in range(rows):
        centred = (raw_one_ref[:, cut(q)] - mean) * inv
        act = gain * centred + shift
        gate = sigmoid(act)
        grad = back[:, cut(q)] + cot_ref[:, cut(q)].astype(f32)
        slope = grad * (gate * (1.0 + act * (1.0 - gate)))
        out_ref[:, cut(q)] = slope
        if q in (0, rows - 1):
            slopes.append(slope)
        shift_sum = slope if shift_sum is None else shift_sum + slope
        term = slope * centred
        gain_sum = term if gain_sum is None else gain_sum + term
    for_all(sums_ref, column_sums([shift_sum, gain_sum]))
    edge_rows(edge_ref, place_ref, groups, slopes[0], slopes[-1])


def halves(place_ref, own, nc, rows_at):
    low = place_ref[0] & 1
    found = []
    for side in (low, 1 - low):
        for pair in range(nc // 2):
            found.append(rows_at(pl.multiple_of((2 * pair + side) * own, own)))
    return jnp.concatenate(found, axis=0)


def first_back_body(
    cfg, place_ref, slope_ref, slope_above_ref, slope_below_ref, raw_ref, above_ref, below_ref,
    means_ref, stats_ref, norm_ref, grads_two_ref, own_ref, halo_ref, hidden_ref, stack_two_ref,
    keep_ref, send_ref, stack_ref, grads_ref, squares_ref, cells_ref,
):
    rows, chans, own, nc, one_width, groups, pixel_count = cfg
    wide = (rows + 2) * LANES
    total = jnp.sum(stats_ref[...], axis=0)
    grads = jnp.concatenate(
        [total[1:2], total[0:1], grads_two_ref[1:2], grads_two_ref[0:1]], axis=0
    )
    grads_ref[...] = grads
    squares_ref[...] = jnp.sum(grads * grads).reshape(1, 1)
    columns = to_columns([total[0:1] / pixel_count, total[1:2] / pixel_count])
    shift_mean, gain_mean = columns[:, 0:1], columns[:, 1:2]
    mean, inv = means_ref[:, 0:1], means_ref[:, 1:2]
    scale = norm_ref[:, 0:1] * inv
    for p in range(rows + 2):
        if p == 0:
            raw, slope = above_ref[...], slope_above_ref[...]
        elif p == rows + 1:
            raw, slope = below_ref[...], slope_below_ref[...]
        else:
            raw, slope = raw_ref[:, cut(p - 1)], slope_ref[:, cut(p - 1)]
        grad = scale * (slope - shift_mean - (raw - mean) * inv * gain_mean)
        if p == 0:
            grad = jnp.where(place_ref[1] > 0, grad, 0.0)
        elif p == rows + 1:
            grad = jnp.where(place_ref[1] < groups - 1, grad, 0.0)
        fill_stack(stack_ref, 0, BACKWARD, p, grad)
    cells_ref[:, :LANES] = halo_ref[:, :LANES]
    cells_ref[:, LANES : wide - LANES] = own_ref[:, LANES : wide - LANES]
    cells_ref[:, wide - LANES :] = halo_ref[:, LANES:]
    half = chans // 2
    ordered = halves(
        place_ref, own, nc,
        lambda start: stack_ref[pl.ds(chans + start, own), LANES : (rows + 1) * LANES],
    )
    hidden = halves(place_ref, own, nc, lambda start: hidden_ref[pl.ds(start, own), :]).astype(bf16)
    for a in range(3):
        grad = matmul_nt(ordered, cells_ref[:, a * LANES : (a + rows) * LANES])
        to = slice(a * one_width, (a + 1) * one_width)
        keep_ref[:, to] = grad[:half]
        send_ref[:, to] = grad[half:].astype(bf16)
        grad = matmul_nt(hidden, stack_two_ref[:, (2 - a) * LANES : (2 - a + rows) * LANES])
        start = 3 * one_width + a * 3 * chans
        keep_ref[:, start : start + 3 * chans] = grad[:half]
        send_ref[:, start : start + 3 * chans] = grad[half:].astype(bf16)


def inputs_back_body(cfg, stack_ref, kernel_ref, mixed_ref, back_ref):
    rows, chans, lid, lid_own, cam_own, spg, nc = cfg
    per_strip = rows // spg
    back = None
    for a in range(3):
        term = matmul(
            kernel_ref[:, a * 3 * chans : (a + 1) * 3 * chans],
            stack_ref[:, (2 - a) * LANES : (2 - a + rows) * LANES],
        )
        back = term if back is None else back + term
    for s in range(spg):
        cells = slice(s * per_strip * LANES, (s + 1) * per_strip * LANES)
        for c in range(nc):
            block = s * nc + c
            back_ref[block, 0:lid_own, :] = back[c * lid_own : (c + 1) * lid_own, cells].astype(bf16)
            back_ref[block, lid_own : 2 * lid_own, :] = mixed_ref[block]
            start = lid + c * cam_own
            back_ref[block, 2 * lid_own : 2 * lid_own + cam_own, :] = back[
                start : start + cam_own, cells
            ].astype(bf16)


def adam(weight, gradient, first, second, rate):
    first = beta_one * first + (1.0 - beta_one) * gradient
    second = beta_two * second + (1.0 - beta_two) * gradient * gradient
    fix_one = 1.0 - beta_one**STEP
    fix_two = 1.0 - beta_two**STEP
    stepped = first / fix_one / (jnp.sqrt(second / fix_two) + adam_eps)
    return weight - rate * (stepped + weight_decay * weight), first, second


def add_body(mine_ref, other_ref, out_ref):
    out_ref[...] = (mine_ref[...] + other_ref[...].astype(f32)).astype(bf16)


def sum_body(pieces_ref, out_ref):
    out_ref[...] = jnp.sum(pieces_ref[...].astype(f32), axis=0).astype(bf16)


def merge_body(copies, mine_ref, other_ref, out_ref):
    width = mine_ref.shape[1]
    piece = (mine_ref[...].astype(f32) + other_ref[...].astype(f32)).astype(bf16)
    values = piece.astype(f32)
    squares = jnp.sum(values * values).reshape(1, 1)
    high = squares.astype(bf16).astype(f32)
    middle = (squares - high).astype(bf16).astype(f32)
    low = squares - high - middle
    shape = (piece.shape[0], LANES)
    row = lax.broadcasted_iota(jnp.int32, shape, 0)
    lane = lax.broadcasted_iota(jnp.int32, shape, 1)
    terms = jnp.where(lane == 0, high, jnp.where(lane == 1, middle, jnp.where(lane == 2, low, 0.0)))
    terms = jnp.where(row == 0, terms, 0.0).astype(bf16)
    for copy in range(copies):
        out_ref[copy, :, :width] = piece
        out_ref[copy, :, width:] = terms


def tail_body(width, pieces_ref, out_ref):
    out_ref[...] = jnp.broadcast_to(jnp.sum(pieces_ref[:, :, width:].astype(f32)), out_ref.shape)


def adam_body(lid, cam, mid, chans, smalls, *refs):
    square_refs, grads_ref, refs = refs[:chans], refs[chans], refs[chans + 1 :]
    small_fars, fars, refs = refs[:smalls], refs[smalls : smalls + 9], refs[smalls + 9 :]
    small_outs, far_outs, refs = refs[:4], refs[4:13], refs[13:]
    small_nears, nears, refs = refs[:smalls], refs[smalls : smalls + 9], refs[smalls + 9 :]
    small_ins, ins, outs, norm_ref = refs
    one_width = round_up(3 * lid + 3 * cam, 256)
    first = [
        pltpu.make_async_copy(far, near, small_ins.at[i])
        for i, (far, near) in enumerate(zip(small_fars, small_nears, strict=True))
    ]
    reads = [
        [pltpu.make_async_copy(fars[i].at[a], nears[i].at[a], ins.at[i, a]) for i in range(9)]
        for a in range(3)
    ]
    for group in (first, *reads):
        for copy in group:
            copy.start()
    for copy in first:
        copy.wait()
    squares = [ref[0:1, 0:1] for ref in square_refs]
    norm_squares_ref, norm_grad_ref, *norm_state = small_nears
    while len(squares) > 1:
        squares = [squares[i] + squares[i + 1] for i in range(0, len(squares), 2)]
    norm = jnp.sqrt(squares[0] + norm_squares_ref[...])
    norm_ref[...] = norm
    factor = jnp.minimum(1.0, clip_norm / (norm + 1e-06))

    def step(state, at, gradient, rate):
        weight, first, second = (ref[at] for ref in state)
        for ref, value in zip(state, adam(weight, factor * gradient, first, second, rate), strict=True):
            ref[at] = value

    step(norm_state, ..., norm_grad_ref[...], norm_rate)
    writes = [
        [
            pltpu.make_async_copy(near, far, small_ins.at[i])
            for i, (near, far) in enumerate(zip((*norm_state, norm_ref), small_outs, strict=True))
        ]
    ]
    for copy in writes[0]:
        copy.start()
    for a in range(3):
        for copy in reads[a]:
            copy.wait()
        base = a * one_width
        tail = grads_ref[:, base + 3 * lid : base + one_width].astype(f32)
        for b in range(3):
            start = 3 * one_width + (3 * a + b) * mid
            given = (
                tail[:, b * cam : (b + 1) * cam],
                grads_ref[:, base + b * lid : base + (b + 1) * lid].astype(f32),
                grads_ref[:, start : start + mid].astype(f32),
            )
            for i, gradient in enumerate(given):
                step(nears[3 * i : 3 * i + 3], (a, b), gradient, learn_rate)
        writes.append(
            [pltpu.make_async_copy(nears[i].at[a], far_outs[i].at[a], outs.at[i, a]) for i in range(9)]
        )
        for copy in writes[-1]:
            copy.start()
    for group in writes:
        for copy in group:
            copy.wait()


def shards(
    cam_feats,
    cell_index,
    lidar_bev,
    w_cam,
    w_lidar,
    w_mid,
    bn_params,
    cotangent,
    m_cam,
    v_cam,
    m_lidar,
    v_lidar,
    m_mid,
    v_mid,
    m_bn,
    v_bn,
):
    grids, lid_own, strip_rows, width = lidar_bev.shape
    cam_own, points = cam_feats.shape
    own = bn_params.shape[1]
    nc = lax.axis_size("chan")
    ns = lax.axis_size("strip")
    lid, cam, chans = nc * lid_own, nc * cam_own, nc * own
    spg = grids // nc
    groups = ns // spg
    members = spg * nc
    rows = spg * strip_rows
    cells = strip_rows * width
    pixel_count = float(grids * cells * ns)
    devices = ns * nc
    one_width = round_up(3 * lid + 3 * cam, 256)
    two_width = 3 * chans
    total_width = 3 * one_width + 3 * two_width
    chan = lax.axis_index("chan")
    group = lax.axis_index("strip") // spg
    place = jnp.stack([chan, group]).astype(jnp.int32)

    tile_groups = [[g * members + r for r in range(members)] for g in range(groups)]
    half_groups = [
        [(g * spg + s) * nc + 2 * pair + low for pair in range(nc // 2) for s in range(spg)]
        for g in range(groups)
        for low in range(2)
    ]
    core_groups = [
        [(g * spg + s) * nc + 2 * pair + low for s in range(spg) for pair in range(nc // 2)]
        for g in range(groups)
        for low in range(2)
    ]
    strip_groups = [
        [(g * spg + s) * nc + c for s in range(spg)] for g in range(groups) for c in range(nc)
    ]

    def exchange(blocks, parts):
        return lax.all_to_all(blocks, AXES, 0, 0, axis_index_groups=parts, tiled=True)

    def everywhere(copies):
        return lax.all_to_all(copies, AXES, 0, 0, tiled=True)

    def chan_swap(values, bit):
        return lax.ppermute(values, "chan", [(c, c ^ bit) for c in range(nc)])

    def neighbours(edges):
        if groups == 1:
            return edges[0], edges[0]
        if groups == 2:
            pairs = [(i, (i + members) % devices) for i in range(devices)]
            other = lax.ppermute(edges[0], AXES, pairs)
            return other, other
        down = [(i, i + members) for i in range(devices - members)]
        up = [(i + members, i) for i in range(devices - members)]
        return lax.ppermute(edges[0], AXES, down), lax.ppermute(edges[1], AXES, up)

    edge_count = 2 if groups > 2 else 1

    area = rows * LANES
    wide = (rows + 2) * LANES
    def from_all_channels(packed):
        parts, masks = [packed[None]], [0]
        bit = nc // 2
        while bit:
            stacked = parts[0] if len(parts) == 1 else jnp.concatenate(parts, axis=0)
            parts.append(chan_swap(stacked, bit))
            masks += [mask ^ bit for mask in masks]
            bit //= 2
        return parts, masks

    def edge_cells(got):
        last = got[members - nc :, :, cells - width :]
        first = got[:nc, :, :width]
        if groups == 2:
            return jnp.where(group == 0, last, first)[None]
        return jnp.stack([last, first])

    sums_struct = struct((devices, 2, chans), f32)
    packed_width = total_width + LANES

    index_row = cell_index.reshape(1, points)
    block = math.gcd(points, 1024)
    joined = call(
        functools.partial(pool_body, block), struct((grids, lid_own + own + cam_own, cells), bf16)
    )(
        index_row, cam_feats, lidar_bev.reshape(grids, lid_own, cells),
        cotangent.reshape(grids, own, cells),
    )
    got = exchange(joined, tile_groups)
    above, below = neighbours(edge_cells(got))

    turn = (0, 1, 3, 2)
    far = pl.BlockSpec(memory_space=pltpu.HBM)
    near = pl.BlockSpec(memory_space=pltpu.VMEM)
    weights = [w_lidar.transpose(turn), w_cam.transpose(turn), w_mid]
    packed = pl.pallas_call(
        functools.partial(pack_body, lid, cam, chans, one_width),
        in_specs=[far] * 4,
        out_specs=near,
        out_shape=struct((own, packed_width), bf16),
        scratch_shapes=[
            *(pltpu.VMEM(weight.shape, f32) for weight in (bn_params, *weights)),
            pltpu.SemaphoreType.DMA,
            pltpu.SemaphoreType.DMA((3, 3)),
        ],
        compiler_params=pltpu.CompilerParams(vmem_limit_bytes=VMEM_MOST),
    )(bn_params, *weights)
    parts, masks = from_all_channels(packed)
    kernel_one, kernel_two_t, norm = call(
        functools.partial(unpack_body, own, one_width, two_width, masks),
        [
            struct((chans, 3 * one_width), bf16),
            struct((chans, 3 * two_width), bf16),
            struct((chans, LANES), f32),
        ],
        scratch=[pltpu.VMEM((chans, packed_width), bf16)],
        smem=1,
    )(place, *parts)

    kernel_one_t, kernel_two = call(
        functools.partial(turn_body, lid, cam, one_width, chans),
        [struct((lid + cam, 3 * two_width), bf16), struct((chans, 3 * two_width), bf16)],
    )(kernel_one, kernel_two_t)
    own_stack, cot, part_one = call(
        functools.partial(first_body, (nc, spg, rows, lid, cam, lid_own, cam_own, one_width)),
        [
            struct((one_width, wide), bf16),
            struct((chans, area), bf16),
            struct((chans, area), f32),
        ],
    )(got, kernel_one)
    halo_stack, cot_halo, raw_one, sums_one, edges_one = call(
        functools.partial(
            first_halo_body, (nc, rows, lid, cam, lid_own, cam_own, one_width, groups)
        ),
        [
            struct((one_width, 2 * LANES), bf16),
            struct((chans, 2 * LANES), bf16),
            struct((chans, area), f32),
            sums_struct,
            struct((edge_count, chans, LANES), f32),
        ],
        smem=1,
        after=(kernel_one_t, kernel_two),
    )(place, part_one, above, below, kernel_one)

    above_one, below_one = neighbours(edges_one)
    stats_one = everywhere(sums_one)
    raw_two, sums_two, edges_two, hidden, means_one = call(
        functools.partial(second_body, (rows, chans, groups, pixel_count)),
        [
            struct((chans, area), f32),
            sums_struct,
            struct((edge_count, chans, LANES), f32),
            struct((chans, area), f32),
            struct((chans, LANES), f32),
        ],
        scratch=[pltpu.VMEM((two_width, wide), bf16)],
        smem=1,
    )(place, raw_one, above_one, below_one, stats_one, norm, kernel_two)

    above_two, below_two = neighbours(edges_two)
    stats_two = everywhere(sums_two)
    slope_two, sums_three, means_two, mixed_blocks = call(
        functools.partial(slope_body, (rows, own, spg, nc, pixel_count)),
        [
            struct((chans, wide), f32),
            sums_struct,
            struct((chans, LANES), f32),
            struct((members, own, cells), bf16),
        ],
        smem=1,
    )(place, raw_two, above_two, below_two, stats_two, norm, cot, cot_halo, hidden)

    stats_three = everywhere(sums_three)
    slope_one, sums_four, edges_four, grad_stack, grads_two = call(
        functools.partial(mid_back_body, (rows, chans, groups, pixel_count)),
        [
            struct((chans, area), f32),
            sums_struct,
            struct((edge_count, chans, LANES), f32),
            struct((two_width, wide), bf16),
            struct((2, chans), f32),
        ],
        smem=1,
    )(
        place, slope_two, raw_two, above_two, below_two, means_two, stats_three, norm,
        kernel_two_t, raw_one, means_one, cot,
    )

    above_four, below_four = neighbours(edges_four)
    stats_four = everywhere(sums_four)
    keep, send, grad_stack_one, grad_bn_all, norm_squares = call(
        functools.partial(
            first_back_body, (rows, chans, own, nc, one_width, groups, pixel_count)
        ),
        [
            struct((chans // 2, total_width), f32),
            struct((chans // 2, total_width), bf16),
            struct((two_width, wide), bf16),
            struct((4, chans), f32),
            struct((1, 1), f32),
        ],
        scratch=[pltpu.VMEM((one_width, wide), bf16)],
        smem=1,
    )(
        place, slope_one, above_four, below_four, raw_one, above_one, below_one, means_one,
        stats_four, norm, grads_two, own_stack, halo_stack, hidden, grad_stack,
    )
    back_blocks = call(
        functools.partial(inputs_back_body, (rows, chans, lid, lid_own, cam_own, spg, nc)),
        struct((members, lid_own + own + cam_own, cells), bf16),
    )(grad_stack_one, kernel_one_t, mixed_blocks)
    home = exchange(back_blocks, core_groups)

    halved = call(add_body, struct(keep.shape, bf16), after=(back_blocks,))(keep, chan_swap(send, 1))
    piece_rows = own // spg
    pieces = exchange(halved.reshape(members // 2, piece_rows, total_width), half_groups)
    piece = call(sum_body, struct((piece_rows, total_width), bf16))(pieces)
    other = jnp.zeros_like(piece)
    shift = members
    while shift < devices:
        if shift > members:
            piece = (piece.astype(f32) + other.astype(f32)).astype(bf16)
        other = lax.ppermute(piece, AXES, [(i, i ^ shift) for i in range(devices)])
        shift *= 2
    merged = call(
        functools.partial(merge_body, spg), struct((spg, piece_rows, packed_width), bf16)
    )(piece, other)
    merged, home = lax.optimization_barrier((merged, home))
    merged = exchange(merged, strip_groups)
    own_grads = merged.reshape(own, packed_width)
    keep_home, send_home = call(
        split_body, [struct((members // 2, *home.shape[1:]), bf16)] * 2, smem=1
    )(place, home)
    images = [struct(lidar_bev.shape, f32), struct(cotangent.shape, f32), struct((cam_own, points), f32)]
    grad_lidar, mixed, grad_cam, token = pl.pallas_call(
        functools.partial(home_body, block),
        in_specs=[pl.BlockSpec(memory_space=pltpu.SMEM)] + [near] * 3,
        out_specs=[far] * 3 + [near],
        out_shape=[*images, struct((8, LANES), f32)],
        scratch_shapes=[
            *(pltpu.VMEM(image.shape, f32) for image in images),
            pltpu.SemaphoreType.DMA((3,)),
        ],
        compiler_params=pltpu.CompilerParams(vmem_limit_bytes=VMEM_BYTES),
    )(place, index_row, keep_home, chan_swap(send_home, 1))
    tall = lambda array: array.transpose(turn)
    state = [
        *(tall(array) for array in (w_cam, m_cam, v_cam)),
        *(tall(array) for array in (w_lidar, m_lidar, v_lidar)),
        w_mid, m_mid, v_mid,
    ]
    squares = call(
        functools.partial(tail_body, total_width),
        struct((8, LANES), f32),
        after=(token,),
    )(merged)
    squares = [squares] + [
        lax.ppermute(squares, "chan", [(c, c ^ mask) for c in range(nc)]) for mask in range(1, nc)
    ]
    grad_bn = lax.dynamic_slice(grad_bn_all, (0, chan * own), (4, own))
    norm_state = [bn_params, m_bn, v_bn]
    small = [norm_squares, grad_bn, *norm_state]
    results = [*norm_state, norm_squares, *state]
    updated = pl.pallas_call(
        functools.partial(adam_body, lid, cam, chans, nc, len(small)),
        in_specs=[near] * (nc + 1) + [far] * (len(small) + 9),
        out_specs=[far] * 13,
        out_shape=[struct(array.shape, f32) for array in results],
        scratch_shapes=[
            *(pltpu.VMEM(array.shape, f32) for array in small + state),
            pltpu.SemaphoreType.DMA((len(small),)),
            pltpu.SemaphoreType.DMA((9, 3)),
            pltpu.SemaphoreType.DMA((9, 3)),
            pltpu.VMEM((1, 1), f32),
        ],
        compiler_params=pltpu.CompilerParams(vmem_limit_bytes=VMEM_MOST),
    )(*squares, own_grads, *small, *state)
    turned = [tall(array) for array in updated[4:10]]
    return (mixed, grad_cam, grad_lidar, updated[3].reshape(()), *turned, *updated[10:], *updated[:3])


def solution(mesh):
    return jax.shard_map(
        shards,
        mesh=mesh,
        in_specs=(
            P("chan", "strip"),
            P("strip"),
            P(None, "chan", "strip", None),
            P(None, None, None, "chan"),
            P(None, None, None, "chan"),
            P(None, None, "chan", None),
            P(None, "chan"),
            P(None, "chan", "strip", None),
            P(None, None, None, "chan"),
            P(None, None, None, "chan"),
            P(None, None, None, "chan"),
            P(None, None, None, "chan"),
            P(None, None, "chan", None),
            P(None, None, "chan", None),
            P(None, "chan"),
            P(None, "chan"),
        ),
        out_specs=(
            P(None, "chan", "strip", None),
            P("chan", "strip"),
            P(None, "chan", "strip", None),
            P(),
            P(None, None, None, "chan"),
            P(None, None, None, "chan"),
            P(None, None, None, "chan"),
            P(None, None, None, "chan"),
            P(None, None, None, "chan"),
            P(None, None, None, "chan"),
            P(None, None, "chan", None),
            P(None, None, "chan", None),
            P(None, None, "chan", None),
            P(None, "chan"),
            P(None, "chan"),
            P(None, "chan"),
        ),
        check_vma=False,
    )
```

```python
import functools
import math

import jax
import jax.numpy as jnp
from jax import lax
from jax.experimental import pallas as pl
from jax.experimental.pallas import tpu as pltpu
from jax.sharding import PartitionSpec as P

STEP = 10


beta_one = 0.9
beta_two = 0.999
adam_eps = 1e-08
learn_rate = 0.02
norm_rate = 1.5
weight_decay = 0.01
norm_eps = 1e-05
clip_norm = 1.0

AXES = ("strip", "chan")
LANES = 128
VMEM_BYTES = 24 * 1024 * 1024
VMEM_MOST = 60 * 1024 * 1024

f32 = jnp.float32
bf16 = jnp.bfloat16


def round_up(value, step):
    return (value + step - 1) // step * step


def call(body, out_shape, scratch=(), smem=0, after=()):
    waits = len(after)

    def run(*operands):
        specs = [pl.BlockSpec(memory_space=pltpu.SMEM)] * smem
        specs += [pl.BlockSpec(memory_space=pltpu.VMEM)] * (len(operands) - smem)
        specs = [pl.BlockSpec(memory_space=pl.ANY)] * waits + specs
        return pl.pallas_call(
            lambda *refs: body(*refs[waits:]),
            out_shape=out_shape,
            in_specs=specs,
            out_specs=jax.tree.map(lambda _: pl.BlockSpec(memory_space=pltpu.VMEM), out_shape),
            scratch_shapes=list(scratch),
            compiler_params=pltpu.CompilerParams(vmem_limit_bytes=VMEM_BYTES),
        )(*after, *operands)

    return run


def struct(shape, dtype):
    return jax.ShapeDtypeStruct(shape, dtype)


def cut(position):
    return slice(position * LANES, (position + 1) * LANES)


def sides(row):
    lane = lax.broadcasted_iota(jnp.int32, row.shape, 1)
    before = jnp.where(lane == 0, 0.0, pltpu.roll(row, 1, axis=1))
    after = jnp.where(lane == LANES - 1, 0.0, pltpu.roll(row, LANES - 1, axis=1))
    return before, after


def column_sums(parts):
    return jnp.concatenate([jnp.sum(part.T, axis=0, keepdims=True) for part in parts], axis=0)


def for_all(ref, values):
    ref[...] = jnp.broadcast_to(values[None], ref.shape)


def to_columns(rows):
    channels = rows[0].shape[1]
    rest = jnp.zeros((LANES - len(rows), channels), f32)
    return jnp.concatenate(list(rows) + [rest], axis=0).T


def matmul(left, right):
    return lax.dot_general(left, right, (((1,), (0,)), ((), ())), preferred_element_type=f32)


def matmul_nt(left, right):
    return lax.dot_general(left, right, (((1,), (1,)), ((), ())), preferred_element_type=f32)


def sigmoid(values):
    return 0.5 + 0.5 * jnp.tanh(0.5 * values)


def moments(received, pixel_count):
    total = jnp.sum(received, axis=0)
    mean = total[0:1] / pixel_count
    variance = total[1:2] / pixel_count - mean * mean
    return mean, lax.rsqrt(variance + norm_eps)


def one_hot(low, cells):
    count = low.shape[1]
    tile = 16
    given = jnp.broadcast_to(low.astype(f32), (tile, count)).astype(bf16)
    row = lax.broadcasted_iota(jnp.int32, (tile, count), 0).astype(f32).astype(bf16)
    one, zero = jnp.ones((), bf16), jnp.zeros((), bf16)
    return jnp.concatenate(
        [
            jnp.where(given - jnp.asarray(start, bf16) == row, one, zero)
            for start in range(0, cells, tile)
        ],
        axis=0,
    )


def split_body(place_ref, got_ref, keep_ref, send_ref):
    low = place_ref[0] & 1
    for pair in range(keep_ref.shape[0]):
        keep_ref[pair] = got_ref[2 * pair + low]
        send_ref[pair] = got_ref[2 * pair + 1 - low]


def pool_body(block, index_ref, feat_ref, lidar_ref, cot_ref, out_ref):
    grids, own, cells = lidar_ref.shape
    chans, points = feat_ref.shape
    out_ref[:, :own] = lidar_ref[...]
    out_ref[:, own : 2 * own] = cot_ref[...]
    rows = round_up(chans, 8)
    total = None
    for start in range(0, points, block):
        at = slice(start, start + block)
        index = index_ref[:, at]
        high, low = index // cells, index % cells
        feat = feat_ref[:, at].astype(f32)
        feat = jnp.concatenate([feat, jnp.zeros((rows - chans, block), f32)], axis=0)
        spread = jnp.concatenate([jnp.where(high == grid, feat, 0.0) for grid in range(grids)], axis=0)
        term = matmul_nt(spread.astype(bf16), one_hot(low, cells))
        total = term if total is None else total + term
    out_ref[:, 2 * own :] = total.reshape(grids, rows, cells)[:, :chans].astype(bf16)


def home_body(
    block, place_ref, index_ref, keep_ref, got_ref, lidar_far, mixed_far, cam_far, token_ref,
    lidar_ref, mixed_ref, cam_ref, sems,
):
    grids, own, _, _ = lidar_ref.shape
    cells = keep_ref.shape[2]
    chans, points = cam_ref.shape
    low = place_ref[0] & 1
    blocks = [(ref, pair, 2 * pair + parity) for ref, parity in ((keep_ref, low), (got_ref, 1 - low)) for pair in range(grids // 2)]
    token_ref[...] = jnp.zeros(token_ref.shape, f32)
    copies = []
    for i, (near, far) in enumerate(((lidar_ref, lidar_far), (mixed_ref, mixed_far))):
        for ref, pair, grid in blocks:
            near[grid] = ref[pair, i * own : (i + 1) * own, :].astype(f32).reshape(near.shape[1:])
        copies.append(pltpu.make_async_copy(near, far, sems.at[i]))
        copies[-1].start()
    rows = round_up(chans, 8)
    grad = jnp.concatenate([ref[:, 2 * own : 2 * own + chans, :] for ref in (keep_ref, got_ref)], axis=0)
    grad = jnp.concatenate([grad.astype(f32), jnp.zeros((grids, rows - chans, cells), f32)], axis=1)
    grad = grad.reshape(grids * rows, cells).astype(bf16)
    for start in range(0, points, block):
        at = slice(start, start + block)
        index = index_ref[:, at]
        high, low_part = index // cells, index % cells
        picked = matmul(grad, one_hot(low_part, cells))
        total = jnp.zeros((rows, block), f32)
        for i, (_, _, grid) in enumerate(blocks):
            total = jnp.where(high == grid, picked[i * rows : (i + 1) * rows], total)
        cam_ref[:, at] = total[:chans]
    copies.append(pltpu.make_async_copy(cam_ref, cam_far, sems.at[2]))
    copies[-1].start()
    for copy in copies:
        copy.wait()


def pack_body(
    lid, cam, mid, one_width, norm_ref, lidar_far, cam_far, mid_far, out_ref,
    near_ref, lidar_ref, cam_ref, mid_ref, norm_sem, sems,
):
    rows = lidar_ref.shape[2]
    norm_copy = pltpu.make_async_copy(norm_ref, near_ref, norm_sem)
    norm_copy.start()
    pairs = ((lidar_far, lidar_ref), (cam_far, cam_ref), (mid_far, mid_ref))
    copies = [
        [pltpu.make_async_copy(far.at[a], near.at[a], sems.at[i, a]) for i, (far, near) in enumerate(pairs)]
        for a in range(3)
    ]
    for group in copies:
        for copy in group:
            copy.start()
    for a in range(3):
        for copy in copies[a]:
            copy.wait()
        base = a * one_width
        for b in range(3):
            out_ref[:, base + b * lid : base + (b + 1) * lid] = lidar_ref[a, b].astype(bf16)
        used = 3 * lid + 3 * cam
        rest = [cam_ref[a, b] for b in range(3)]
        if one_width > used:
            rest.append(jnp.zeros((rows, one_width - used), f32))
        out_ref[:, base + 3 * lid : base + one_width] = jnp.concatenate(rest, axis=1).astype(bf16)
        for b in range(3):
            start = 3 * one_width + (3 * a + b) * mid
            out_ref[:, start : start + mid] = mid_ref[a, b].astype(bf16)
    norm_copy.wait()
    norm = near_ref[...]
    norm = jnp.concatenate([norm, jnp.zeros((LANES - norm.shape[0], rows), f32)], axis=0)
    norm = jnp.concatenate([norm, jnp.zeros((LANES, LANES - rows), f32)], axis=1).T[:rows, :4]
    high = norm.astype(bf16)
    left = norm - high.astype(f32)
    middle = left.astype(bf16)
    low = (left - middle.astype(f32)).astype(bf16)
    tail = jnp.concatenate(
        [high.astype(f32), middle.astype(f32), low.astype(f32), jnp.zeros((rows, LANES - 12), f32)],
        axis=1,
    )
    out_ref[:, 3 * one_width + 9 * mid :] = tail.astype(bf16)


def place_rows(own, masks, chan, parts, all_ref):
    place = 0
    for part in parts:
        for j in range(part.shape[0]):
            row = pl.multiple_of((chan ^ masks[place]) * own, own)
            all_ref[pl.ds(row, own), :] = part[j]
            place += 1


def unpack_body(own, one_width, two_width, masks, place_ref, *refs):
    parts, (one_ref, two_ref, norm_ref, all_ref) = refs[:-4], refs[-4:]
    place_rows(own, masks, place_ref[0], parts, all_ref)
    one_ref[...] = all_ref[:, : 3 * one_width]
    two_ref[...] = all_ref[:, 3 * one_width : 3 * (one_width + two_width)]
    tail = all_ref[:, 3 * (one_width + two_width) :].astype(f32)
    norm = tail[:, 0:4] + tail[:, 4:8] + tail[:, 8:12]
    norm_ref[...] = jnp.concatenate([norm, jnp.zeros((norm.shape[0], LANES - 4), f32)], axis=1)


def turn_body(lid, cam, one_width, outs, one_ref, two_t_ref, one_t_ref, two_ref):
    for t in range(9):
        at = slice(t * outs, (t + 1) * outs)
        two_ref[:, at] = two_t_ref[:, at].T
    for a in range(3):
        for b in range(3):
            to = slice((3 * a + b) * outs, (3 * a + b + 1) * outs)
            start = a * one_width + b * lid
            one_t_ref[0:lid, to] = one_ref[:, start : start + lid].T
        start = a * one_width + 3 * lid
        turned = one_ref[:, start : start + one_width - 3 * lid].T
        for b in range(3):
            to = slice((3 * a + b) * outs, (3 * a + b + 1) * outs)
            one_t_ref[lid : lid + cam, to] = turned[b * cam : (b + 1) * cam]


def edge_rows(edge_ref, place_ref, groups, first, last):
    if groups == 2:
        edge_ref[0] = jnp.where(place_ref[1] == 0, last, first)
    else:
        edge_ref[0] = last
        edge_ref[1] = first


def fill_stack(stack_ref, base, order, p, row):
    count = row.shape[0]
    for b, shifted in zip(order, (*sides(row), row), strict=True):
        start = base + b * count
        stack_ref[start : start + count, cut(p)] = shifted.astype(bf16)


FORWARD = (0, 2, 1)
BACKWARD = (2, 0, 1)


def first_body(cfg, got_ref, kernel_ref, stack_ref, cot_ref, part_ref):
    nc, spg, rows, lid, cam, lid_own, cam_own, one_width = cfg
    per_strip = rows // spg

    def take(q, first, count):
        s, r = q // per_strip, q % per_strip
        pieces = [got_ref[s * nc + c, first : first + count, cut(r)] for c in range(nc)]
        return jnp.concatenate([piece.astype(f32) for piece in pieces], axis=0)

    used = 3 * (lid + cam)
    stack_ref[:, cut(0)] = jnp.zeros((one_width, LANES), bf16)
    stack_ref[:, cut(rows + 1)] = jnp.zeros((one_width, LANES), bf16)
    if one_width > used:
        stack_ref[used:, :] = jnp.zeros((one_width - used, (rows + 2) * LANES), bf16)
    for q in range(rows):
        fill_stack(stack_ref, 0, FORWARD, q + 1, take(q, 0, lid_own))
        fill_stack(stack_ref, 3 * lid, FORWARD, q + 1, take(q, 2 * lid_own, cam_own))
        cot_ref[:, cut(q)] = take(q, lid_own, lid_own).astype(bf16)
    total = None
    for a in range(3):
        term = matmul(
            kernel_ref[:, a * one_width : (a + 1) * one_width],
            stack_ref[:, a * LANES : (a + rows) * LANES],
        )
        total = term if total is None else total + term
    part_ref[...] = total


def first_halo_body(
    cfg, place_ref, part_ref, above_ref, below_ref, kernel_ref,
    halo_ref, cot_ref, out_ref, sums_ref, edge_ref,
):
    nc, rows, lid, cam, lid_own, cam_own, one_width, groups = cfg
    has_above = place_ref[1] > 0
    has_below = place_ref[1] < groups - 1
    used = 3 * (lid + cam)
    if one_width > used:
        halo_ref[used:, :] = jnp.zeros((one_width - used, 2 * LANES), bf16)
    for side, (ref, given) in enumerate(((above_ref, has_above), (below_ref, has_below))):
        row = jnp.concatenate([ref[c, :lid_own].astype(f32) for c in range(nc)], axis=0)
        fill_stack(halo_ref, 0, FORWARD, side, jnp.where(given, row, 0.0))
        row = jnp.concatenate([ref[c, 2 * lid_own :].astype(f32) for c in range(nc)], axis=0)
        fill_stack(halo_ref, 3 * lid, FORWARD, side, jnp.where(given, row, 0.0))
        cot_ref[:, cut(side)] = jnp.concatenate([ref[c, lid_own : 2 * lid_own] for c in range(nc)], axis=0)
    lines = [part_ref[:, cut(q)] for q in range(rows)]
    lines[0] = lines[0] + matmul(kernel_ref[:, :one_width], halo_ref[:, cut(0)])
    lines[-1] = lines[-1] + matmul(kernel_ref[:, 2 * one_width :], halo_ref[:, cut(1)])
    finish_sums(lines, out_ref, sums_ref, edge_ref, place_ref, groups)


def finish_sums(lines, out_ref, sums_ref, edge_ref, place_ref, groups):
    sums = squares = None
    for q, row in enumerate(lines):
        out_ref[:, cut(q)] = row
        sums = row if sums is None else sums + row
        squares = row * row if squares is None else squares + row * row
    for_all(sums_ref, column_sums([sums, squares]))
    edge_rows(edge_ref, place_ref, groups, lines[0], lines[-1])


def second_body(
    cfg, place_ref, raw_ref, above_ref, below_ref, stats_ref, norm_ref, kernel_ref,
    out_ref, sums_ref, edge_ref, hidden_ref, means_ref, stack_ref,
):
    rows, chans, groups, pixel_count = cfg
    mean, inv = moments(stats_ref[...], pixel_count)
    columns = to_columns([mean, inv])
    means_ref[...] = columns
    mean, inv = columns[:, 0:1], columns[:, 1:2]
    gain, shift = norm_ref[:, 0:1], norm_ref[:, 1:2]
    for p in range(rows + 2):
        if p == 0:
            raw = above_ref[...]
        elif p == rows + 1:
            raw = below_ref[...]
        else:
            raw = raw_ref[:, cut(p - 1)]
        act = gain * ((raw - mean) * inv) + shift
        hidden = act * sigmoid(act)
        if p == 0:
            hidden = jnp.where(place_ref[1] > 0, hidden, 0.0)
        elif p == rows + 1:
            hidden = jnp.where(place_ref[1] < groups - 1, hidden, 0.0)
        else:
            hidden_ref[:, cut(p - 1)] = hidden
        fill_stack(stack_ref, 0, FORWARD, p, hidden)
    total = None
    for a in range(3):
        term = matmul(
            kernel_ref[:, a * 3 * chans : (a + 1) * 3 * chans],
            stack_ref[:, a * LANES : (a + rows) * LANES],
        )
        total = term if total is None else total + term
    lines = [total[:, cut(q)] for q in range(rows)]
    finish_sums(lines, out_ref, sums_ref, edge_ref, place_ref, groups)


def slope_body(
    cfg, place_ref, raw_ref, above_ref, below_ref, stats_ref, norm_ref, cot_ref, cot_halo_ref, hidden_ref,
    slope_ref, sums_ref, means_ref, mixed_ref,
):
    rows, own, spg, nc, pixel_count = cfg
    per_strip = rows // spg
    mean, inv = moments(stats_ref[...], pixel_count)
    columns = to_columns([mean, inv])
    means_ref[...] = columns
    mean, inv = columns[:, 0:1], columns[:, 1:2]
    gain, shift = norm_ref[:, 2:3], norm_ref[:, 3:4]
    shift_sum = gain_sum = None
    for p in range(rows + 2):
        if p == 0:
            raw, cot = above_ref[...], cot_halo_ref[:, cut(0)]
        elif p == rows + 1:
            raw, cot = below_ref[...], cot_halo_ref[:, cut(1)]
        else:
            raw, cot = raw_ref[:, cut(p - 1)], cot_ref[:, cut(p - 1)]
        centred = (raw - mean) * inv
        act = gain * centred + shift
        gate = sigmoid(act)
        slope = cot.astype(f32) * (gate * (1.0 + act * (1.0 - gate)))
        slope_ref[:, cut(p)] = slope
        if 0 < p <= rows:
            shift_sum = slope if shift_sum is None else shift_sum + slope
            term = slope * centred
            gain_sum = term if gain_sum is None else gain_sum + term
            mixed = (hidden_ref[:, cut(p - 1)] + act * gate).astype(bf16)
            s, r = (p - 1) // per_strip, (p - 1) % per_strip
            for c in range(nc):
                mixed_ref[s * nc + c, :, cut(r)] = mixed[c * own : (c + 1) * own]
    for_all(sums_ref, column_sums([shift_sum, gain_sum]))


def mid_back_body(
    cfg, place_ref, slope_ref, raw_ref, above_ref, below_ref, means_two_ref, stats_ref, norm_ref,
    kernel_ref, raw_one_ref, means_one_ref, cot_ref,
    out_ref, sums_ref, edge_ref, stack_ref, grads_ref,
):
    rows, chans, groups, pixel_count = cfg
    total = jnp.sum(stats_ref[...], axis=0)
    grads_ref[...] = total
    columns = to_columns([total[0:1] / pixel_count, total[1:2] / pixel_count])
    shift_mean, gain_mean = columns[:, 0:1], columns[:, 1:2]
    mean, inv = means_two_ref[:, 0:1], means_two_ref[:, 1:2]
    scale = norm_ref[:, 2:3] * inv
    for p in range(rows + 2):
        if p == 0:
            raw = above_ref[...]
        elif p == rows + 1:
            raw = below_ref[...]
        else:
            raw = raw_ref[:, cut(p - 1)]
        centred = (raw - mean) * inv
        grad = scale * (slope_ref[:, cut(p)] - shift_mean - centred * gain_mean)
        if p == 0:
            grad = jnp.where(place_ref[1] > 0, grad, 0.0)
        elif p == rows + 1:
            grad = jnp.where(place_ref[1] < groups - 1, grad, 0.0)
        fill_stack(stack_ref, 0, BACKWARD, p, grad)
    back = None
    for a in range(3):
        term = matmul(
            kernel_ref[:, a * 3 * chans : (a + 1) * 3 * chans],
            stack_ref[:, (2 - a) * LANES : (2 - a + rows) * LANES],
        )
        back = term if back is None else back + term
    mean, inv = means_one_ref[:, 0:1], means_one_ref[:, 1:2]
    gain, shift = norm_ref[:, 0:1], norm_ref[:, 1:2]
    shift_sum = gain_sum = None
    slopes = []
    for q in range(rows):
        centred = (raw_one_ref[:, cut(q)] - mean) * inv
        act = gain * centred + shift
        gate = sigmoid(act)
        grad = back[:, cut(q)] + cot_ref[:, cut(q)].astype(f32)
        slope = grad * (gate * (1.0 + act * (1.0 - gate)))
        out_ref[:, cut(q)] = slope
        if q in (0, rows - 1):
            slopes.append(slope)
        shift_sum = slope if shift_sum is None else shift_sum + slope
        term = slope * centred
        gain_sum = term if gain_sum is None else gain_sum + term
    for_all(sums_ref, column_sums([shift_sum, gain_sum]))
    edge_rows(edge_ref, place_ref, groups, slopes[0], slopes[-1])


def halves(place_ref, own, nc, rows_at):
    low = place_ref[0] & 1
    found = []
    for side in (low, 1 - low):
        for pair in range(nc // 2):
            found.append(rows_at(pl.multiple_of((2 * pair + side) * own, own)))
    return jnp.concatenate(found, axis=0)


def first_back_body(
    cfg, place_ref, slope_ref, slope_above_ref, slope_below_ref, raw_ref, above_ref, below_ref,
    means_ref, stats_ref, norm_ref, grads_two_ref, own_ref, halo_ref, hidden_ref, stack_two_ref,
    keep_ref, send_ref, stack_ref, grads_ref, squares_ref, cells_ref,
):
    rows, chans, own, nc, one_width, groups, pixel_count = cfg
    wide = (rows + 2) * LANES
    total = jnp.sum(stats_ref[...], axis=0)
    grads = jnp.concatenate(
        [total[1:2], total[0:1], grads_two_ref[1:2], grads_two_ref[0:1]], axis=0
    )
    grads_ref[...] = grads
    squares_ref[...] = jnp.broadcast_to(jnp.sum(grads * grads), squares_ref.shape)
    columns = to_columns([total[0:1] / pixel_count, total[1:2] / pixel_count])
    shift_mean, gain_mean = columns[:, 0:1], columns[:, 1:2]
    mean, inv = means_ref[:, 0:1], means_ref[:, 1:2]
    scale = norm_ref[:, 0:1] * inv
    for p in range(rows + 2):
        if p == 0:
            raw, slope = above_ref[...], slope_above_ref[...]
        elif p == rows + 1:
            raw, slope = below_ref[...], slope_below_ref[...]
        else:
            raw, slope = raw_ref[:, cut(p - 1)], slope_ref[:, cut(p - 1)]
        grad = scale * (slope - shift_mean - (raw - mean) * inv * gain_mean)
        if p == 0:
            grad = jnp.where(place_ref[1] > 0, grad, 0.0)
        elif p == rows + 1:
            grad = jnp.where(place_ref[1] < groups - 1, grad, 0.0)
        fill_stack(stack_ref, 0, BACKWARD, p, grad)
    cells_ref[:, :LANES] = halo_ref[:, :LANES]
    cells_ref[:, LANES : wide - LANES] = own_ref[:, LANES : wide - LANES]
    cells_ref[:, wide - LANES :] = halo_ref[:, LANES:]
    half = chans // 2
    ordered = halves(
        place_ref, own, nc,
        lambda start: stack_ref[pl.ds(chans + start, own), LANES : (rows + 1) * LANES],
    )
    hidden = halves(place_ref, own, nc, lambda start: hidden_ref[pl.ds(start, own), :]).astype(bf16)
    for a in range(3):
        grad = matmul_nt(ordered, cells_ref[:, a * LANES : (a + rows) * LANES])
        to = slice(a * one_width, (a + 1) * one_width)
        keep_ref[:, to] = grad[:half]
        send_ref[:, to] = grad[half:].astype(bf16)
        grad = matmul_nt(hidden, stack_two_ref[:, (2 - a) * LANES : (2 - a + rows) * LANES])
        start = 3 * one_width + a * 3 * chans
        keep_ref[:, start : start + 3 * chans] = grad[:half]
        send_ref[:, start : start + 3 * chans] = grad[half:].astype(bf16)


def inputs_back_body(cfg, stack_ref, kernel_ref, mixed_ref, back_ref):
    rows, chans, lid, lid_own, cam_own, spg, nc = cfg
    per_strip = rows // spg
    back = None
    for a in range(3):
        term = matmul(
            kernel_ref[:, a * 3 * chans : (a + 1) * 3 * chans],
            stack_ref[:, (2 - a) * LANES : (2 - a + rows) * LANES],
        )
        back = term if back is None else back + term
    for s in range(spg):
        cells = slice(s * per_strip * LANES, (s + 1) * per_strip * LANES)
        for c in range(nc):
            block = s * nc + c
            back_ref[block, 0:lid_own, :] = back[c * lid_own : (c + 1) * lid_own, cells].astype(bf16)
            back_ref[block, lid_own : 2 * lid_own, :] = mixed_ref[block]
            start = lid + c * cam_own
            back_ref[block, 2 * lid_own : 2 * lid_own + cam_own, :] = back[
                start : start + cam_own, cells
            ].astype(bf16)


def adam(weight, gradient, first, second, rate):
    first = beta_one * first + (1.0 - beta_one) * gradient
    second = beta_two * second + (1.0 - beta_two) * gradient * gradient
    fix_one = 1.0 - beta_one**STEP
    fix_two = 1.0 - beta_two**STEP
    stepped = first / fix_one / (jnp.sqrt(second / fix_two) + adam_eps)
    return weight - rate * (stepped + weight_decay * weight), first, second


def add_body(mine_ref, other_ref, out_ref):
    out_ref[...] = (mine_ref[...] + other_ref[...].astype(f32)).astype(bf16)


def sum_body(pieces_ref, out_ref):
    out_ref[...] = jnp.sum(pieces_ref[...].astype(f32), axis=0).astype(bf16)


def merge_body(copies, mine_ref, other_ref, out_ref):
    width = mine_ref.shape[1]
    piece = (mine_ref[...].astype(f32) + other_ref[...].astype(f32)).astype(bf16)
    values = piece.astype(f32)
    squares = jnp.sum(values * values).reshape(1, 1)
    high = squares.astype(bf16).astype(f32)
    middle = (squares - high).astype(bf16).astype(f32)
    low = squares - high - middle
    shape = (piece.shape[0], LANES)
    row = lax.broadcasted_iota(jnp.int32, shape, 0)
    lane = lax.broadcasted_iota(jnp.int32, shape, 1)
    terms = jnp.where(lane == 0, high, jnp.where(lane == 1, middle, jnp.where(lane == 2, low, 0.0)))
    terms = jnp.where(row == 0, terms, 0.0).astype(bf16)
    for copy in range(copies):
        out_ref[copy, :, :width] = piece
        out_ref[copy, :, width:] = terms


def tail_body(width, pieces_ref, out_ref):
    out_ref[...] = jnp.broadcast_to(jnp.sum(pieces_ref[:, :, width:].astype(f32)), out_ref.shape)


def adam_body(lid, cam, mid, chans, smalls, *refs):
    grads_far, refs = refs[0], refs[1:]
    small_fars, fars, refs = refs[:smalls], refs[smalls : smalls + 9], refs[smalls + 9 :]
    small_outs, far_outs, refs = refs[:4], refs[4:13], refs[13:]
    small_nears, nears, refs = refs[:smalls], refs[smalls : smalls + 9], refs[smalls + 9 :]
    small_ins, ins, outs, norm_ref, grads_ref, grads_sem = refs
    one_width = round_up(3 * lid + 3 * cam, 256)
    first = [
        pltpu.make_async_copy(far, near, small_ins.at[i])
        for i, (far, near) in enumerate(zip(small_fars, small_nears, strict=True))
    ]
    reads = [
        [pltpu.make_async_copy(fars[i].at[a], nears[i].at[a], ins.at[i, a]) for i in range(9)]
        for a in range(3)
    ]
    grads_copy = pltpu.make_async_copy(grads_far, grads_ref, grads_sem)
    for group in (first, [grads_copy], *reads):
        for copy in group:
            copy.start()
    for copy in first:
        copy.wait()
    squares = [ref[0:1, 0:1] for ref in small_nears[:chans]]
    norm_squares_ref, norm_grad_ref, *norm_state = small_nears[chans:]
    while len(squares) > 1:
        squares = [squares[i] + squares[i + 1] for i in range(0, len(squares), 2)]
    norm = jnp.sqrt(squares[0] + norm_squares_ref[0:1, 0:1])
    norm_ref[...] = norm
    factor = jnp.minimum(1.0, clip_norm / (norm + 1e-06))

    def step(state, at, gradient, rate):
        weight, first, second = (ref[at] for ref in state)
        for ref, value in zip(state, adam(weight, factor * gradient, first, second, rate), strict=True):
            ref[at] = value

    step(norm_state, ..., norm_grad_ref[...], norm_rate)
    writes = [
        [
            pltpu.make_async_copy(near, far, small_ins.at[i])
            for i, (near, far) in enumerate(zip((*norm_state, norm_ref), small_outs, strict=True))
        ]
    ]
    for copy in writes[0]:
        copy.start()
    grads_copy.wait()
    for a in range(3):
        for copy in reads[a]:
            copy.wait()
        base = a * one_width
        tail = grads_ref[:, base + 3 * lid : base + one_width].astype(f32)
        for b in range(3):
            start = 3 * one_width + (3 * a + b) * mid
            given = (
                tail[:, b * cam : (b + 1) * cam],
                grads_ref[:, base + b * lid : base + (b + 1) * lid].astype(f32),
                grads_ref[:, start : start + mid].astype(f32),
            )
            for i, gradient in enumerate(given):
                step(nears[3 * i : 3 * i + 3], (a, b), gradient, learn_rate)
        writes.append(
            [pltpu.make_async_copy(nears[i].at[a], far_outs[i].at[a], outs.at[i, a]) for i in range(9)]
        )
        for copy in writes[-1]:
            copy.start()
    for group in writes:
        for copy in group:
            copy.wait()


def shards(
    cam_feats,
    cell_index,
    lidar_bev,
    w_cam,
    w_lidar,
    w_mid,
    bn_params,
    cotangent,
    m_cam,
    v_cam,
    m_lidar,
    v_lidar,
    m_mid,
    v_mid,
    m_bn,
    v_bn,
):
    grids, lid_own, strip_rows, width = lidar_bev.shape
    cam_own, points = cam_feats.shape
    own = bn_params.shape[1]
    nc = lax.axis_size("chan")
    ns = lax.axis_size("strip")
    lid, cam, chans = nc * lid_own, nc * cam_own, nc * own
    spg = grids // nc
    groups = ns // spg
    members = spg * nc
    rows = spg * strip_rows
    cells = strip_rows * width
    pixel_count = float(grids * cells * ns)
    devices = ns * nc
    one_width = round_up(3 * lid + 3 * cam, 256)
    two_width = 3 * chans
    total_width = 3 * one_width + 3 * two_width
    chan = lax.axis_index("chan")
    group = lax.axis_index("strip") // spg
    place = jnp.stack([chan, group]).astype(jnp.int32)

    tile_groups = [[g * members + r for r in range(members)] for g in range(groups)]
    half_groups = [
        [(g * spg + s) * nc + 2 * pair + low for pair in range(nc // 2) for s in range(spg)]
        for g in range(groups)
        for low in range(2)
    ]
    core_groups = [
        [(g * spg + s) * nc + 2 * pair + low for s in range(spg) for pair in range(nc // 2)]
        for g in range(groups)
        for low in range(2)
    ]
    strip_groups = [
        [(g * spg + s) * nc + c for s in range(spg)] for g in range(groups) for c in range(nc)
    ]

    def exchange(blocks, parts):
        return lax.all_to_all(blocks, AXES, 0, 0, axis_index_groups=parts, tiled=True)

    def everywhere(copies):
        return lax.all_to_all(copies, AXES, 0, 0, tiled=True)

    def chan_swap(values, bit):
        return lax.ppermute(values, "chan", [(c, c ^ bit) for c in range(nc)])

    def neighbours(edges):
        if groups == 1:
            return edges[0], edges[0]
        if groups == 2:
            pairs = [(i, (i + members) % devices) for i in range(devices)]
            other = lax.ppermute(edges[0], AXES, pairs)
            return other, other
        down = [(i, i + members) for i in range(devices - members)]
        up = [(i + members, i) for i in range(devices - members)]
        return lax.ppermute(edges[0], AXES, down), lax.ppermute(edges[1], AXES, up)

    edge_count = 2 if groups > 2 else 1

    area = rows * LANES
    wide = (rows + 2) * LANES
    def from_all_channels(packed):
        parts, masks = [packed[None]], [0]
        bit = nc // 2
        while bit:
            stacked = parts[0] if len(parts) == 1 else jnp.concatenate(parts, axis=0)
            parts.append(chan_swap(stacked, bit))
            masks += [mask ^ bit for mask in masks]
            bit //= 2
        return parts, masks

    def edge_cells(got):
        last = got[members - nc :, :, cells - width :]
        first = got[:nc, :, :width]
        if groups == 2:
            return jnp.where(group == 0, last, first)[None]
        return jnp.stack([last, first])

    sums_struct = struct((devices, 2, chans), f32)
    packed_width = total_width + LANES

    index_row = cell_index.reshape(1, points)
    block = math.gcd(points, 1024)
    joined = call(
        functools.partial(pool_body, block), struct((grids, lid_own + own + cam_own, cells), bf16)
    )(
        index_row, cam_feats, lidar_bev.reshape(grids, lid_own, cells),
        cotangent.reshape(grids, own, cells),
    )
    got = exchange(joined, tile_groups)
    above, below = neighbours(edge_cells(got))

    turn = (0, 1, 3, 2)
    far = pl.BlockSpec(memory_space=pltpu.HBM)
    near = pl.BlockSpec(memory_space=pltpu.VMEM)
    weights = [w_lidar.transpose(turn), w_cam.transpose(turn), w_mid]
    packed = pl.pallas_call(
        functools.partial(pack_body, lid, cam, chans, one_width),
        in_specs=[far] * 4,
        out_specs=near,
        out_shape=struct((own, packed_width), bf16),
        scratch_shapes=[
            *(pltpu.VMEM(weight.shape, f32) for weight in (bn_params, *weights)),
            pltpu.SemaphoreType.DMA,
            pltpu.SemaphoreType.DMA((3, 3)),
        ],
        compiler_params=pltpu.CompilerParams(vmem_limit_bytes=VMEM_MOST),
    )(bn_params, *weights)
    parts, masks = from_all_channels(packed)
    kernel_one, kernel_two_t, norm = call(
        functools.partial(unpack_body, own, one_width, two_width, masks),
        [
            struct((chans, 3 * one_width), bf16),
            struct((chans, 3 * two_width), bf16),
            struct((chans, LANES), f32),
        ],
        scratch=[pltpu.VMEM((chans, packed_width), bf16)],
        smem=1,
    )(place, *parts)

    kernel_one_t, kernel_two = call(
        functools.partial(turn_body, lid, cam, one_width, chans),
        [struct((lid + cam, 3 * two_width), bf16), struct((chans, 3 * two_width), bf16)],
    )(kernel_one, kernel_two_t)
    own_stack, cot, part_one = call(
        functools.partial(first_body, (nc, spg, rows, lid, cam, lid_own, cam_own, one_width)),
        [
            struct((one_width, wide), bf16),
            struct((chans, area), bf16),
            struct((chans, area), f32),
        ],
    )(got, kernel_one)
    halo_stack, cot_halo, raw_one, sums_one, edges_one = call(
        functools.partial(
            first_halo_body, (nc, rows, lid, cam, lid_own, cam_own, one_width, groups)
        ),
        [
            struct((one_width, 2 * LANES), bf16),
            struct((chans, 2 * LANES), bf16),
            struct((chans, area), f32),
            sums_struct,
            struct((edge_count, chans, LANES), f32),
        ],
        smem=1,
        after=(kernel_one_t, kernel_two),
    )(place, part_one, above, below, kernel_one)

    above_one, below_one = neighbours(edges_one)
    stats_one = everywhere(sums_one)
    raw_two, sums_two, edges_two, hidden, means_one = call(
        functools.partial(second_body, (rows, chans, groups, pixel_count)),
        [
            struct((chans, area), f32),
            sums_struct,
            struct((edge_count, chans, LANES), f32),
            struct((chans, area), f32),
            struct((chans, LANES), f32),
        ],
        scratch=[pltpu.VMEM((two_width, wide), bf16)],
        smem=1,
    )(place, raw_one, above_one, below_one, stats_one, norm, kernel_two)

    above_two, below_two = neighbours(edges_two)
    stats_two = everywhere(sums_two)
    slope_two, sums_three, means_two, mixed_blocks = call(
        functools.partial(slope_body, (rows, own, spg, nc, pixel_count)),
        [
            struct((chans, wide), f32),
            sums_struct,
            struct((chans, LANES), f32),
            struct((members, own, cells), bf16),
        ],
        smem=1,
    )(place, raw_two, above_two, below_two, stats_two, norm, cot, cot_halo, hidden)

    stats_three = everywhere(sums_three)
    slope_one, sums_four, edges_four, grad_stack, grads_two = call(
        functools.partial(mid_back_body, (rows, chans, groups, pixel_count)),
        [
            struct((chans, area), f32),
            sums_struct,
            struct((edge_count, chans, LANES), f32),
            struct((two_width, wide), bf16),
            struct((2, chans), f32),
        ],
        smem=1,
    )(
        place, slope_two, raw_two, above_two, below_two, means_two, stats_three, norm,
        kernel_two_t, raw_one, means_one, cot,
    )

    above_four, below_four = neighbours(edges_four)
    stats_four = everywhere(sums_four)
    keep, send, grad_stack_one, grad_bn_all, norm_squares = call(
        functools.partial(
            first_back_body, (rows, chans, own, nc, one_width, groups, pixel_count)
        ),
        [
            struct((chans // 2, total_width), f32),
            struct((chans // 2, total_width), bf16),
            struct((two_width, wide), bf16),
            struct((4, chans), f32),
            struct((8, LANES), f32),
        ],
        scratch=[pltpu.VMEM((one_width, wide), bf16)],
        smem=1,
    )(
        place, slope_one, above_four, below_four, raw_one, above_one, below_one, means_one,
        stats_four, norm, grads_two, own_stack, halo_stack, hidden, grad_stack,
    )
    back_blocks = call(
        functools.partial(inputs_back_body, (rows, chans, lid, lid_own, cam_own, spg, nc)),
        struct((members, lid_own + own + cam_own, cells), bf16),
    )(grad_stack_one, kernel_one_t, mixed_blocks)
    home = exchange(back_blocks, core_groups)

    halved = call(add_body, struct(keep.shape, bf16), after=(back_blocks,))(keep, chan_swap(send, 1))
    piece_rows = own // spg
    pieces = exchange(halved.reshape(members // 2, piece_rows, total_width), half_groups)
    piece = call(sum_body, struct((piece_rows, total_width), bf16))(pieces)
    other = jnp.zeros_like(piece)
    shift = members
    while shift < devices:
        if shift > members:
            piece = (piece.astype(f32) + other.astype(f32)).astype(bf16)
        other = lax.ppermute(piece, AXES, [(i, i ^ shift) for i in range(devices)])
        shift *= 2
    merged = call(
        functools.partial(merge_body, spg), struct((spg, piece_rows, packed_width), bf16)
    )(piece, other)
    merged, home = lax.optimization_barrier((merged, home))
    merged = exchange(merged, strip_groups)
    own_grads = merged.reshape(own, packed_width)
    keep_home, send_home = call(
        split_body, [struct((members // 2, *home.shape[1:]), bf16)] * 2, smem=1
    )(place, home)
    images = [struct(lidar_bev.shape, f32), struct(cotangent.shape, f32), struct((cam_own, points), f32)]
    grad_lidar, mixed, grad_cam, token = pl.pallas_call(
        functools.partial(home_body, block),
        in_specs=[pl.BlockSpec(memory_space=pltpu.SMEM)] + [near] * 3,
        out_specs=[far] * 3 + [near],
        out_shape=[*images, struct((8, LANES), f32)],
        scratch_shapes=[
            *(pltpu.VMEM(image.shape, f32) for image in images),
            pltpu.SemaphoreType.DMA((3,)),
        ],
        compiler_params=pltpu.CompilerParams(vmem_limit_bytes=VMEM_BYTES),
    )(place, index_row, keep_home, chan_swap(send_home, 1))
    tall = lambda array: array.transpose(turn)
    state = [
        *(tall(array) for array in (w_cam, m_cam, v_cam)),
        *(tall(array) for array in (w_lidar, m_lidar, v_lidar)),
        w_mid, m_mid, v_mid,
    ]
    squares = call(
        functools.partial(tail_body, total_width),
        struct((8, LANES), f32),
        after=(token,),
    )(merged)
    squares = [squares] + [
        lax.ppermute(squares, "chan", [(c, c ^ mask) for c in range(nc)]) for mask in range(1, nc)
    ]
    grad_bn = lax.dynamic_slice(grad_bn_all, (0, chan * own), (4, own))
    norm_state = [bn_params, m_bn, v_bn]
    small = [*squares, norm_squares, grad_bn, *norm_state]
    results = [*norm_state, struct((1, 1), f32), *state]
    updated = pl.pallas_call(
        functools.partial(adam_body, lid, cam, chans, nc, len(small)),
        in_specs=[far] * (len(small) + 10),
        out_specs=[far] * 13,
        out_shape=[struct(array.shape, f32) for array in results],
        scratch_shapes=[
            *(pltpu.VMEM(array.shape, f32) for array in small + state),
            pltpu.SemaphoreType.DMA((len(small),)),
            pltpu.SemaphoreType.DMA((9, 3)),
            pltpu.SemaphoreType.DMA((9, 3)),
            pltpu.VMEM((1, 1), f32),
            pltpu.VMEM(own_grads.shape, bf16),
            pltpu.SemaphoreType.DMA,
        ],
        compiler_params=pltpu.CompilerParams(vmem_limit_bytes=VMEM_MOST),
    )(own_grads, *small, *state)
    turned = [tall(array) for array in updated[4:10]]
    return (mixed, grad_cam, grad_lidar, updated[3].reshape(()), *turned, *updated[10:], *updated[:3])


def solution(mesh):
    return jax.shard_map(
        shards,
        mesh=mesh,
        in_specs=(
            P("chan", "strip"),
            P("strip"),
            P(None, "chan", "strip", None),
            P(None, None, None, "chan"),
            P(None, None, None, "chan"),
            P(None, None, "chan", None),
            P(None, "chan"),
            P(None, "chan", "strip", None),
            P(None, None, None, "chan"),
            P(None, None, None, "chan"),
            P(None, None, None, "chan"),
            P(None, None, None, "chan"),
            P(None, None, "chan", None),
            P(None, None, "chan", None),
            P(None, "chan"),
            P(None, "chan"),
        ),
        out_specs=(
            P(None, "chan", "strip", None),
            P("chan", "strip"),
            P(None, "chan", "strip", None),
            P(),
            P(None, None, None, "chan"),
            P(None, None, None, "chan"),
            P(None, None, None, "chan"),
            P(None, None, None, "chan"),
            P(None, None, None, "chan"),
            P(None, None, None, "chan"),
            P(None, None, "chan", None),
            P(None, None, "chan", None),
            P(None, None, "chan", None),
            P(None, "chan"),
            P(None, "chan"),
            P(None, "chan"),
        ),
        check_vma=False,
    )
```

```python
import functools
import math

import jax
import jax.numpy as jnp
from jax import lax
from jax.experimental import pallas as pl
from jax.experimental.pallas import tpu as pltpu
from jax.sharding import PartitionSpec as P

STEP = 10


beta_one = 0.9
beta_two = 0.999
adam_eps = 1e-08
learn_rate = 0.02
norm_rate = 1.5
weight_decay = 0.01
norm_eps = 1e-05
clip_norm = 1.0

AXES = ("strip", "chan")
LANES = 128
VMEM_BYTES = 24 * 1024 * 1024
VMEM_MOST = 60 * 1024 * 1024

f32 = jnp.float32
bf16 = jnp.bfloat16


def round_up(value, step):
    return (value + step - 1) // step * step


def call(body, out_shape, scratch=(), smem=0, after=()):
    waits = len(after)

    def run(*operands):
        specs = [pl.BlockSpec(memory_space=pltpu.SMEM)] * smem
        specs += [pl.BlockSpec(memory_space=pltpu.VMEM)] * (len(operands) - smem)
        specs = [pl.BlockSpec(memory_space=pl.ANY)] * waits + specs
        return pl.pallas_call(
            lambda *refs: body(*refs[waits:]),
            out_shape=out_shape,
            in_specs=specs,
            out_specs=jax.tree.map(lambda _: pl.BlockSpec(memory_space=pltpu.VMEM), out_shape),
            scratch_shapes=list(scratch),
            compiler_params=pltpu.CompilerParams(vmem_limit_bytes=VMEM_BYTES),
        )(*after, *operands)

    return run


def struct(shape, dtype):
    return jax.ShapeDtypeStruct(shape, dtype)


def cut(position):
    return slice(position * LANES, (position + 1) * LANES)


def sides(row):
    lane = lax.broadcasted_iota(jnp.int32, row.shape, 1)
    before = jnp.where(lane == 0, 0.0, pltpu.roll(row, 1, axis=1))
    after = jnp.where(lane == LANES - 1, 0.0, pltpu.roll(row, LANES - 1, axis=1))
    return before, after


def column_sums(parts):
    return jnp.concatenate([jnp.sum(part.T, axis=0, keepdims=True) for part in parts], axis=0)


def for_all(ref, values):
    ref[...] = jnp.broadcast_to(values[None], ref.shape)


def to_columns(rows):
    channels = rows[0].shape[1]
    rest = jnp.zeros((LANES - len(rows), channels), f32)
    return jnp.concatenate(list(rows) + [rest], axis=0).T


def matmul(left, right):
    return lax.dot_general(left, right, (((1,), (0,)), ((), ())), preferred_element_type=f32)


def matmul_nt(left, right):
    return lax.dot_general(left, right, (((1,), (1,)), ((), ())), preferred_element_type=f32)


def sigmoid(values):
    return 0.5 + 0.5 * jnp.tanh(0.5 * values)


def moments(received, pixel_count):
    total = jnp.sum(received, axis=0)
    mean = total[0:1] / pixel_count
    variance = total[1:2] / pixel_count - mean * mean
    return mean, lax.rsqrt(variance + norm_eps)


def one_hot(low, cells):
    count = low.shape[1]
    tile = 16
    given = jnp.broadcast_to(low.astype(f32), (tile, count)).astype(bf16)
    row = lax.broadcasted_iota(jnp.int32, (tile, count), 0).astype(f32).astype(bf16)
    one, zero = jnp.ones((), bf16), jnp.zeros((), bf16)
    return jnp.concatenate(
        [
            jnp.where(given - jnp.asarray(start, bf16) == row, one, zero)
            for start in range(0, cells, tile)
        ],
        axis=0,
    )


def split_body(place_ref, got_ref, keep_ref, send_ref):
    low = place_ref[0] & 1
    for pair in range(keep_ref.shape[0]):
        keep_ref[pair] = got_ref[2 * pair + low]
        send_ref[pair] = got_ref[2 * pair + 1 - low]


def pool_body(block, index_ref, feat_ref, lidar_ref, cot_ref, out_ref):
    grids, own, cells = lidar_ref.shape
    chans, points = feat_ref.shape
    out_ref[:, :own] = lidar_ref[...]
    out_ref[:, own : 2 * own] = cot_ref[...]
    rows = round_up(chans, 8)
    total = None
    for start in range(0, points, block):
        at = slice(start, start + block)
        index = index_ref[:, at]
        high, low = index // cells, index % cells
        feat = feat_ref[:, at].astype(f32)
        feat = jnp.concatenate([feat, jnp.zeros((rows - chans, block), f32)], axis=0)
        spread = jnp.concatenate([jnp.where(high == grid, feat, 0.0) for grid in range(grids)], axis=0)
        term = matmul_nt(spread.astype(bf16), one_hot(low, cells))
        total = term if total is None else total + term
    out_ref[:, 2 * own :] = total.reshape(grids, rows, cells)[:, :chans].astype(bf16)


def home_body(
    block, place_ref, index_ref, keep_ref, got_ref, lidar_far, mixed_far, cam_far, token_ref,
    lidar_ref, mixed_ref, cam_ref, sems,
):
    grids, own, _, _ = lidar_ref.shape
    cells = keep_ref.shape[2]
    chans, points = cam_ref.shape
    low = place_ref[0] & 1
    blocks = [(ref, pair, 2 * pair + parity) for ref, parity in ((keep_ref, low), (got_ref, 1 - low)) for pair in range(grids // 2)]
    token_ref[...] = jnp.zeros(token_ref.shape, f32)
    copies = []
    for i, (near, far) in enumerate(((lidar_ref, lidar_far), (mixed_ref, mixed_far))):
        for ref, pair, grid in blocks:
            near[grid] = ref[pair, i * own : (i + 1) * own, :].astype(f32).reshape(near.shape[1:])
        copies.append(pltpu.make_async_copy(near, far, sems.at[i]))
        copies[-1].start()
    rows = round_up(chans, 8)
    grad = jnp.concatenate([ref[:, 2 * own : 2 * own + chans, :] for ref in (keep_ref, got_ref)], axis=0)
    grad = jnp.concatenate([grad.astype(f32), jnp.zeros((grids, rows - chans, cells), f32)], axis=1)
    grad = grad.reshape(grids * rows, cells).astype(bf16)
    for start in range(0, points, block):
        at = slice(start, start + block)
        index = index_ref[:, at]
        high, low_part = index // cells, index % cells
        picked = matmul(grad, one_hot(low_part, cells))
        total = jnp.zeros((rows, block), f32)
        for i, (_, _, grid) in enumerate(blocks):
            total = jnp.where(high == grid, picked[i * rows : (i + 1) * rows], total)
        cam_ref[:, at] = total[:chans]
    copies.append(pltpu.make_async_copy(cam_ref, cam_far, sems.at[2]))
    copies[-1].start()
    for copy in copies:
        copy.wait()


def pack_body(
    lid, cam, mid, one_width, norm_ref, lidar_far, cam_far, mid_far, out_ref,
    near_ref, lidar_ref, cam_ref, mid_ref, norm_sem, sems,
):
    rows = lidar_ref.shape[2]
    norm_copy = pltpu.make_async_copy(norm_ref, near_ref, norm_sem)
    norm_copy.start()
    pairs = ((lidar_far, lidar_ref), (cam_far, cam_ref), (mid_far, mid_ref))
    copies = [
        [pltpu.make_async_copy(far.at[a], near.at[a], sems.at[i, a]) for i, (far, near) in enumerate(pairs)]
        for a in range(3)
    ]
    for group in copies:
        for copy in group:
            copy.start()
    for a in range(3):
        for copy in copies[a]:
            copy.wait()
        base = a * one_width
        for b in range(3):
            out_ref[:, base + b * lid : base + (b + 1) * lid] = lidar_ref[a, b].astype(bf16)
        used = 3 * lid + 3 * cam
        rest = [cam_ref[a, b] for b in range(3)]
        if one_width > used:
            rest.append(jnp.zeros((rows, one_width - used), f32))
        out_ref[:, base + 3 * lid : base + one_width] = jnp.concatenate(rest, axis=1).astype(bf16)
        for b in range(3):
            start = 3 * one_width + (3 * a + b) * mid
            out_ref[:, start : start + mid] = mid_ref[a, b].astype(bf16)
    norm_copy.wait()
    norm = near_ref[...]
    norm = jnp.concatenate([norm, jnp.zeros((LANES - norm.shape[0], rows), f32)], axis=0)
    norm = jnp.concatenate([norm, jnp.zeros((LANES, LANES - rows), f32)], axis=1).T[:rows, :4]
    high = norm.astype(bf16)
    left = norm - high.astype(f32)
    middle = left.astype(bf16)
    low = (left - middle.astype(f32)).astype(bf16)
    tail = jnp.concatenate(
        [high.astype(f32), middle.astype(f32), low.astype(f32), jnp.zeros((rows, LANES - 12), f32)],
        axis=1,
    )
    out_ref[:, 3 * one_width + 9 * mid :] = tail.astype(bf16)


def place_rows(own, masks, chan, parts, all_ref):
    place = 0
    for part in parts:
        for j in range(part.shape[0]):
            row = pl.multiple_of((chan ^ masks[place]) * own, own)
            all_ref[pl.ds(row, own), :] = part[j]
            place += 1


def unpack_body(own, one_width, two_width, masks, place_ref, *refs):
    parts, (one_ref, two_ref, norm_ref, all_ref) = refs[:-4], refs[-4:]
    place_rows(own, masks, place_ref[0], parts, all_ref)
    one_ref[...] = all_ref[:, : 3 * one_width]
    two_ref[...] = all_ref[:, 3 * one_width : 3 * (one_width + two_width)]
    tail = all_ref[:, 3 * (one_width + two_width) :].astype(f32)
    norm = tail[:, 0:4] + tail[:, 4:8] + tail[:, 8:12]
    norm_ref[...] = jnp.concatenate([norm, jnp.zeros((norm.shape[0], LANES - 4), f32)], axis=1)


def turn_body(lid, cam, one_width, outs, one_ref, two_t_ref, one_t_ref, two_ref):
    for t in range(9):
        at = slice(t * outs, (t + 1) * outs)
        two_ref[:, at] = two_t_ref[:, at].T
    for a in range(3):
        for b in range(3):
            to = slice((3 * a + b) * outs, (3 * a + b + 1) * outs)
            start = a * one_width + b * lid
            one_t_ref[0:lid, to] = one_ref[:, start : start + lid].T
        start = a * one_width + 3 * lid
        turned = one_ref[:, start : start + one_width - 3 * lid].T
        for b in range(3):
            to = slice((3 * a + b) * outs, (3 * a + b + 1) * outs)
            one_t_ref[lid : lid + cam, to] = turned[b * cam : (b + 1) * cam]


def edge_rows(edge_ref, place_ref, groups, first, last):
    if groups == 2:
        edge_ref[0] = jnp.where(place_ref[1] == 0, last, first)
    else:
        edge_ref[0] = last
        edge_ref[1] = first


def fill_stack(stack_ref, base, order, p, row):
    count = row.shape[0]
    for b, shifted in zip(order, (*sides(row), row), strict=True):
        start = base + b * count
        stack_ref[start : start + count, cut(p)] = shifted.astype(bf16)


FORWARD = (0, 2, 1)
BACKWARD = (2, 0, 1)


def first_body(cfg, got_ref, kernel_ref, stack_ref, cot_ref, part_ref):
    nc, spg, rows, lid, cam, lid_own, cam_own, one_width = cfg
    per_strip = rows // spg

    def take(q, first, count):
        s, r = q // per_strip, q % per_strip
        pieces = [got_ref[s * nc + c, first : first + count, cut(r)] for c in range(nc)]
        return jnp.concatenate([piece.astype(f32) for piece in pieces], axis=0)

    used = 3 * (lid + cam)
    stack_ref[:, cut(0)] = jnp.zeros((one_width, LANES), bf16)
    stack_ref[:, cut(rows + 1)] = jnp.zeros((one_width, LANES), bf16)
    if one_width > used:
        stack_ref[used:, :] = jnp.zeros((one_width - used, (rows + 2) * LANES), bf16)
    for q in range(rows):
        fill_stack(stack_ref, 0, FORWARD, q + 1, take(q, 0, lid_own))
        fill_stack(stack_ref, 3 * lid, FORWARD, q + 1, take(q, 2 * lid_own, cam_own))
        cot_ref[:, cut(q)] = take(q, lid_own, lid_own).astype(bf16)
    total = None
    for a in range(3):
        term = matmul(
            kernel_ref[:, a * one_width : (a + 1) * one_width],
            stack_ref[:, a * LANES : (a + rows) * LANES],
        )
        total = term if total is None else total + term
    part_ref[...] = total


def first_halo_body(
    cfg, place_ref, part_ref, above_ref, below_ref, kernel_ref,
    halo_ref, cot_ref, out_ref, sums_ref, edge_ref,
):
    nc, rows, lid, cam, lid_own, cam_own, one_width, groups = cfg
    has_above = place_ref[1] > 0
    has_below = place_ref[1] < groups - 1
    used = 3 * (lid + cam)
    if one_width > used:
        halo_ref[used:, :] = jnp.zeros((one_width - used, 2 * LANES), bf16)
    for side, (ref, given) in enumerate(((above_ref, has_above), (below_ref, has_below))):
        row = jnp.concatenate([ref[c, :lid_own].astype(f32) for c in range(nc)], axis=0)
        fill_stack(halo_ref, 0, FORWARD, side, jnp.where(given, row, 0.0))
        row = jnp.concatenate([ref[c, 2 * lid_own :].astype(f32) for c in range(nc)], axis=0)
        fill_stack(halo_ref, 3 * lid, FORWARD, side, jnp.where(given, row, 0.0))
        cot_ref[:, cut(side)] = jnp.concatenate([ref[c, lid_own : 2 * lid_own] for c in range(nc)], axis=0)
    lines = [part_ref[:, cut(q)] for q in range(rows)]
    lines[0] = lines[0] + matmul(kernel_ref[:, :one_width], halo_ref[:, cut(0)])
    lines[-1] = lines[-1] + matmul(kernel_ref[:, 2 * one_width :], halo_ref[:, cut(1)])
    finish_sums(lines, out_ref, sums_ref, edge_ref, place_ref, groups)


def finish_sums(lines, out_ref, sums_ref, edge_ref, place_ref, groups):
    sums = squares = None
    for q, row in enumerate(lines):
        out_ref[:, cut(q)] = row
        sums = row if sums is None else sums + row
        squares = row * row if squares is None else squares + row * row
    for_all(sums_ref, column_sums([sums, squares]))
    edge_rows(edge_ref, place_ref, groups, lines[0], lines[-1])


def second_body(
    cfg, place_ref, raw_ref, above_ref, below_ref, stats_ref, norm_ref, kernel_ref,
    out_ref, sums_ref, edge_ref, hidden_ref, means_ref, stack_ref,
):
    rows, chans, groups, pixel_count = cfg
    mean, inv = moments(stats_ref[...], pixel_count)
    columns = to_columns([mean, inv])
    means_ref[...] = columns
    mean, inv = columns[:, 0:1], columns[:, 1:2]
    gain, shift = norm_ref[:, 0:1], norm_ref[:, 1:2]
    for p in range(rows + 2):
        if p == 0:
            raw = above_ref[...]
        elif p == rows + 1:
            raw = below_ref[...]
        else:
            raw = raw_ref[:, cut(p - 1)]
        act = gain * ((raw - mean) * inv) + shift
        hidden = act * sigmoid(act)
        if p == 0:
            hidden = jnp.where(place_ref[1] > 0, hidden, 0.0)
        elif p == rows + 1:
            hidden = jnp.where(place_ref[1] < groups - 1, hidden, 0.0)
        else:
            hidden_ref[:, cut(p - 1)] = hidden
        fill_stack(stack_ref, 0, FORWARD, p, hidden)
    total = None
    for a in range(3):
        term = matmul(
            kernel_ref[:, a * 3 * chans : (a + 1) * 3 * chans],
            stack_ref[:, a * LANES : (a + rows) * LANES],
        )
        total = term if total is None else total + term
    lines = [total[:, cut(q)] for q in range(rows)]
    finish_sums(lines, out_ref, sums_ref, edge_ref, place_ref, groups)


def slope_body(
    cfg, place_ref, raw_ref, above_ref, below_ref, stats_ref, norm_ref, cot_ref, cot_halo_ref, hidden_ref,
    slope_ref, sums_ref, means_ref, mixed_ref,
):
    rows, own, spg, nc, pixel_count = cfg
    per_strip = rows // spg
    mean, inv = moments(stats_ref[...], pixel_count)
    columns = to_columns([mean, inv])
    means_ref[...] = columns
    mean, inv = columns[:, 0:1], columns[:, 1:2]
    gain, shift = norm_ref[:, 2:3], norm_ref[:, 3:4]
    shift_sum = gain_sum = None
    for p in range(rows + 2):
        if p == 0:
            raw, cot = above_ref[...], cot_halo_ref[:, cut(0)]
        elif p == rows + 1:
            raw, cot = below_ref[...], cot_halo_ref[:, cut(1)]
        else:
            raw, cot = raw_ref[:, cut(p - 1)], cot_ref[:, cut(p - 1)]
        centred = (raw - mean) * inv
        act = gain * centred + shift
        gate = sigmoid(act)
        slope = cot.astype(f32) * (gate * (1.0 + act * (1.0 - gate)))
        slope_ref[:, cut(p)] = slope
        if 0 < p <= rows:
            shift_sum = slope if shift_sum is None else shift_sum + slope
            term = slope * centred
            gain_sum = term if gain_sum is None else gain_sum + term
            mixed = (hidden_ref[:, cut(p - 1)] + act * gate).astype(bf16)
            s, r = (p - 1) // per_strip, (p - 1) % per_strip
            for c in range(nc):
                mixed_ref[s * nc + c, :, cut(r)] = mixed[c * own : (c + 1) * own]
    for_all(sums_ref, column_sums([shift_sum, gain_sum]))


def mid_back_body(
    cfg, place_ref, slope_ref, raw_ref, above_ref, below_ref, means_two_ref, stats_ref, norm_ref,
    kernel_ref, raw_one_ref, means_one_ref, cot_ref,
    out_ref, sums_ref, edge_ref, stack_ref, grads_ref,
):
    rows, chans, groups, pixel_count = cfg
    total = jnp.sum(stats_ref[...], axis=0)
    grads_ref[...] = total
    columns = to_columns([total[0:1] / pixel_count, total[1:2] / pixel_count])
    shift_mean, gain_mean = columns[:, 0:1], columns[:, 1:2]
    mean, inv = means_two_ref[:, 0:1], means_two_ref[:, 1:2]
    scale = norm_ref[:, 2:3] * inv
    for p in range(rows + 2):
        if p == 0:
            raw = above_ref[...]
        elif p == rows + 1:
            raw = below_ref[...]
        else:
            raw = raw_ref[:, cut(p - 1)]
        centred = (raw - mean) * inv
        grad = scale * (slope_ref[:, cut(p)] - shift_mean - centred * gain_mean)
        if p == 0:
            grad = jnp.where(place_ref[1] > 0, grad, 0.0)
        elif p == rows + 1:
            grad = jnp.where(place_ref[1] < groups - 1, grad, 0.0)
        fill_stack(stack_ref, 0, BACKWARD, p, grad)
    back = None
    for a in range(3):
        term = matmul(
            kernel_ref[:, a * 3 * chans : (a + 1) * 3 * chans],
            stack_ref[:, (2 - a) * LANES : (2 - a + rows) * LANES],
        )
        back = term if back is None else back + term
    mean, inv = means_one_ref[:, 0:1], means_one_ref[:, 1:2]
    gain, shift = norm_ref[:, 0:1], norm_ref[:, 1:2]
    shift_sum = gain_sum = None
    slopes = []
    for q in range(rows):
        centred = (raw_one_ref[:, cut(q)] - mean) * inv
        act = gain * centred + shift
        gate = sigmoid(act)
        grad = back[:, cut(q)] + cot_ref[:, cut(q)].astype(f32)
        slope = grad * (gate * (1.0 + act * (1.0 - gate)))
        out_ref[:, cut(q)] = slope
        if q in (0, rows - 1):
            slopes.append(slope)
        shift_sum = slope if shift_sum is None else shift_sum + slope
        term = slope * centred
        gain_sum = term if gain_sum is None else gain_sum + term
    for_all(sums_ref, column_sums([shift_sum, gain_sum]))
    edge_rows(edge_ref, place_ref, groups, slopes[0], slopes[-1])


def halves(place_ref, own, nc, rows_at):
    low = place_ref[0] & 1
    found = []
    for side in (low, 1 - low):
        for pair in range(nc // 2):
            found.append(rows_at(pl.multiple_of((2 * pair + side) * own, own)))
    return jnp.concatenate(found, axis=0)


def first_back_body(
    cfg, place_ref, slope_ref, slope_above_ref, slope_below_ref, raw_ref, above_ref, below_ref,
    means_ref, stats_ref, norm_ref, grads_two_ref, own_ref, halo_ref, hidden_ref, stack_two_ref,
    keep_ref, send_ref, stack_ref, grads_ref, squares_ref, cells_ref,
):
    rows, chans, own, nc, one_width, groups, pixel_count = cfg
    wide = (rows + 2) * LANES
    total = jnp.sum(stats_ref[...], axis=0)
    grads = jnp.concatenate(
        [total[1:2], total[0:1], grads_two_ref[1:2], grads_two_ref[0:1]], axis=0
    )
    grads_ref[...] = grads
    squares_ref[...] = jnp.broadcast_to(jnp.sum(grads * grads), squares_ref.shape)
    columns = to_columns([total[0:1] / pixel_count, total[1:2] / pixel_count])
    shift_mean, gain_mean = columns[:, 0:1], columns[:, 1:2]
    mean, inv = means_ref[:, 0:1], means_ref[:, 1:2]
    scale = norm_ref[:, 0:1] * inv
    for p in range(rows + 2):
        if p == 0:
            raw, slope = above_ref[...], slope_above_ref[...]
        elif p == rows + 1:
            raw, slope = below_ref[...], slope_below_ref[...]
        else:
            raw, slope = raw_ref[:, cut(p - 1)], slope_ref[:, cut(p - 1)]
        grad = scale * (slope - shift_mean - (raw - mean) * inv * gain_mean)
        if p == 0:
            grad = jnp.where(place_ref[1] > 0, grad, 0.0)
        elif p == rows + 1:
            grad = jnp.where(place_ref[1] < groups - 1, grad, 0.0)
        fill_stack(stack_ref, 0, BACKWARD, p, grad)
    cells_ref[:, :LANES] = halo_ref[:, :LANES]
    cells_ref[:, LANES : wide - LANES] = own_ref[:, LANES : wide - LANES]
    cells_ref[:, wide - LANES :] = halo_ref[:, LANES:]
    half = chans // 2
    ordered = halves(
        place_ref, own, nc,
        lambda start: stack_ref[pl.ds(chans + start, own), LANES : (rows + 1) * LANES],
    )
    hidden = halves(place_ref, own, nc, lambda start: hidden_ref[pl.ds(start, own), :]).astype(bf16)
    for a in range(3):
        grad = matmul_nt(ordered, cells_ref[:, a * LANES : (a + rows) * LANES])
        to = slice(a * one_width, (a + 1) * one_width)
        keep_ref[:, to] = grad[:half]
        send_ref[:, to] = grad[half:].astype(bf16)
        grad = matmul_nt(hidden, stack_two_ref[:, (2 - a) * LANES : (2 - a + rows) * LANES])
        start = 3 * one_width + a * 3 * chans
        keep_ref[:, start : start + 3 * chans] = grad[:half]
        send_ref[:, start : start + 3 * chans] = grad[half:].astype(bf16)


def inputs_back_body(cfg, stack_ref, kernel_ref, mixed_ref, back_ref):
    rows, chans, lid, lid_own, cam_own, spg, nc = cfg
    per_strip = rows // spg
    back = None
    for a in range(3):
        term = matmul(
            kernel_ref[:, a * 3 * chans : (a + 1) * 3 * chans],
            stack_ref[:, (2 - a) * LANES : (2 - a + rows) * LANES],
        )
        back = term if back is None else back + term
    for s in range(spg):
        cells = slice(s * per_strip * LANES, (s + 1) * per_strip * LANES)
        for c in range(nc):
            block = s * nc + c
            back_ref[block, 0:lid_own, :] = back[c * lid_own : (c + 1) * lid_own, cells].astype(bf16)
            back_ref[block, lid_own : 2 * lid_own, :] = mixed_ref[block]
            start = lid + c * cam_own
            back_ref[block, 2 * lid_own : 2 * lid_own + cam_own, :] = back[
                start : start + cam_own, cells
            ].astype(bf16)


def adam(weight, gradient, first, second, rate):
    first = beta_one * first + (1.0 - beta_one) * gradient
    second = beta_two * second + (1.0 - beta_two) * gradient * gradient
    fix_one = 1.0 - beta_one**STEP
    fix_two = 1.0 - beta_two**STEP
    stepped = first * (1.0 / fix_one) / (jnp.sqrt(second * (1.0 / fix_two)) + adam_eps)
    return weight - rate * (stepped + weight_decay * weight), first, second


def add_body(mine_ref, other_ref, out_ref):
    out_ref[...] = (mine_ref[...] + other_ref[...].astype(f32)).astype(bf16)


def sum_body(pieces_ref, out_ref):
    out_ref[...] = jnp.sum(pieces_ref[...].astype(f32), axis=0).astype(bf16)


def merge_body(copies, mine_ref, other_ref, out_ref):
    width = mine_ref.shape[1]
    piece = (mine_ref[...].astype(f32) + other_ref[...].astype(f32)).astype(bf16)
    values = piece.astype(f32)
    squares = jnp.sum(values * values).reshape(1, 1)
    high = squares.astype(bf16).astype(f32)
    middle = (squares - high).astype(bf16).astype(f32)
    low = squares - high - middle
    shape = (piece.shape[0], LANES)
    row = lax.broadcasted_iota(jnp.int32, shape, 0)
    lane = lax.broadcasted_iota(jnp.int32, shape, 1)
    terms = jnp.where(lane == 0, high, jnp.where(lane == 1, middle, jnp.where(lane == 2, low, 0.0)))
    terms = jnp.where(row == 0, terms, 0.0).astype(bf16)
    for copy in range(copies):
        out_ref[copy, :, :width] = piece
        out_ref[copy, :, width:] = terms


def tail_body(width, pieces_ref, out_ref):
    out_ref[...] = jnp.broadcast_to(jnp.sum(pieces_ref[:, :, width:].astype(f32)), out_ref.shape)


def adam_body(lid, cam, mid, chans, smalls, *refs):
    grads_far, refs = refs[0], refs[1:]
    small_fars, fars, refs = refs[:smalls], refs[smalls : smalls + 9], refs[smalls + 9 :]
    small_outs, far_outs, refs = refs[:4], refs[4:13], refs[13:]
    small_nears, nears, refs = refs[:smalls], refs[smalls : smalls + 9], refs[smalls + 9 :]
    small_ins, ins, outs, norm_ref, grads_ref, grads_sem = refs
    one_width = round_up(3 * lid + 3 * cam, 256)
    first = [
        pltpu.make_async_copy(far, near, small_ins.at[i])
        for i, (far, near) in enumerate(zip(small_fars, small_nears, strict=True))
    ]
    reads = [
        [pltpu.make_async_copy(fars[i].at[a], nears[i].at[a], ins.at[i, a]) for i in range(9)]
        for a in range(3)
    ]
    grads_copy = pltpu.make_async_copy(grads_far, grads_ref, grads_sem)
    for group in (first, [grads_copy], *reads):
        for copy in group:
            copy.start()
    for copy in first:
        copy.wait()
    squares = [ref[0:1, 0:1] for ref in small_nears[:chans]]
    norm_squares_ref, norm_grad_ref, *norm_state = small_nears[chans:]
    while len(squares) > 1:
        squares = [squares[i] + squares[i + 1] for i in range(0, len(squares), 2)]
    norm = jnp.sqrt(squares[0] + norm_squares_ref[0:1, 0:1])
    norm_ref[...] = norm
    factor = jnp.minimum(1.0, clip_norm / (norm + 1e-06))

    def step(state, at, gradient, rate):
        weight, first, second = (ref[at] for ref in state)
        for ref, value in zip(state, adam(weight, factor * gradient, first, second, rate), strict=True):
            ref[at] = value

    step(norm_state, ..., norm_grad_ref[...], norm_rate)
    writes = [
        [
            pltpu.make_async_copy(near, far, small_ins.at[i])
            for i, (near, far) in enumerate(zip((*norm_state, norm_ref), small_outs, strict=True))
        ]
    ]
    for copy in writes[0]:
        copy.start()
    grads_copy.wait()
    for a in range(3):
        for copy in reads[a]:
            copy.wait()
        base = a * one_width
        tail = grads_ref[:, base + 3 * lid : base + one_width].astype(f32)
        for b in range(3):
            start = 3 * one_width + (3 * a + b) * mid
            given = (
                tail[:, b * cam : (b + 1) * cam],
                grads_ref[:, base + b * lid : base + (b + 1) * lid].astype(f32),
                grads_ref[:, start : start + mid].astype(f32),
            )
            for i, gradient in enumerate(given):
                step(nears[3 * i : 3 * i + 3], (a, b), gradient, learn_rate)
        writes.append(
            [pltpu.make_async_copy(nears[i].at[a], far_outs[i].at[a], outs.at[i, a]) for i in range(9)]
        )
        for copy in writes[-1]:
            copy.start()
    for group in writes:
        for copy in group:
            copy.wait()


def shards(
    cam_feats,
    cell_index,
    lidar_bev,
    w_cam,
    w_lidar,
    w_mid,
    bn_params,
    cotangent,
    m_cam,
    v_cam,
    m_lidar,
    v_lidar,
    m_mid,
    v_mid,
    m_bn,
    v_bn,
):
    grids, lid_own, strip_rows, width = lidar_bev.shape
    cam_own, points = cam_feats.shape
    own = bn_params.shape[1]
    nc = lax.axis_size("chan")
    ns = lax.axis_size("strip")
    lid, cam, chans = nc * lid_own, nc * cam_own, nc * own
    spg = grids // nc
    groups = ns // spg
    members = spg * nc
    rows = spg * strip_rows
    cells = strip_rows * width
    pixel_count = float(grids * cells * ns)
    devices = ns * nc
    one_width = round_up(3 * lid + 3 * cam, 256)
    two_width = 3 * chans
    total_width = 3 * one_width + 3 * two_width
    chan = lax.axis_index("chan")
    group = lax.axis_index("strip") // spg
    place = jnp.stack([chan, group]).astype(jnp.int32)

    tile_groups = [[g * members + r for r in range(members)] for g in range(groups)]
    half_groups = [
        [(g * spg + s) * nc + 2 * pair + low for pair in range(nc // 2) for s in range(spg)]
        for g in range(groups)
        for low in range(2)
    ]
    core_groups = [
        [(g * spg + s) * nc + 2 * pair + low for s in range(spg) for pair in range(nc // 2)]
        for g in range(groups)
        for low in range(2)
    ]
    strip_groups = [
        [(g * spg + s) * nc + c for s in range(spg)] for g in range(groups) for c in range(nc)
    ]

    def exchange(blocks, parts):
        return lax.all_to_all(blocks, AXES, 0, 0, axis_index_groups=parts, tiled=True)

    def everywhere(copies):
        return lax.all_to_all(copies, AXES, 0, 0, tiled=True)

    def chan_swap(values, bit):
        return lax.ppermute(values, "chan", [(c, c ^ bit) for c in range(nc)])

    def neighbours(edges):
        if groups == 1:
            return edges[0], edges[0]
        if groups == 2:
            pairs = [(i, (i + members) % devices) for i in range(devices)]
            other = lax.ppermute(edges[0], AXES, pairs)
            return other, other
        down = [(i, i + members) for i in range(devices - members)]
        up = [(i + members, i) for i in range(devices - members)]
        return lax.ppermute(edges[0], AXES, down), lax.ppermute(edges[1], AXES, up)

    edge_count = 2 if groups > 2 else 1

    area = rows * LANES
    wide = (rows + 2) * LANES
    def from_all_channels(packed):
        parts, masks = [packed[None]], [0]
        bit = nc // 2
        while bit:
            stacked = parts[0] if len(parts) == 1 else jnp.concatenate(parts, axis=0)
            parts.append(chan_swap(stacked, bit))
            masks += [mask ^ bit for mask in masks]
            bit //= 2
        return parts, masks

    def edge_cells(got):
        last = got[members - nc :, :, cells - width :]
        first = got[:nc, :, :width]
        if groups == 2:
            return jnp.where(group == 0, last, first)[None]
        return jnp.stack([last, first])

    sums_struct = struct((devices, 2, chans), f32)
    packed_width = total_width + LANES

    index_row = cell_index.reshape(1, points)
    block = math.gcd(points, 1024)
    joined = call(
        functools.partial(pool_body, block), struct((grids, lid_own + own + cam_own, cells), bf16)
    )(
        index_row, cam_feats, lidar_bev.reshape(grids, lid_own, cells),
        cotangent.reshape(grids, own, cells),
    )
    got = exchange(joined, tile_groups)
    above, below = neighbours(edge_cells(got))

    turn = (0, 1, 3, 2)
    far = pl.BlockSpec(memory_space=pltpu.HBM)
    near = pl.BlockSpec(memory_space=pltpu.VMEM)
    weights = [w_lidar.transpose(turn), w_cam.transpose(turn), w_mid]
    packed = pl.pallas_call(
        functools.partial(pack_body, lid, cam, chans, one_width),
        in_specs=[far] * 4,
        out_specs=near,
        out_shape=struct((own, packed_width), bf16),
        scratch_shapes=[
            *(pltpu.VMEM(weight.shape, f32) for weight in (bn_params, *weights)),
            pltpu.SemaphoreType.DMA,
            pltpu.SemaphoreType.DMA((3, 3)),
        ],
        compiler_params=pltpu.CompilerParams(vmem_limit_bytes=VMEM_MOST),
    )(bn_params, *weights)
    parts, masks = from_all_channels(packed)
    kernel_one, kernel_two_t, norm = call(
        functools.partial(unpack_body, own, one_width, two_width, masks),
        [
            struct((chans, 3 * one_width), bf16),
            struct((chans, 3 * two_width), bf16),
            struct((chans, LANES), f32),
        ],
        scratch=[pltpu.VMEM((chans, packed_width), bf16)],
        smem=1,
    )(place, *parts)

    kernel_one_t, kernel_two = call(
        functools.partial(turn_body, lid, cam, one_width, chans),
        [struct((lid + cam, 3 * two_width), bf16), struct((chans, 3 * two_width), bf16)],
    )(kernel_one, kernel_two_t)
    own_stack, cot, part_one = call(
        functools.partial(first_body, (nc, spg, rows, lid, cam, lid_own, cam_own, one_width)),
        [
            struct((one_width, wide), bf16),
            struct((chans, area), bf16),
            struct((chans, area), f32),
        ],
    )(got, kernel_one)
    halo_stack, cot_halo, raw_one, sums_one, edges_one = call(
        functools.partial(
            first_halo_body, (nc, rows, lid, cam, lid_own, cam_own, one_width, groups)
        ),
        [
            struct((one_width, 2 * LANES), bf16),
            struct((chans, 2 * LANES), bf16),
            struct((chans, area), f32),
            sums_struct,
            struct((edge_count, chans, LANES), f32),
        ],
        smem=1,
        after=(kernel_one_t, kernel_two),
    )(place, part_one, above, below, kernel_one)

    above_one, below_one = neighbours(edges_one)
    stats_one = everywhere(sums_one)
    raw_two, sums_two, edges_two, hidden, means_one = call(
        functools.partial(second_body, (rows, chans, groups, pixel_count)),
        [
            struct((chans, area), f32),
            sums_struct,
            struct((edge_count, chans, LANES), f32),
            struct((chans, area), f32),
            struct((chans, LANES), f32),
        ],
        scratch=[pltpu.VMEM((two_width, wide), bf16)],
        smem=1,
    )(place, raw_one, above_one, below_one, stats_one, norm, kernel_two)

    above_two, below_two = neighbours(edges_two)
    stats_two = everywhere(sums_two)
    slope_two, sums_three, means_two, mixed_blocks = call(
        functools.partial(slope_body, (rows, own, spg, nc, pixel_count)),
        [
            struct((chans, wide), f32),
            sums_struct,
            struct((chans, LANES), f32),
            struct((members, own, cells), bf16),
        ],
        smem=1,
    )(place, raw_two, above_two, below_two, stats_two, norm, cot, cot_halo, hidden)

    stats_three = everywhere(sums_three)
    slope_one, sums_four, edges_four, grad_stack, grads_two = call(
        functools.partial(mid_back_body, (rows, chans, groups, pixel_count)),
        [
            struct((chans, area), f32),
            sums_struct,
            struct((edge_count, chans, LANES), f32),
            struct((two_width, wide), bf16),
            struct((2, chans), f32),
        ],
        smem=1,
    )(
        place, slope_two, raw_two, above_two, below_two, means_two, stats_three, norm,
        kernel_two_t, raw_one, means_one, cot,
    )

    above_four, below_four = neighbours(edges_four)
    stats_four = everywhere(sums_four)
    keep, send, grad_stack_one, grad_bn_all, norm_squares = call(
        functools.partial(
            first_back_body, (rows, chans, own, nc, one_width, groups, pixel_count)
        ),
        [
            struct((chans // 2, total_width), f32),
            struct((chans // 2, total_width), bf16),
            struct((two_width, wide), bf16),
            struct((4, chans), f32),
            struct((8, LANES), f32),
        ],
        scratch=[pltpu.VMEM((one_width, wide), bf16)],
        smem=1,
    )(
        place, slope_one, above_four, below_four, raw_one, above_one, below_one, means_one,
        stats_four, norm, grads_two, own_stack, halo_stack, hidden, grad_stack,
    )
    back_blocks = call(
        functools.partial(inputs_back_body, (rows, chans, lid, lid_own, cam_own, spg, nc)),
        struct((members, lid_own + own + cam_own, cells), bf16),
    )(grad_stack_one, kernel_one_t, mixed_blocks)
    home = exchange(back_blocks, core_groups)

    halved = call(add_body, struct(keep.shape, bf16), after=(back_blocks,))(keep, chan_swap(send, 1))
    piece_rows = own // spg
    pieces = exchange(halved.reshape(members // 2, piece_rows, total_width), half_groups)
    piece = call(sum_body, struct((piece_rows, total_width), bf16))(pieces)
    other = jnp.zeros_like(piece)
    shift = members
    while shift < devices:
        if shift > members:
            piece = (piece.astype(f32) + other.astype(f32)).astype(bf16)
        other = lax.ppermute(piece, AXES, [(i, i ^ shift) for i in range(devices)])
        shift *= 2
    merged = call(
        functools.partial(merge_body, spg), struct((spg, piece_rows, packed_width), bf16)
    )(piece, other)
    merged, home = lax.optimization_barrier((merged, home))
    merged = exchange(merged, strip_groups)
    own_grads = merged.reshape(own, packed_width)
    keep_home, send_home = call(
        split_body, [struct((members // 2, *home.shape[1:]), bf16)] * 2, smem=1
    )(place, home)
    images = [struct(lidar_bev.shape, f32), struct(cotangent.shape, f32), struct((cam_own, points), f32)]
    grad_lidar, mixed, grad_cam, token = pl.pallas_call(
        functools.partial(home_body, block),
        in_specs=[pl.BlockSpec(memory_space=pltpu.SMEM)] + [near] * 3,
        out_specs=[far] * 3 + [near],
        out_shape=[*images, struct((8, LANES), f32)],
        scratch_shapes=[
            *(pltpu.VMEM(image.shape, f32) for image in images),
            pltpu.SemaphoreType.DMA((3,)),
        ],
        compiler_params=pltpu.CompilerParams(vmem_limit_bytes=VMEM_BYTES),
    )(place, index_row, keep_home, chan_swap(send_home, 1))
    tall = lambda array: array.transpose(turn)
    state = [
        *(tall(array) for array in (w_cam, m_cam, v_cam)),
        *(tall(array) for array in (w_lidar, m_lidar, v_lidar)),
        w_mid, m_mid, v_mid,
    ]
    squares = call(
        functools.partial(tail_body, total_width),
        struct((8, LANES), f32),
        after=(token,),
    )(merged)
    squares = [squares] + [
        lax.ppermute(squares, "chan", [(c, c ^ mask) for c in range(nc)]) for mask in range(1, nc)
    ]
    grad_bn = lax.dynamic_slice(grad_bn_all, (0, chan * own), (4, own))
    norm_state = [bn_params, m_bn, v_bn]
    small = [*squares, norm_squares, grad_bn, *norm_state]
    results = [*norm_state, struct((1, 1), f32), *state]
    updated = pl.pallas_call(
        functools.partial(adam_body, lid, cam, chans, nc, len(small)),
        in_specs=[far] * (len(small) + 10),
        out_specs=[far] * 13,
        out_shape=[struct(array.shape, f32) for array in results],
        scratch_shapes=[
            *(pltpu.VMEM(array.shape, f32) for array in small + state),
            pltpu.SemaphoreType.DMA((len(small),)),
            pltpu.SemaphoreType.DMA((9, 3)),
            pltpu.SemaphoreType.DMA((9, 3)),
            pltpu.VMEM((1, 1), f32),
            pltpu.VMEM(own_grads.shape, bf16),
            pltpu.SemaphoreType.DMA,
        ],
        compiler_params=pltpu.CompilerParams(vmem_limit_bytes=VMEM_MOST),
    )(own_grads, *small, *state)
    turned = [tall(array) for array in updated[4:10]]
    return (mixed, grad_cam, grad_lidar, updated[3].reshape(()), *turned, *updated[10:], *updated[:3])


def solution(mesh):
    return jax.shard_map(
        shards,
        mesh=mesh,
        in_specs=(
            P("chan", "strip"),
            P("strip"),
            P(None, "chan", "strip", None),
            P(None, None, None, "chan"),
            P(None, None, None, "chan"),
            P(None, None, "chan", None),
            P(None, "chan"),
            P(None, "chan", "strip", None),
            P(None, None, None, "chan"),
            P(None, None, None, "chan"),
            P(None, None, None, "chan"),
            P(None, None, None, "chan"),
            P(None, None, "chan", None),
            P(None, None, "chan", None),
            P(None, "chan"),
            P(None, "chan"),
        ),
        out_specs=(
            P(None, "chan", "strip", None),
            P("chan", "strip"),
            P(None, "chan", "strip", None),
            P(),
            P(None, None, None, "chan"),
            P(None, None, None, "chan"),
            P(None, None, None, "chan"),
            P(None, None, None, "chan"),
            P(None, None, None, "chan"),
            P(None, None, None, "chan"),
            P(None, None, "chan", None),
            P(None, None, "chan", None),
            P(None, None, "chan", None),
            P(None, "chan"),
            P(None, "chan"),
            P(None, "chan"),
        ),
        check_vma=False,
    )
```
